32 devices in a mesh: group: 1, node: 16 (over z, y, core), local: 2 (over x).
Axes of the slice: x: 2, y: 2, z: 4, core: 2. Of those that a mesh axis runs over, the one named last changes fastest.
Arguments:
- moe_rows: bfloat16 [256, 7168], P(('group', 'node', 'local')), may hold values from -6 to 6
- route_ids: int32 [256, 8], P(('group', 'node', 'local')), may hold values from 0 to 15, all different within a row; in each aligned block of 8 rows (0 to 7, 8 to 15, ...) at most 8 rows name the same one
- route_gates: float32 [256, 8], P(('group', 'node', 'local')), may hold values from 0.05 to 1
- w_gate: bfloat16 [16, 7168, 1024], P('node', None, 'local'), may hold values from -0.0625 to 0.0625
- w_up: bfloat16 [16, 7168, 1024], P('node', None, 'local'), may hold values from -0.0625 to 0.0625
- w_down: bfloat16 [16, 1024, 7168], P('node', 'local'), may hold values from -0.1875 to 0.1875
- query_latent: bfloat16 [64, 64, 512], P(('group', 'node', 'local')), may hold values from -16 to 16
- query_rope: bfloat16 [64, 64, 64], P(('group', 'node', 'local')), may hold values from -4 to 4
- cache_latent: bfloat16 [64, 512, 512], P(('group', 'node', 'local')), may hold values from -4 to 4
- cache_rope: bfloat16 [64, 64, 512], P(('group', 'node', 'local')), may hold values from -4 to 4
- cache_lengths: int32 [64], P(('group', 'node', 'local')), may hold values from 64 to 512, as said below
Outputs:
- moe_out: bfloat16 [256, 7168], P(('group', 'node', 'local'))
- attn_latent: bfloat16 [64, 64, 512], P(('group', 'node', 'local'))
The draws below stay inside these ranges and needn't reach their ends.
Inputs may be any that keep to these rules, and one draw needn't show every extreme that they name: `route_ids`: each row names 8 different experts. In the rows of one device (aligned blocks of 8 rows) no expert is named by more than 8 rows; some expert is named by exactly 8 rows in some block. `cache_lengths`: some row's length is exactly 512.
All inputs are finite; a program needn't handle non-finite values.
Results may differ from the reference program's by a relative error of at most 0.0057.
Values may be sent and summed in bfloat16 or wider, within the bound.
No kernel may reach another device: no remote copies, remote signals or barrier semaphores. Data moves between devices by JAX's collectives and lax.ppermute only.
A program may use at most 128 MiB of HBM per device.

```python
import math
import jax
import jax.numpy as jnp
import numpy as np
from jax import lax

D = 7168
FF = 1024
HEADS = 64
LAT = 512
ROPE = 64
CACHE = 512
TOK_DEV = 8
EXPERTS = 16
TOPK = 8
CAP = 8
ROWS = 256
ATT_ROWS = 64


def draw_cache_latent(key, part):
    key = jax.random.fold_in(key, 11)
    values = jnp.clip(jax.random.normal(key, (ATT_ROWS, CACHE, LAT), jnp.float32), -4.0, 4.0)
    return values.astype(jnp.bfloat16)


def draw_query_latent(key, part):
    key = jax.random.fold_in(key, 12)
    values = jnp.clip(jax.random.normal(key, (ATT_ROWS, HEADS, LAT), jnp.float32), -4.0, 4.0)
    return values.astype(jnp.bfloat16)


def draw_cache_lengths(key, part):
    key = jax.random.fold_in(key, 13)
    subkeys = jax.random.split(key, 2)
    lengths = jax.random.randint(subkeys[0], (ATT_ROWS,), CACHE // 8, CACHE + 1)
    full_row = jax.random.randint(subkeys[1], (), 0, ATT_ROWS)
    return lengths.at[full_row].set(CACHE).astype(jnp.int32)


def steps_of(rng, extent, pieces, least, high):
    loudness = 1.0
    for dim, shards_of in pieces:
        heights = jax.random.uniform(jax.random.fold_in(jax.random.fold_in(rng, 6), dim), (shards_of,), jnp.float32, least / len(pieces), high / len(pieces))
        loudness = loudness * jnp.repeat(jnp.exp(heights), extent[dim] // shards_of).reshape((-1,) + (1,) * (len(extent) - 1 - dim))
    return loudness


def deal_out(key, own, number, rows, amount, top, most, lean):
    order = jax.random.permutation(key, amount)
    heavy_load, common = shares(amount, rows * top, most, lean, True), shares(amount, rows * top, most, lean, False)
    places = jnp.arange(amount)

    def named(sizes, turn):
        used = int((sizes > 0).sum())
        fixed = max(1, used // 4)
        moved = fixed + (places - fixed + turn * (used - fixed)) % max(1, amount - fixed)
        return jnp.zeros((amount,), jnp.int32).at[order[jnp.where(places < fixed, places, moved)]].set(jnp.asarray(sizes, jnp.int32))

    sizes = jnp.where(number % 4 == 0, named(heavy_load, number // 4), named(common, number - number // 4 - 1))
    mixed = jax.random.permutation(jax.random.fold_in(own, 3), amount)
    source_of, receiver = mixed[0:amount // 2 * 2:2], mixed[1:amount // 2 * 2:2]
    margin = jnp.minimum(sizes[source_of] - 1, most - sizes[receiver]) // 2
    margin = jnp.where((source_of == order[0]) | (receiver == order[0]) | (sizes[receiver] == 0), 0, jnp.maximum(margin, 0))
    moved = jax.random.randint(jax.random.fold_in(own, 4), (amount // 2,), 0, 1 << 20) % (margin + 1)
    sizes = sizes.at[source_of].add(-moved).at[receiver].add(moved)
    labels = jnp.searchsorted(jnp.cumsum(sizes), jnp.arange(rows * top), side="right").astype(jnp.int32)
    grid = labels.reshape(top, rows).T
    grid = grid[jax.random.permutation(jax.random.fold_in(own, 1), rows)]
    turn = jax.random.randint(jax.random.fold_in(own, 2), (rows, 1), 0, top)
    return jnp.take_along_axis(grid, (jnp.arange(top)[None, :] + turn) % top, axis=1)


def shares(count, total, most, skew, full):
    weights = [(1 << 20) // math.isqrt(rank ** skew) + 1 for rank in range(1, count + 1)]
    largest = most if full else min(most, max(-(-total // count), total * weights[0] // sum(weights)))
    least = 1 if total - largest >= count - 1 else 0
    given, spare = [largest] + [least] * (count - 1), total - largest - least * (count - 1)
    while spare > 0:
        movable = [i for i in range(1, count) if given[i] < largest] or [i for i in range(1, count) if given[i] < most]
        pool, budget = sum([weights[i] for i in movable]), spare
        for i in movable:
            addition = min(most - given[i], max(1, budget * weights[i] // pool), spare)
            given[i] = given[i] + addition
            spare = spare - addition
    return np.array(given)


def centred(rng, shape, spread, most, shards=(), kind=jnp.bfloat16):
    loudness = steps_of(rng, shape, shards, -0.22, 0.18) if shards else 1.0
    entries = jax.random.normal(rng, shape, jnp.float32) * spread * loudness
    return jnp.minimum(jnp.maximum(entries, -most), most).astype(kind)


def setup_inputs(seed: int = 0, part: int = 0) -> dict:
    key_list = jax.random.split(jax.random.key(seed), 12)
    part_splits = jax.random.split(jax.random.fold_in(key_list[11], part), 12)
    moe_rows = centred(part_splits[0], (ROWS, D), 1.0, 6.0, ((0, 32),))
    route_ids_keys = jax.random.split(jax.random.fold_in(part_splits[1], 1), ROWS // TOK_DEV)
    route_ids_turns = jax.random.permutation(jax.random.fold_in(part_splits[1], 3), ROWS // TOK_DEV)
    route_ids = jax.vmap(lambda own, number: deal_out(jax.random.fold_in(part_splits[1], 2), own, number, TOK_DEV, EXPERTS, TOPK, CAP, 2))(route_ids_keys, route_ids_turns).reshape((ROWS, TOPK))
    route_gates = jnp.clip(0.05 + 0.95 * jax.random.uniform(part_splits[2], (ROWS, TOPK), jnp.float32) ** steps_of(part_splits[2], (ROWS, TOPK), ((0, 32),), -0.2, 0.2), 0.05, 1.0)
    w_gate = centred(key_list[3], (EXPERTS, D, FF), D ** -0.5, 0.0625, ((0, 16), (2, 2)))
    w_up = centred(key_list[4], (EXPERTS, D, FF), D ** -0.5, 0.0625, ((0, 16), (2, 2)))
    w_down = centred(key_list[5], (EXPERTS, FF, D), FF ** -0.5, 0.1875, ((0, 16), (1, 2)))
    query_latent = draw_query_latent(jax.random.fold_in(jax.random.fold_in(key_list[11], part), 71), part)
    query_rope = centred(part_splits[7], (ATT_ROWS, HEADS, ROPE), 1.0, 4.0, ((0, 32),))
    cache_latent = draw_cache_latent(jax.random.fold_in(jax.random.fold_in(key_list[11], part), 71), part)
    cache_rope = centred(part_splits[9], (ATT_ROWS, ROPE, CACHE), 1.0, 4.0, ((0, 32),))
    cache_lengths = draw_cache_lengths(jax.random.fold_in(jax.random.fold_in(key_list[11], part), 71), part)
    return {"moe_rows": moe_rows, "route_ids": route_ids, "route_gates": route_gates, "w_gate": w_gate, "w_up": w_up, "w_down": w_down, "query_latent": query_latent, "query_rope": query_rope, "cache_latent": cache_latent, "cache_rope": cache_rope, "cache_lengths": cache_lengths}


score_scale = 192.0 ** -0.5


def slot_numbers(block_ids, expert_count):
    member = jnp.sum((block_ids[:, :, None] == jnp.arange(expert_count, dtype=jnp.int32)[None, None, :]).astype(jnp.int32), axis=1)
    before = jnp.cumsum(member, axis=0) - member
    return jnp.take_along_axis(before, block_ids, axis=1).astype(jnp.int32)


def expert_rows(row_block, gate_mat, up_mat, down_mat):
    gate_act = jnp.dot(row_block, gate_mat, preferred_element_type=jnp.float32)
    up_act = jnp.dot(row_block, up_mat, preferred_element_type=jnp.float32)
    hidden = (jax.nn.silu(gate_act) * up_act).astype(jnp.bfloat16)
    return jnp.dot(hidden, down_mat, preferred_element_type=jnp.float32).astype(jnp.bfloat16)


def reference(moe_rows, route_ids, route_gates, w_gate, w_up, w_down, query_latent, query_rope, cache_latent, cache_rope, cache_lengths):
    block_count = ROWS // TOK_DEV
    block_ids = route_ids.reshape(block_count, TOK_DEV, TOPK)
    slot_index = jax.vmap(lambda single: slot_numbers(single, EXPERTS))(block_ids).reshape(ROWS, TOPK)
    gate_share = 2.5 * route_gates / jnp.sum(route_gates, axis=1, keepdims=True)
    row_number = jnp.broadcast_to(jnp.arange(ROWS, dtype=jnp.int32)[:, None], (ROWS, TOPK))
    block_number = (row_number // TOK_DEV).astype(jnp.int32)
    slot_table = jnp.full((EXPERTS, block_count, CAP), -1, jnp.int32).at[route_ids, block_number, slot_index].set(row_number)
    weight_table = jnp.zeros((EXPERTS, block_count, CAP), jnp.float32).at[route_ids, block_number, slot_index].set(gate_share)

    def add_expert(running_sum, expert):
        chosen = slot_table[expert].reshape(-1)
        safe_rows = jnp.maximum(chosen, 0)
        out_rows = expert_rows(moe_rows[safe_rows], w_gate[expert], w_up[expert], w_down[expert])
        term_rows = weight_table[expert].reshape(-1)[:, None] * out_rows.astype(jnp.float32)
        return running_sum.at[safe_rows].add(term_rows), None

    running_sum, _ = lax.scan(add_expert, jnp.zeros((ROWS, D), jnp.float32), jnp.arange(EXPERTS, dtype=jnp.int32))
    moe_out = running_sum.astype(jnp.bfloat16)

    latent_f = cache_latent.astype(jnp.float32)
    scores = jnp.einsum("rhc,rjc->rhj", query_latent.astype(jnp.float32), latent_f)
    scores = (scores + jnp.einsum("rhp,rpj->rhj", query_rope.astype(jnp.float32), cache_rope.astype(jnp.float32))) * score_scale
    in_range = jnp.arange(CACHE, dtype=jnp.int32)[None, None, :] < cache_lengths[:, None, None]
    scores = jnp.where(in_range, scores, -jnp.inf)
    row_peak = jnp.max(scores, axis=-1, keepdims=True)
    lifted = jnp.where(in_range, jnp.exp(scores - row_peak), 0.0)
    weights = (lifted / jnp.sum(lifted, axis=-1, keepdims=True)).astype(jnp.bfloat16)
    weights = lax.optimization_barrier(weights)
    attn_latent = jnp.einsum("rhj,rjc->rhc", weights.astype(jnp.float32), latent_f).astype(jnp.bfloat16)
    return (moe_out, attn_latent)
```

```python
import jax
import jax.numpy as jnp
import numpy as np
from jax import lax
from jax.sharding import PartitionSpec as P

score_scale = 192.0 ** (-0.5)
whole = ("node", "local")


def attention(query_latent, query_rope, cache_latent, cache_rope, cache_lengths):
    slot_count = cache_latent.shape[1]
    scores = jnp.einsum(
        "rhc,rjc->rhj", query_latent, cache_latent, preferred_element_type=jnp.float32
    )
    scores = (
        scores
        + jnp.einsum("rhp,rpj->rhj", query_rope, cache_rope, preferred_element_type=jnp.float32)
    ) * score_scale
    in_range = jnp.arange(slot_count, dtype=jnp.int32)[None, None, :] < cache_lengths[:, None, None]
    scores = jnp.where(in_range, scores, -jnp.inf)
    row_peak = jnp.max(scores, axis=-1, keepdims=True)
    lifted = jnp.where(in_range, jnp.exp(scores - row_peak), 0.0)
    weights = (lifted / jnp.sum(lifted, axis=-1, keepdims=True)).astype(jnp.bfloat16)
    return jnp.einsum(
        "rhj,rjc->rhc", weights, cache_latent, preferred_element_type=jnp.float32
    ).astype(jnp.bfloat16)


def share_columns(route_ids, route_gates, expert_count):
    gate_share = 2.5 * route_gates / jnp.sum(route_gates, axis=1, keepdims=True)
    chosen = route_ids[:, :, None] == jnp.arange(expert_count, dtype=jnp.int32)[None, None, :]
    table = jnp.sum(jnp.where(chosen, gate_share[:, :, None], 0.0), axis=1)
    high = table.astype(jnp.bfloat16)
    low = (table - high.astype(jnp.float32)).astype(jnp.bfloat16)
    empty = jnp.zeros((table.shape[0], -2 * expert_count % 128), jnp.bfloat16)
    return jnp.concatenate([high, low, empty], axis=1)


class Grid:
    def __init__(self):
        nodes, local = lax.axis_size("node"), lax.axis_size("local")
        self.sizes = (nodes // 4, 2, 2, local)
        node = lax.axis_index("node")
        self.place = (node // 4, node // 2 % 2, node % 2, lax.axis_index("local"))

    def shift(self, value, digit, step):
        pairs = []
        for place in np.ndindex(*self.sizes):
            other = list(place)
            other[digit] = (other[digit] + step) % self.sizes[digit]
            pairs.append(
                (
                    int(np.ravel_multi_index(place, self.sizes)),
                    int(np.ravel_multi_index(other, self.sizes)),
                )
            )
        return lax.ppermute(value, whole, pairs)

    def scatter_sum(self, value, digit, dim):
        size, here = self.sizes[digit], self.place[digit]
        total = lax.dynamic_index_in_dim(value, here, dim, keepdims=False).astype(jnp.float32)
        for step in range(1, size):
            part = lax.dynamic_index_in_dim(value, (here + step) % size, dim, keepdims=False)
            total = total + self.shift(part, digit, step).astype(jnp.float32)
        return total.astype(value.dtype)


HIGH, MIDDLE, CORE, LOCAL = range(4)


def body(
    moe_rows,
    route_ids,
    route_gates,
    w_gate,
    w_up,
    w_down,
    query_latent,
    query_rope,
    cache_latent,
    cache_rope,
    cache_lengths,
):
    grid = Grid()
    experts = lax.axis_size("node")
    width = moe_rows.shape[1]
    outgoing = jnp.concatenate(
        [moe_rows, share_columns(route_ids, route_gates, experts)], axis=1
    )
    gathered = lax.all_gather(outgoing, whole, axis=0, tiled=True)
    attn_latent = attention(query_latent, query_rope, cache_latent, cache_rope, cache_lengths)
    rows = gathered[:, :width]
    table = gathered[:, width : width + 2 * experts].astype(jnp.float32)
    table = table[:, :experts] + table[:, experts:]
    mine = jnp.arange(experts, dtype=jnp.int32) == lax.axis_index("node")
    share = jnp.sum(jnp.where(mine[None, :], table, 0.0), axis=1, keepdims=True)
    gate_act = jnp.dot(rows, w_gate[0], preferred_element_type=jnp.float32)
    up_act = jnp.dot(rows, w_up[0], preferred_element_type=jnp.float32)
    hidden = (jax.nn.silu(gate_act) * up_act).astype(jnp.bfloat16)
    pieces = []
    half = width // 2
    for piece in range(2):
        columns = w_down[0][:, piece * half : (piece + 1) * half]
        product = share * jnp.dot(hidden, columns, preferred_element_type=jnp.float32)
        product = product.astype(jnp.bfloat16).reshape(grid.sizes + (-1, half))
        product = grid.scatter_sum(product, CORE, 2)
        if piece == 0:
            product = grid.scatter_sum(product, LOCAL, 2)
            product = grid.scatter_sum(product, MIDDLE, 1)
        else:
            product = grid.scatter_sum(product, MIDDLE, 1)
            product = grid.scatter_sum(product, LOCAL, 1)
        pieces.append(grid.scatter_sum(product, HIGH, 0))
    moe_out = jnp.concatenate(pieces, axis=1)
    return (moe_out, attn_latent)


def solution(mesh):
    rows = P(("group", "node", "local"), None)
    blocks = P(("group", "node", "local"), None, None)
    return jax.shard_map(
        body,
        mesh=mesh,
        in_specs=(
            rows,
            rows,
            rows,
            P("node", None, "local"),
            P("node", None, "local"),
            P("node", "local", None),
            blocks,
            blocks,
            blocks,
            blocks,
            P(("group", "node", "local")),
        ),
        out_specs=(rows, blocks),
        check_vma=False,
    )
```

```python
import jax
import jax.numpy as jnp
import numpy as np
from jax import lax
from jax.sharding import PartitionSpec as P

score_scale = 192.0 ** (-0.5)
whole = ("node", "local")


def attention(query_latent, query_rope, cache_latent, cache_rope, cache_lengths):
    slot_count = cache_latent.shape[1]
    scores = jnp.einsum(
        "rhc,rjc->rhj", query_latent, cache_latent, preferred_element_type=jnp.float32
    )
    scores = (
        scores
        + jnp.einsum("rhp,rpj->rhj", query_rope, cache_rope, preferred_element_type=jnp.float32)
    ) * score_scale
    in_range = jnp.arange(slot_count, dtype=jnp.int32)[None, None, :] < cache_lengths[:, None, None]
    scores = jnp.where(in_range, scores, -jnp.inf)
    row_peak = jnp.max(scores, axis=-1, keepdims=True)
    lifted = jnp.where(in_range, jnp.exp(scores - row_peak), 0.0)
    weights = (lifted / jnp.sum(lifted, axis=-1, keepdims=True)).astype(jnp.bfloat16)
    return jnp.einsum(
        "rhj,rjc->rhc", weights, cache_latent, preferred_element_type=jnp.float32
    ).astype(jnp.bfloat16)


def share_columns(route_ids, route_gates, expert_count):
    gate_share = 2.5 * route_gates / jnp.sum(route_gates, axis=1, keepdims=True)
    chosen = route_ids[:, :, None] == jnp.arange(expert_count, dtype=jnp.int32)[None, None, :]
    table = jnp.sum(jnp.where(chosen, gate_share[:, :, None], 0.0), axis=1)
    high = table.astype(jnp.bfloat16)
    low = (table - high.astype(jnp.float32)).astype(jnp.bfloat16)
    empty = jnp.zeros((table.shape[0], -2 * expert_count % 128), jnp.bfloat16)
    return jnp.concatenate([high, low, empty], axis=1)


class Grid:
    def __init__(self):
        nodes, local = lax.axis_size("node"), lax.axis_size("local")
        self.sizes = (nodes // 4, 2, 2, local)

    def shift(self, value, digit, step):
        pairs = []
        for place in np.ndindex(*self.sizes):
            other = list(place)
            other[digit] = (other[digit] + step) % self.sizes[digit]
            pairs.append(
                (
                    int(np.ravel_multi_index(place, self.sizes)),
                    int(np.ravel_multi_index(other, self.sizes)),
                )
            )
        return lax.ppermute(value, whole, pairs)

    def gather(self, value, digit, dim):
        blocks = [value]
        for step in range(1, self.sizes[digit]):
            blocks.append(self.shift(value, digit, step))
        return jnp.stack(blocks, axis=dim)

    def scatter_sum(self, value, digit, dim):
        size = self.sizes[digit]
        total = lax.index_in_dim(value, 0, dim, keepdims=False).astype(jnp.float32)
        for step in range(1, size):
            part = lax.index_in_dim(value, step, dim, keepdims=False)
            total = total + self.shift(part, digit, size - step).astype(jnp.float32)
        return total.astype(value.dtype)


HIGH, MIDDLE, CORE, LOCAL = range(4)


def body(
    moe_rows,
    route_ids,
    route_gates,
    w_gate,
    w_up,
    w_down,
    query_latent,
    query_rope,
    cache_latent,
    cache_rope,
    cache_lengths,
):
    grid = Grid()
    experts = lax.axis_size("node")
    width = moe_rows.shape[1]
    half = width // 2
    shares = share_columns(route_ids, route_gates, experts)
    outgoing = jnp.concatenate([moe_rows, shares], axis=1)
    column = grid.gather(outgoing, HIGH, 0)
    first = grid.gather(column[..., :half], LOCAL, 0)
    second = grid.gather(column[..., half:], MIDDLE, 0)
    first = grid.gather(first, MIDDLE, 0)
    second = grid.gather(second, LOCAL, 1)
    first = grid.gather(first, CORE, 0).reshape(-1, half)
    second = grid.gather(second, CORE, 0).reshape(first.shape[0], -1)
    attn_latent = attention(query_latent, query_rope, cache_latent, cache_rope, cache_lengths)
    table = second[:, half : half + 2 * experts].astype(jnp.float32)
    second = second[:, :half]
    table = table[:, :experts] + table[:, experts:]
    mine = jnp.arange(experts, dtype=jnp.int32) == lax.axis_index("node")
    share = jnp.sum(jnp.where(mine[None, :], table, 0.0), axis=1, keepdims=True)

    def project(weight):
        lower = jnp.dot(first, weight[:half], preferred_element_type=jnp.float32)
        upper = jnp.dot(second, weight[half:], preferred_element_type=jnp.float32)
        return lower + upper

    hidden = (jax.nn.silu(project(w_gate[0])) * project(w_up[0])).astype(jnp.bfloat16)
    pieces = []
    for piece in range(2):
        columns = w_down[0][:, piece * half : (piece + 1) * half]
        product = share * jnp.dot(hidden, columns, preferred_element_type=jnp.float32)
        product = product.astype(jnp.bfloat16)
        product = product.reshape(
            grid.sizes[CORE], grid.sizes[MIDDLE], grid.sizes[LOCAL], grid.sizes[HIGH], -1, half
        )
        product = grid.scatter_sum(product, CORE, 0)
        if piece == 0:
            product = grid.scatter_sum(product, MIDDLE, 0)
            product = grid.scatter_sum(product, LOCAL, 0)
        else:
            product = grid.scatter_sum(product, LOCAL, 1)
            product = grid.scatter_sum(product, MIDDLE, 0)
        pieces.append(grid.scatter_sum(product, HIGH, 0))
    moe_out = jnp.concatenate(pieces, axis=1)
    return (moe_out, attn_latent)


def solution(mesh):
    rows = P(("group", "node", "local"), None)
    blocks = P(("group", "node", "local"), None, None)
    return jax.shard_map(
        body,
        mesh=mesh,
        in_specs=(
            rows,
            rows,
            rows,
            P("node", None, "local"),
            P("node", None, "local"),
            P("node", "local", None),
            blocks,
            blocks,
            blocks,
            blocks,
            P(("group", "node", "local")),
        ),
        out_specs=(rows, blocks),
        check_vma=False,
    )
```

```python
import functools

import jax
import jax.numpy as jnp
import numpy as np
from jax import lax
from jax.experimental import pallas as pl
from jax.experimental.pallas import tpu as pltpu
from jax.sharding import Mesh
from jax.sharding import PartitionSpec as P

score_scale = 192.0 ** (-0.5)
everyone = ("high", "middle", "core", "local")
MEBI = 1024 * 1024


def attention(query_latent, query_rope, cache_latent, cache_rope, cache_lengths):
    slot_count = cache_latent.shape[1]
    scores = jnp.einsum(
        "rhc,rjc->rhj", query_latent, cache_latent, preferred_element_type=jnp.float32
    )
    scores = (
        scores
        + jnp.einsum("rhp,rpj->rhj", query_rope, cache_rope, preferred_element_type=jnp.float32)
    ) * score_scale
    in_range = jnp.arange(slot_count, dtype=jnp.int32)[None, None, :] < cache_lengths[:, None, None]
    scores = jnp.where(in_range, scores, -jnp.inf)
    row_peak = jnp.max(scores, axis=-1, keepdims=True)
    lifted = jnp.where(in_range, jnp.exp(scores - row_peak), 0.0)
    weights = (lifted / jnp.sum(lifted, axis=-1, keepdims=True)).astype(jnp.bfloat16)
    return jnp.einsum(
        "rhj,rjc->rhc", weights, cache_latent, preferred_element_type=jnp.float32
    ).astype(jnp.bfloat16)


class Grid:
    def __init__(self):
        self.sizes = tuple(lax.axis_size(name) for name in everyone)
        self.mixed = self.sizes[1] == self.sizes[3]

    def shift(self, value, pick, step):
        pairs = []
        for place in np.ndindex(*self.sizes):
            other = list(place)
            digit = pick(place[2])
            other[digit] = (other[digit] + step) % self.sizes[digit]
            pairs.append(
                (
                    int(np.ravel_multi_index(place, self.sizes)),
                    int(np.ravel_multi_index(other, self.sizes)),
                )
            )
        return lax.ppermute(value, everyone, pairs)

    def first(self, core):
        return 1 if self.mixed and core == 1 else 3

    def second(self, core):
        return 3 if self.mixed and core == 1 else 1

    def core(self, core):
        return 2

    def gather(self, line):
        near = [line]
        for step in range(1, self.sizes[self.first(0)]):
            near.append(self.shift(line, self.first, step))
        mine = list(near)
        for step in range(1, self.sizes[self.second(0)]):
            mine += [self.shift(block, self.second, step) for block in near]
        other = [self.shift(block, self.core, 1) for block in mine]
        return mine + other

    def scatter_sum(self, blocks):
        def add(parts):
            total = parts[0].astype(jnp.float32)
            for part in parts[1:]:
                total = total + part.astype(jnp.float32)
            return total.astype(parts[0].dtype)

        count = len(blocks) // 2
        mine = [
            add([blocks[i], self.shift(blocks[count + i], self.core, 1)])
            for i in reversed(range(count))
        ][::-1]
        extent = self.sizes[self.second(0)]
        wide = count // extent
        near = []
        for i in reversed(range(wide)):
            parts = [mine[i]]
            for step in range(1, extent):
                parts.append(self.shift(mine[step * wide + i], self.second, extent - step))
            near.append(add(parts))
        near = near[::-1]
        parts = [near[0]]
        for step in range(1, wide):
            parts.append(self.shift(near[step], self.first, wide - step))
        return add(parts)


def pack_kernel(experts, rows_ref, ids_ref, gates_ref, out_ref):
    copies, _, total = out_ref.shape
    width = rows_ref.shape[1]
    extra = total - width
    gates = gates_ref[...]
    shares = 2.5 * gates / jnp.sum(gates, axis=1, keepdims=True)
    ids = ids_ref[...]
    lane = lax.broadcasted_iota(jnp.int32, (ids.shape[0], extra), 1)
    expert = jnp.where(lane < experts, lane, lane - experts)
    table = jnp.zeros(lane.shape, jnp.float32)
    for k in range(ids.shape[1]):
        table += jnp.where(expert == ids[:, k : k + 1], shares[:, k : k + 1], 0.0)
    high = table.astype(jnp.bfloat16).astype(jnp.float32)
    table = jnp.where(lane < experts, high, jnp.where(lane < 2 * experts, table - high, 0.0))
    table = table.astype(jnp.bfloat16)
    for copy in range(copies):
        out_ref[copy, :, :width] = rows_ref[...]
        out_ref[copy, :, width:] = table


def pack(copies, experts, moe_rows, route_ids, route_gates):
    rows, width = moe_rows.shape
    total = width + pl.cdiv(2 * experts, 128) * 128
    return pl.pallas_call(
        functools.partial(pack_kernel, experts),
        out_shape=jax.ShapeDtypeStruct((copies, rows, total), jnp.bfloat16),
        name="pack",
    )(moe_rows, route_ids, route_gates)


def hidden_kernel(count, experts, node_ref, *refs):
    blocks, tails = refs[:count], refs[count : 2 * count]
    gate_ref, up_ref, hidden_ref, share_ref, gate_sum, up_sum = refs[2 * count :]
    step = pl.program_id(0)

    @pl.when(step == 0)
    def _():
        gate_sum[...] = jnp.zeros_like(gate_sum)
        up_sum[...] = jnp.zeros_like(up_sum)
        table = jnp.concatenate([tail[...] for tail in tails], axis=0).astype(jnp.float32)
        lane = lax.broadcasted_iota(jnp.int32, table.shape, 1)
        mine = (lane == node_ref[0]) | (lane == node_ref[0] + experts)
        share = jnp.sum(jnp.where(mine, table, 0.0), axis=1, keepdims=True)
        share_ref[...] = jnp.broadcast_to(share, share_ref.shape)

    rows = jnp.concatenate([block[...] for block in blocks], axis=0)
    gate_sum[...] += jnp.dot(rows, gate_ref[...], preferred_element_type=jnp.float32)
    up_sum[...] += jnp.dot(rows, up_ref[...], preferred_element_type=jnp.float32)

    @pl.when(step == pl.num_programs(0) - 1)
    def _():
        hidden_ref[...] = (jax.nn.silu(gate_sum[...]) * up_sum[...]).astype(jnp.bfloat16)


def hidden_of(blocks, w_gate, w_up, experts, node):
    width, units = w_gate.shape
    count, size = len(blocks), blocks[0].shape[0]
    tail = blocks[0].shape[1] - width
    rows = count * size
    tile = 1024
    return pl.pallas_call(
        functools.partial(hidden_kernel, count, experts),
        grid_spec=pltpu.PrefetchScalarGridSpec(
            num_scalar_prefetch=1,
            grid=(width // tile,),
            in_specs=[pl.BlockSpec((size, tile), lambda j, node: (0, j))] * count
            + [pl.BlockSpec((size, tail), lambda j, node: (0, width // tail))] * count
            + [pl.BlockSpec((tile, units), lambda j, node: (j, 0))] * 2,
            out_specs=[
                pl.BlockSpec((rows, units), lambda j, node: (0, 0)),
                pl.BlockSpec((rows, 128), lambda j, node: (0, 0)),
            ],
            scratch_shapes=[pltpu.VMEM((rows, units), jnp.float32)] * 2,
        ),
        out_shape=[
            jax.ShapeDtypeStruct((rows, units), jnp.bfloat16),
            jax.ShapeDtypeStruct((rows, 128), jnp.float32),
        ],
        cost_estimate=pl.CostEstimate(
            flops=4 * rows * width * units,
            bytes_accessed=4 * width * units + 2 * rows * width,
            transcendentals=rows * units,
        ),
        compiler_params=pltpu.CompilerParams(vmem_limit_bytes=24 * MEBI),
        name="gate_up",
    )(node, *blocks, *blocks, w_gate, w_up)


def down_kernel(hidden_ref, share_ref, down_ref, *outs):
    product = jnp.dot(hidden_ref[...], down_ref[...], preferred_element_type=jnp.float32)
    product = (product * share_ref[:, :1]).astype(jnp.bfloat16)
    size = outs[0].shape[0]
    for i, out in enumerate(outs):
        out[...] = product[i * size : (i + 1) * size]


def down_of(hidden, share, w_down, count, start, columns):
    rows, units = hidden.shape
    size = rows // count
    tile = 512
    offset = start // tile
    return pl.pallas_call(
        down_kernel,
        grid=(columns // tile,),
        in_specs=[
            pl.BlockSpec((rows, units), lambda j: (0, 0)),
            pl.BlockSpec((rows, 128), lambda j: (0, 0)),
            pl.BlockSpec((units, tile), lambda j: (0, j + offset)),
        ],
        out_specs=[pl.BlockSpec((size, tile), lambda j: (0, j))] * count,
        out_shape=[jax.ShapeDtypeStruct((size, columns), jnp.bfloat16)] * count,
        cost_estimate=pl.CostEstimate(
            flops=2 * rows * columns * units,
            bytes_accessed=2 * columns * (units + rows),
            transcendentals=0,
        ),
        compiler_params=pltpu.CompilerParams(vmem_limit_bytes=16 * MEBI),
        name="down",
    )(hidden, share, w_down)


def body(
    moe_rows,
    route_ids,
    route_gates,
    w_gate,
    w_up,
    w_down,
    query_latent,
    query_rope,
    cache_latent,
    cache_rope,
    cache_lengths,
):
    grid = Grid()
    high, middle, cores, _ = grid.sizes
    experts = high * middle * cores
    tokens, width = moe_rows.shape
    node = lax.axis_index(("high", "middle", "core")).astype(jnp.int32).reshape(1)
    outgoing = pack(high, experts, moe_rows, route_ids, route_gates)
    line = lax.all_to_all(outgoing, "high", split_axis=0, concat_axis=0, tiled=True)
    blocks = grid.gather(line.reshape(high * tokens, -1))
    attn_latent = attention(query_latent, query_rope, cache_latent, cache_rope, cache_lengths)
    hidden, share = hidden_of(blocks, w_gate[0], w_up[0], experts, node)
    pieces = []
    half = width // 2
    for piece in range(2):
        products = down_of(hidden, share, w_down[0], len(blocks), piece * half, half)
        total = grid.scatter_sum(products).reshape(high, tokens, half)
        parts = lax.all_to_all(total, "high", split_axis=0, concat_axis=0, tiled=True)
        pieces.append(jnp.sum(parts.astype(jnp.float32), axis=0).astype(jnp.bfloat16))
    return (jnp.concatenate(pieces, axis=1), attn_latent)


def solution(mesh):
    groups, nodes, local = mesh.devices.shape
    split = Mesh(mesh.devices.reshape(groups, nodes // 4, 2, 2, local), ("group",) + everyone)
    node = ("high", "middle", "core")
    whole = ("group",) + everyone
    rows = P(whole, None)
    blocks = P(whole, None, None)
    return jax.shard_map(
        body,
        mesh=split,
        in_specs=(
            rows,
            rows,
            rows,
            P(node, None, "local"),
            P(node, None, "local"),
            P(node, "local", None),
            blocks,
            blocks,
            blocks,
            blocks,
            P(whole),
        ),
        out_specs=(rows, blocks),
        check_vma=False,
    )
```

```python
import functools

import jax
import jax.numpy as jnp
import numpy as np
from jax import lax
from jax.experimental import pallas as pl
from jax.experimental.pallas import tpu as pltpu
from jax.sharding import Mesh
from jax.sharding import PartitionSpec as P

score_scale = 192.0 ** (-0.5)
everyone = ("high", "middle", "core", "local")
MEBI = 1024 * 1024


def attention(query_latent, query_rope, cache_latent, cache_rope, cache_lengths):
    slot_count = cache_latent.shape[1]
    scores = jnp.einsum(
        "rhc,rjc->rhj", query_latent, cache_latent, preferred_element_type=jnp.float32
    )
    scores = (
        scores
        + jnp.einsum("rhp,rpj->rhj", query_rope, cache_rope, preferred_element_type=jnp.float32)
    ) * score_scale
    in_range = jnp.arange(slot_count, dtype=jnp.int32)[None, None, :] < cache_lengths[:, None, None]
    scores = jnp.where(in_range, scores, -jnp.inf)
    row_peak = jnp.max(scores, axis=-1, keepdims=True)
    lifted = jnp.where(in_range, jnp.exp(scores - row_peak), 0.0)
    weights = (lifted / jnp.sum(lifted, axis=-1, keepdims=True)).astype(jnp.bfloat16)
    return jnp.einsum(
        "rhj,rjc->rhc", weights, cache_latent, preferred_element_type=jnp.float32
    ).astype(jnp.bfloat16)


class Grid:
    def __init__(self):
        self.sizes = tuple(lax.axis_size(name) for name in everyone)
        self.mixed = self.sizes[1] == self.sizes[3]

    def swap(self, value, pick, mask):
        pairs = []
        for place in np.ndindex(*self.sizes):
            other = list(place)
            other[pick(place[2])] ^= mask
            pairs.append(
                (
                    int(np.ravel_multi_index(place, self.sizes)),
                    int(np.ravel_multi_index(other, self.sizes)),
                )
            )
        return lax.ppermute(value, everyone, pairs)

    def high(self, core):
        return 0

    def core(self, core):
        return 2

    def first(self, core):
        return 1 if self.mixed and core == 1 else 3

    def second(self, core):
        return 3 if self.mixed and core == 1 else 1

    def extent(self, pick):
        return self.sizes[pick(0)]

    def gather(self, rows):
        lines = [rows] + [self.swap(rows, self.high, m) for m in range(1, self.extent(self.high))]
        half = len(lines) // 2
        places = []
        for lines in (lines[:half], lines[half:]):
            line = jnp.concatenate(lines, axis=0)
            near = [line]
            near += [self.swap(line, self.first, m) for m in range(1, self.extent(self.first))]
            mine = list(near)
            for m in range(1, self.extent(self.second)):
                mine += [self.swap(block, self.second, m) for block in near]
            places.append(mine + [self.swap(block, self.core, 1) for block in mine])
        return [list(blocks) for blocks in zip(*places)]

    def scatter_sum(self, mine, other):
        size = mine[0].shape[0]
        last, rest = [self.swap(part, self.core, 1) for part in other]
        sums = [add([mine[-1], last])]
        for i in range(len(mine) - 1):
            sums.insert(i, add([mine[i], rest[i * size : (i + 1) * size]]))
        wide = self.extent(self.first)
        near = []
        for i in range(wide):
            parts = [sums[i]]
            for m in range(1, self.extent(self.second)):
                parts.append(self.swap(sums[m * wide + i], self.second, m))
            near.append(parts)
        near = [add(parts) for parts in near]
        line = add([near[0]] + [self.swap(near[m], self.first, m) for m in range(1, wide)])
        rows = size // self.extent(self.high)
        parts = [line[:rows]]
        for m in range(1, self.extent(self.high)):
            parts.append(self.swap(line[m * rows : (m + 1) * rows], self.high, m))
        return add(parts)


def add(parts):
    total = parts[0].astype(jnp.float32)
    for part in parts[1:]:
        total = total + part.astype(jnp.float32)
    return total.astype(parts[0].dtype)


def pack_kernel(experts, rows_ref, ids_ref, gates_ref, out_ref):
    width = rows_ref.shape[1]
    extra = out_ref.shape[1] - width
    gates = gates_ref[...]
    shares = 2.5 * gates / jnp.sum(gates, axis=1, keepdims=True)
    ids = ids_ref[...]
    lane = lax.broadcasted_iota(jnp.int32, (ids.shape[0], extra), 1)
    expert = jnp.where(lane < experts, lane, lane - experts)
    table = jnp.zeros(lane.shape, jnp.float32)
    for k in range(ids.shape[1]):
        table += jnp.where(expert == ids[:, k : k + 1], shares[:, k : k + 1], 0.0)
    high = table.astype(jnp.bfloat16).astype(jnp.float32)
    table = jnp.where(lane < experts, high, jnp.where(lane < 2 * experts, table - high, 0.0))
    out_ref[:, :width] = rows_ref[...]
    out_ref[:, width:] = table.astype(jnp.bfloat16)


def pack(experts, moe_rows, route_ids, route_gates):
    rows, width = moe_rows.shape
    total = width + pl.cdiv(2 * experts, 128) * 128
    return pl.pallas_call(
        functools.partial(pack_kernel, experts),
        out_shape=jax.ShapeDtypeStruct((rows, total), jnp.bfloat16),
        name="pack",
    )(moe_rows, route_ids, route_gates)


def spread(product, outs):
    start = 0
    for out, columns in outs:
        size = out.shape[0]
        out[:, columns] = product[start : start + size]
        start += size


def expert_kernel(count, outputs, experts, tile, down_tile, node_ref, *refs):
    blocks = refs[:count]
    gate_hbm, up_hbm, down_hbm, hidden_ref, share_ref = refs[count : count + 5]
    outs = refs[count + 5 : count + 5 + outputs]
    gate, up, down, gate_sum, up_sum, gate_sem, up_sem, down_sem = refs[count + 5 + outputs :]
    width = gate.shape[0]
    columns = down.shape[1]
    steps = [pl.ds(k, tile) for k in range(0, width, tile)]
    down_steps = [pl.ds(k, down_tile) for k in range(0, columns, down_tile)]
    copies = []
    for k, part in enumerate(steps):
        pair = (
            pltpu.make_async_copy(gate_hbm.at[part], gate.at[part], gate_sem.at[k]),
            pltpu.make_async_copy(up_hbm.at[part], up.at[part], up_sem.at[k]),
        )
        for copy in pair:
            copy.start()
        copies.append(pair)
    down_copies = []
    for k, part in enumerate(down_steps):
        copy = pltpu.make_async_copy(down_hbm.at[:, part], down.at[:, part], down_sem.at[k])
        copy.start()
        down_copies.append(copy)

    table = jnp.concatenate([block[:, width:] for block in blocks], axis=0).astype(jnp.float32)
    lane = lax.broadcasted_iota(jnp.int32, table.shape, 1)
    mine = (lane == node_ref[0]) | (lane == node_ref[0] + experts)
    share = jnp.sum(jnp.where(mine, table, 0.0), axis=1, keepdims=True)
    share_ref[...] = jnp.broadcast_to(share, share_ref.shape)

    for k, part in enumerate(steps):
        rows = jnp.concatenate([block[:, part] for block in blocks], axis=0)
        for copy, weight, total in zip(copies[k], (gate, up), (gate_sum, up_sum)):
            copy.wait()
            product = jnp.dot(rows, weight[part], preferred_element_type=jnp.float32)
            if k == 0:
                total[...] = product
            else:
                total[...] += product
    hidden_ref[...] = (jax.nn.silu(gate_sum[...]) * up_sum[...]).astype(jnp.bfloat16)
    for k, part in enumerate(down_steps):
        down_copies[k].wait()
        product = jnp.dot(hidden_ref[...], down[:, part], preferred_element_type=jnp.float32)
        product = (product * share_ref[:, :1]).astype(jnp.bfloat16)
        spread(product, [(out, part) for out in outs])


def expert(blocks, w_gate, w_up, w_down, experts, node, sizes, columns):
    width, units = w_gate.shape
    rows = sum(sizes)
    tile, down_tile = 1024, 512
    return pl.pallas_call(
        functools.partial(
            expert_kernel, len(blocks), len(sizes), experts, tile, down_tile
        ),
        in_specs=[pl.BlockSpec(memory_space=pltpu.SMEM)]
        + [pl.BlockSpec(memory_space=pltpu.VMEM)] * len(blocks)
        + [pl.BlockSpec(memory_space=pl.ANY)] * 3,
        out_specs=[pl.BlockSpec(memory_space=pltpu.VMEM)] * (2 + len(sizes)),
        out_shape=[
            jax.ShapeDtypeStruct((rows, units), jnp.bfloat16),
            jax.ShapeDtypeStruct((rows, 128), jnp.float32),
        ]
        + [jax.ShapeDtypeStruct((size, columns), jnp.bfloat16) for size in sizes],
        scratch_shapes=[
            pltpu.VMEM((width, units), jnp.bfloat16),
            pltpu.VMEM((width, units), jnp.bfloat16),
            pltpu.VMEM((units, columns), jnp.bfloat16),
            pltpu.VMEM((rows, units), jnp.float32),
            pltpu.VMEM((rows, units), jnp.float32),
            pltpu.SemaphoreType.DMA((width // tile,)),
            pltpu.SemaphoreType.DMA((width // tile,)),
            pltpu.SemaphoreType.DMA((columns // down_tile,)),
        ],
        cost_estimate=pl.CostEstimate(
            flops=4 * rows * width * units + 2 * rows * columns * units,
            bytes_accessed=4 * width * units + 2 * units * columns,
            transcendentals=rows * units,
        ),
        compiler_params=pltpu.CompilerParams(vmem_limit_bytes=40 * MEBI),
        name="expert",
    )(node, *blocks, w_gate, w_up, w_down)


def down_kernel(hidden_ref, share_ref, down_ref, *outs):
    product = jnp.dot(hidden_ref[...], down_ref[...], preferred_element_type=jnp.float32)
    product = (product * share_ref[:, :1]).astype(jnp.bfloat16)
    spread(product, [(out, pl.ds(0, product.shape[1])) for out in outs])


def down_of(hidden, share, w_down, sizes, start):
    rows, units = hidden.shape
    columns = w_down.shape[1] - start
    tile = 1024
    offset = start // tile
    return pl.pallas_call(
        down_kernel,
        grid=(columns // tile,),
        in_specs=[
            pl.BlockSpec(memory_space=pltpu.VMEM),
            pl.BlockSpec(memory_space=pltpu.VMEM),
            pl.BlockSpec((units, tile), lambda j: (0, j + offset)),
        ],
        out_specs=[pl.BlockSpec((size, tile), lambda j: (0, j)) for size in sizes],
        out_shape=[jax.ShapeDtypeStruct((size, columns), jnp.bfloat16) for size in sizes],
        cost_estimate=pl.CostEstimate(
            flops=2 * rows * columns * units,
            bytes_accessed=2 * columns * (units + rows),
            transcendentals=0,
        ),
        compiler_params=pltpu.CompilerParams(vmem_limit_bytes=40 * MEBI),
        name="down",
    )(hidden, share, w_down)


def body(
    moe_rows,
    route_ids,
    route_gates,
    w_gate,
    w_up,
    w_down,
    query_latent,
    query_rope,
    cache_latent,
    cache_rope,
    cache_lengths,
):
    grid = Grid()
    high, middle, cores, _ = grid.sizes
    experts = high * middle * cores
    tokens, width = moe_rows.shape
    node = lax.axis_index(("high", "middle", "core")).astype(jnp.int32).reshape(1)
    places = grid.gather(pack(experts, moe_rows, route_ids, route_gates))
    attn_latent = attention(query_latent, query_rope, cache_latent, cache_rope, cache_lengths)
    size = high * tokens
    count = len(places) // 2
    sizes = [size] * count + [size, size * (count - 1)]
    places = places[:count] + places[-1:] + places[count:-1]
    blocks = [block for place in places for block in place]
    split = width * 4 // 7
    hidden, share, *products = expert(
        blocks, w_gate[0], w_up[0], w_down[0], experts, node, sizes, split
    )
    lower = grid.scatter_sum(products[:count], products[count:])
    products = down_of(hidden, share, w_down[0], sizes, split)
    upper = grid.scatter_sum(products[:count], products[count:])
    return (jnp.concatenate([lower, upper], axis=1), attn_latent)


def solution(mesh):
    groups, nodes, local = mesh.devices.shape
    split = Mesh(mesh.devices.reshape(groups, nodes // 4, 2, 2, local), ("group",) + everyone)
    node = ("high", "middle", "core")
    whole = ("group",) + everyone
    rows = P(whole, None)
    blocks = P(whole, None, None)
    return jax.shard_map(
        body,
        mesh=split,
        in_specs=(
            rows,
            rows,
            rows,
            P(node, None, "local"),
            P(node, None, "local"),
            P(node, "local", None),
            blocks,
            blocks,
            blocks,
            blocks,
            P(whole),
        ),
        out_specs=(rows, blocks),
        check_vma=False,
    )
```

```python
import functools

import jax
import jax.numpy as jnp
import numpy as np
from jax import lax
from jax.experimental import pallas as pl
from jax.experimental.pallas import tpu as pltpu
from jax.sharding import Mesh
from jax.sharding import PartitionSpec as P

score_scale = 192.0 ** (-0.5)
everyone = ("high", "middle", "core", "local")
MEBI = 1024 * 1024


def attention_kernel(lengths_ref, query_ref, query_rope_ref, cache_ref, cache_rope_ref, out_ref):
    for row in range(query_ref.shape[0]):
        cache = cache_ref[row]
        scores = lax.dot_general(
            query_ref[row], cache, (((1,), (1,)), ((), ())), preferred_element_type=jnp.float32
        )
        scores += jnp.dot(
            query_rope_ref[row], cache_rope_ref[row], preferred_element_type=jnp.float32
        )
        slot = lax.broadcasted_iota(jnp.int32, scores.shape, 1)
        in_range = slot < lengths_ref[row]
        scores = jnp.where(in_range, scores * score_scale, -jnp.inf)
        row_peak = jnp.max(scores, axis=1, keepdims=True)
        lifted = jnp.where(in_range, jnp.exp(scores - row_peak), 0.0)
        weights = (lifted / jnp.sum(lifted, axis=1, keepdims=True)).astype(jnp.bfloat16)
        value = jnp.dot(weights, cache, preferred_element_type=jnp.float32)
        out_ref[row] = value.astype(jnp.bfloat16)


def attention(query_latent, query_rope, cache_latent, cache_rope, cache_lengths):
    rows, heads, latent = query_latent.shape
    slots = cache_latent.shape[1]
    return pl.pallas_call(
        attention_kernel,
        in_specs=[pl.BlockSpec(memory_space=pltpu.SMEM)]
        + [pl.BlockSpec(memory_space=pltpu.VMEM)] * 4,
        out_specs=pl.BlockSpec(memory_space=pltpu.VMEM),
        out_shape=jax.ShapeDtypeStruct(query_latent.shape, jnp.bfloat16),
        cost_estimate=pl.CostEstimate(
            flops=4 * rows * heads * slots * latent,
            bytes_accessed=2 * rows * slots * latent,
            transcendentals=rows * heads * slots,
        ),
        compiler_params=pltpu.CompilerParams(vmem_limit_bytes=8 * MEBI),
        name="attention",
    )(cache_lengths, query_latent, query_rope, cache_latent, cache_rope)


class Grid:
    def __init__(self):
        self.sizes = tuple(lax.axis_size(name) for name in everyone)
        self.mixed = self.sizes[1] == self.sizes[3]

    def swap(self, value, pick, mask):
        pairs = []
        for place in np.ndindex(*self.sizes):
            other = list(place)
            other[pick(place[2])] ^= mask
            pairs.append(
                (
                    int(np.ravel_multi_index(place, self.sizes)),
                    int(np.ravel_multi_index(other, self.sizes)),
                )
            )
        return lax.ppermute(value, everyone, pairs)

    def high(self, core):
        return 0

    def core(self, core):
        return 2

    def first(self, core):
        return 1 if self.mixed and core == 1 else 3

    def second(self, core):
        return 3 if self.mixed and core == 1 else 1

    def extent(self, pick):
        return self.sizes[pick(0)]

    def gather(self, rows, weights):
        weights = list(weights)
        lines = [rows] + [self.swap(rows, self.high, m) for m in range(1, self.extent(self.high))]
        half = len(lines) // 2
        places = []
        for lines in (lines[:half], lines[half:]):
            line = jnp.concatenate(lines, axis=0)
            if places:
                line, places[0][1], weights[0] = lax.optimization_barrier(
                    (line, places[0][1], weights[0])
                )
            near = [line]
            near += [self.swap(line, self.first, m) for m in range(1, self.extent(self.first))]
            if places:
                near[-1], weights[1] = lax.optimization_barrier((near[-1], weights[1]))
            mine = list(near)
            for m in range(1, self.extent(self.second)):
                mine += [self.swap(block, self.second, m) for block in near]
            if places:
                mine[-1], weights[2] = lax.optimization_barrier((mine[-1], weights[2]))
            places.append(mine + [self.swap(block, self.core, 1) for block in mine])
        return [list(blocks) for blocks in zip(*places)], weights

    def last_sum(self, mine, other):
        return add([mine[-1], self.swap(other[0], self.core, 1)])

    def scatter_sum(self, mine, other, last):
        size = mine[0].shape[0]
        rest = self.swap(other[1], self.core, 1)
        sums = [last]
        for i in range(len(mine) - 1):
            sums.insert(i, add([mine[i], rest[i * size : (i + 1) * size]]))
        wide = self.extent(self.first)
        near = []
        for i in range(wide):
            parts = [sums[i]]
            for m in range(1, self.extent(self.second)):
                parts.append(self.swap(sums[m * wide + i], self.second, m))
            near.append(parts)
        near = [add(parts) for parts in near]
        line = add([near[0]] + [self.swap(near[m], self.first, m) for m in range(1, wide)])
        rows = size // self.extent(self.high)
        parts = [line[:rows]]
        for m in range(1, self.extent(self.high)):
            parts.append(self.swap(line[m * rows : (m + 1) * rows], self.high, m))
        return add(parts)


def add(parts):
    total = parts[0].astype(jnp.float32)
    for part in parts[1:]:
        total = total + part.astype(jnp.float32)
    return total.astype(parts[0].dtype)


def pack_kernel(experts, rows_ref, ids_ref, gates_ref, out_ref):
    width = rows_ref.shape[1]
    extra = out_ref.shape[1] - width
    gates = gates_ref[...]
    shares = 2.5 * gates / jnp.sum(gates, axis=1, keepdims=True)
    ids = ids_ref[...]
    lane = lax.broadcasted_iota(jnp.int32, (ids.shape[0], extra), 1)
    expert = jnp.where(lane < experts, lane, lane - experts)
    table = jnp.zeros(lane.shape, jnp.float32)
    for k in range(ids.shape[1]):
        table += jnp.where(expert == ids[:, k : k + 1], shares[:, k : k + 1], 0.0)
    high = table.astype(jnp.bfloat16).astype(jnp.float32)
    table = jnp.where(lane < experts, high, jnp.where(lane < 2 * experts, table - high, 0.0))
    out_ref[:, :width] = rows_ref[...]
    out_ref[:, width:] = table.astype(jnp.bfloat16)


def pack(experts, moe_rows, route_ids, route_gates):
    rows, width = moe_rows.shape
    total = width + pl.cdiv(2 * experts, 128) * 128
    return pl.pallas_call(
        functools.partial(pack_kernel, experts),
        out_shape=jax.ShapeDtypeStruct((rows, total), jnp.bfloat16),
        name="pack",
    )(moe_rows, route_ids, route_gates)


def spread(product, outs):
    start = 0
    for out, columns in outs:
        size = out.shape[0]
        out[:, columns] = product[start : start + size]
        start += size


def bring_kernel(source, target, sems):
    rows = source.shape[0] // sems.shape[0]
    copies = []
    for k in range(sems.shape[0]):
        part = pl.ds(k * rows, rows)
        copies.append(pltpu.make_async_copy(source.at[part], target.at[part], sems.at[k]))
    for copy in copies:
        copy.start()
    for copy in copies:
        copy.wait()


def bring(weight, name):
    return pl.pallas_call(
        bring_kernel,
        in_specs=[pl.BlockSpec(memory_space=pltpu.HBM)],
        out_specs=pl.BlockSpec(memory_space=pltpu.VMEM),
        out_shape=pltpu.VMEM(weight.shape, weight.dtype),
        scratch_shapes=[pltpu.SemaphoreType.DMA((4,))],
        cost_estimate=pl.CostEstimate(
            flops=0, bytes_accessed=2 * weight.size, transcendentals=0
        ),
        compiler_params=pltpu.CompilerParams(vmem_limit_bytes=MEBI),
        name=name,
    )(pltpu.with_memory_space_constraint(weight, pltpu.HBM))


def expert_kernel(count, experts, tile, down_tile, node_ref, *refs):
    blocks = refs[:count]
    gate, up, down, hidden_ref, share_ref = refs[count : count + 5]
    outs = refs[count + 5 : -2]
    gate_sum, up_sum = refs[-2:]
    width = gate.shape[0]
    columns = outs[0].shape[1]

    table = jnp.concatenate([block[:, width:] for block in blocks], axis=0).astype(jnp.float32)
    lane = lax.broadcasted_iota(jnp.int32, table.shape, 1)
    mine = (lane == node_ref[0]) | (lane == node_ref[0] + experts)
    share = jnp.sum(jnp.where(mine, table, 0.0), axis=1, keepdims=True)
    share_ref[...] = jnp.broadcast_to(share, share_ref.shape)

    for k in range(0, width, tile):
        part = pl.ds(k, tile)
        rows = jnp.concatenate([block[:, part] for block in blocks], axis=0)
        for weight, total in ((gate, gate_sum), (up, up_sum)):
            product = jnp.dot(rows, weight[part], preferred_element_type=jnp.float32)
            if k == 0:
                total[...] = product
            else:
                total[...] += product
    hidden_ref[...] = (jax.nn.silu(gate_sum[...]) * up_sum[...]).astype(jnp.bfloat16)
    for k in range(0, columns, down_tile):
        part = pl.ds(k, down_tile)
        product = jnp.dot(hidden_ref[...], down[:, part], preferred_element_type=jnp.float32)
        product = (product * share_ref[:, :1]).astype(jnp.bfloat16)
        spread(product, [(out, part) for out in outs])


def expert(blocks, w_gate, w_up, w_down, experts, node, sizes, columns):
    width, units = w_gate.shape
    rows = sum(sizes)
    return pl.pallas_call(
        functools.partial(expert_kernel, len(blocks), experts, 1024, 512),
        in_specs=[pl.BlockSpec(memory_space=pltpu.SMEM)]
        + [pl.BlockSpec(memory_space=pltpu.VMEM)] * (len(blocks) + 3),
        out_specs=[pl.BlockSpec(memory_space=pltpu.VMEM)] * (2 + len(sizes)),
        out_shape=[
            jax.ShapeDtypeStruct((rows, units), jnp.bfloat16),
            jax.ShapeDtypeStruct((rows, 128), jnp.float32),
        ]
        + [jax.ShapeDtypeStruct((size, columns), jnp.bfloat16) for size in sizes],
        scratch_shapes=[pltpu.VMEM((rows, units), jnp.float32)] * 2,
        cost_estimate=pl.CostEstimate(
            flops=4 * rows * width * units + 2 * rows * columns * units,
            bytes_accessed=4 * width * units + 2 * units * columns,
            transcendentals=rows * units,
        ),
        compiler_params=pltpu.CompilerParams(vmem_limit_bytes=8 * MEBI),
        name="expert",
    )(node, *blocks, w_gate, w_up, w_down)


def down_kernel(start, tile, hidden_ref, share_ref, down_ref, *outs):
    for k in range(0, outs[0].shape[1], tile):
        weight = down_ref[:, pl.ds(start + k, tile)]
        product = jnp.dot(hidden_ref[...], weight, preferred_element_type=jnp.float32)
        product = (product * share_ref[:, :1]).astype(jnp.bfloat16)
        spread(product, [(out, pl.ds(k, tile)) for out in outs])


def down_of(hidden, share, w_down, sizes, start):
    rows, units = hidden.shape
    columns = w_down.shape[1] - start
    return pl.pallas_call(
        functools.partial(down_kernel, start, 512),
        in_specs=[pl.BlockSpec(memory_space=pltpu.VMEM)] * 3,
        out_specs=[pl.BlockSpec(memory_space=pltpu.VMEM)] * len(sizes),
        out_shape=[jax.ShapeDtypeStruct((size, columns), jnp.bfloat16) for size in sizes],
        cost_estimate=pl.CostEstimate(
            flops=2 * rows * columns * units,
            bytes_accessed=2 * columns * (units + rows),
            transcendentals=0,
        ),
        compiler_params=pltpu.CompilerParams(vmem_limit_bytes=8 * MEBI),
        name="down",
    )(hidden, share, w_down)


def body(
    moe_rows,
    route_ids,
    route_gates,
    w_gate,
    w_up,
    w_down,
    query_latent,
    query_rope,
    cache_latent,
    cache_rope,
    cache_lengths,
):
    grid = Grid()
    high, middle, cores, _ = grid.sizes
    experts = high * middle * cores
    tokens, width = moe_rows.shape
    node = lax.axis_index(("high", "middle", "core")).astype(jnp.int32).reshape(1)
    weights = bring(w_gate[0], "gate"), bring(w_up[0], "up"), bring(w_down[0], "down_in")
    outgoing = pack(experts, moe_rows, route_ids, route_gates)
    attn_latent = attention(query_latent, query_rope, cache_latent, cache_rope, cache_lengths)
    places, (gate, up, (down, attn_latent)) = grid.gather(
        outgoing, weights[:2] + ((weights[2], attn_latent),)
    )
    size = high * tokens
    count = len(places) // 2
    sizes = [size] * count + [size, size * (count - 1)]
    places = places[:count] + places[-1:] + places[count:-1]
    blocks = [block for place in places for block in place]
    split = width * 4 // 7
    hidden, share, *products = expert(blocks, gate, up, down, experts, node, sizes, split)
    lower, lower_other = products[:count], products[count:]
    last = grid.last_sum(lower, lower_other)
    hidden, last = lax.optimization_barrier((hidden, last))
    products = down_of(hidden, share, down, sizes, split)
    lower = grid.scatter_sum(lower, lower_other, last)
    upper, upper_other = products[:count], products[count:]
    upper = grid.scatter_sum(upper, upper_other, grid.last_sum(upper, upper_other))
    return (jnp.concatenate([lower, upper], axis=1), attn_latent)


def solution(mesh):
    groups, nodes, local = mesh.devices.shape
    split = Mesh(mesh.devices.reshape(groups, nodes // 4, 2, 2, local), ("group",) + everyone)
    node = ("high", "middle", "core")
    whole = ("group",) + everyone
    rows = P(whole, None)
    blocks = P(whole, None, None)
    return jax.shard_map(
        body,
        mesh=split,
        in_specs=(
            rows,
            rows,
            rows,
            P(node, None, "local"),
            P(node, None, "local"),
            P(node, "local", None),
            blocks,
            blocks,
            blocks,
            blocks,
            P(whole),
        ),
        out_specs=(rows, blocks),
        check_vma=False,
    )
```

```python
import functools

import jax
import jax.numpy as jnp
import numpy as np
from jax import lax
from jax.experimental import pallas as pl
from jax.experimental.pallas import tpu as pltpu
from jax.sharding import Mesh
from jax.sharding import PartitionSpec as P

score_scale = 192.0 ** (-0.5)
everyone = ("high", "middle", "core", "local")
MEBI = 1024 * 1024


def attention_kernel(lengths_ref, query_ref, query_rope_ref, cache_ref, cache_rope_ref, out_ref):
    for row in range(query_ref.shape[0]):
        cache = cache_ref[row]
        scores = lax.dot_general(
            query_ref[row], cache, (((1,), (1,)), ((), ())), preferred_element_type=jnp.float32
        )
        scores += jnp.dot(
            query_rope_ref[row], cache_rope_ref[row], preferred_element_type=jnp.float32
        )
        slot = lax.broadcasted_iota(jnp.int32, scores.shape, 1)
        in_range = slot < lengths_ref[row]
        scores = jnp.where(in_range, scores * score_scale, -jnp.inf)
        row_peak = jnp.max(scores, axis=1, keepdims=True)
        lifted = jnp.where(in_range, jnp.exp(scores - row_peak), 0.0)
        weights = (lifted / jnp.sum(lifted, axis=1, keepdims=True)).astype(jnp.bfloat16)
        value = jnp.dot(weights, cache, preferred_element_type=jnp.float32)
        out_ref[row] = value.astype(jnp.bfloat16)


def attention(query_latent, query_rope, cache_latent, cache_rope, cache_lengths):
    rows, heads, latent = query_latent.shape
    slots = cache_latent.shape[1]
    return pl.pallas_call(
        attention_kernel,
        in_specs=[pl.BlockSpec(memory_space=pltpu.SMEM)]
        + [pl.BlockSpec(memory_space=pltpu.VMEM)] * 4,
        out_specs=pl.BlockSpec(memory_space=pltpu.VMEM),
        out_shape=jax.ShapeDtypeStruct(query_latent.shape, jnp.bfloat16),
        cost_estimate=pl.CostEstimate(
            flops=4 * rows * heads * slots * latent,
            bytes_accessed=2 * rows * slots * latent,
            transcendentals=rows * heads * slots,
        ),
        compiler_params=pltpu.CompilerParams(vmem_limit_bytes=8 * MEBI),
        name="attention",
    )(cache_lengths, query_latent, query_rope, cache_latent, cache_rope)


class Grid:
    def __init__(self):
        self.sizes = tuple(lax.axis_size(name) for name in everyone)
        self.mixed = self.sizes[1] == self.sizes[3]

    def swap(self, value, pick, mask):
        pairs = []
        for place in np.ndindex(*self.sizes):
            other = list(place)
            other[pick(place[2])] ^= mask
            pairs.append(
                (
                    int(np.ravel_multi_index(place, self.sizes)),
                    int(np.ravel_multi_index(other, self.sizes)),
                )
            )
        return lax.ppermute(value, everyone, pairs)

    def high(self, core):
        return 0

    def core(self, core):
        return 2

    def first(self, core):
        return 1 if self.mixed and core == 1 else 3

    def second(self, core):
        return 3 if self.mixed and core == 1 else 1

    def extent(self, pick):
        return self.sizes[pick(0)]

    def far(self, near):
        return [
            self.swap(block, self.second, m)
            for m in range(1, self.extent(self.second))
            for block in near
        ]

    def near(self, line):
        return [line] + [self.swap(line, self.first, m) for m in range(1, self.extent(self.first))]

    def gather(self, rows, weights):
        gate, up, down = weights
        line, m, half = rows, 1, self.extent(self.high) // 2
        while m < half:
            line, m = join([line, self.swap(line, self.high, m)]), 2 * m
        later = self.swap(line, self.high, half)
        near = self.near(line)
        far = self.far(near)
        later, near, far[0], gate = lax.optimization_barrier((later, near, far[0], gate))
        later_near = self.near(later)
        later_near[-1], far[-1], up = lax.optimization_barrier((later_near[-1], far[-1], up))
        later_far = self.far(later_near)
        later_far[-1], down = lax.optimization_barrier((later_far[-1], down))
        groups = []
        for mine in (near + far, later_near + later_far):
            groups.append(mine + [self.swap(block, self.core, 1) for block in mine])
        return [list(blocks) for blocks in zip(*groups)], (gate, up, down)

    def last_sum(self, mine, other):
        return add([mine[-1], self.swap(other[0], self.core, 1)])

    def rest_sums(self, mine, other):
        size = mine[0].shape[0]
        rest = self.swap(other[1], self.core, 1)
        return [
            add([part, rest[i * size : (i + 1) * size]]) for i, part in enumerate(mine[:-1])
        ]

    def back(self, sums, place):
        return self.swap(sums[place], self.second, place // self.extent(self.first))

    def line_sum(self, sums, last):
        wide = self.extent(self.first)
        near = [[part] for part in sums[:wide]]
        for place in range(wide, len(sums)):
            moved = last if place == len(sums) - 1 else self.back(sums, place)
            near[place % wide].append(moved)
        near = [add(parts) for parts in near]
        return add([near[0]] + [self.swap(near[m], self.first, m) for m in range(1, wide)])

    def high_sum(self, line):
        rows = line.shape[0] // self.extent(self.high)
        parts = [line[:rows]]
        for m in range(1, self.extent(self.high)):
            parts.append(self.swap(line[m * rows : (m + 1) * rows], self.high, m))
        return add(parts)


def join_kernel(*refs):
    refs[-1][...] = jnp.concatenate([ref[...] for ref in refs[:-1]], axis=0)


def join(parts):
    rows = sum(part.shape[0] for part in parts)
    return pl.pallas_call(
        join_kernel,
        in_specs=[pl.BlockSpec(memory_space=pltpu.VMEM)] * len(parts),
        out_specs=pl.BlockSpec(memory_space=pltpu.VMEM),
        out_shape=jax.ShapeDtypeStruct((rows, parts[0].shape[1]), parts[0].dtype),
        compiler_params=pltpu.CompilerParams(vmem_limit_bytes=2 * MEBI),
        name="join",
    )(*parts)


def add(parts):
    total = parts[0].astype(jnp.float32)
    for part in parts[1:]:
        total = total + part.astype(jnp.float32)
    return total.astype(parts[0].dtype)


def pack_kernel(experts, rows_ref, ids_ref, gates_ref, out_ref):
    width = rows_ref.shape[1]
    extra = out_ref.shape[1] - width
    gates = gates_ref[...]
    shares = 2.5 * gates / jnp.sum(gates, axis=1, keepdims=True)
    ids = ids_ref[...]
    lane = lax.broadcasted_iota(jnp.int32, (ids.shape[0], extra), 1)
    expert = jnp.where(lane < experts, lane, lane - experts)
    table = jnp.zeros(lane.shape, jnp.float32)
    for k in range(ids.shape[1]):
        table += jnp.where(expert == ids[:, k : k + 1], shares[:, k : k + 1], 0.0)
    high = table.astype(jnp.bfloat16).astype(jnp.float32)
    table = jnp.where(lane < experts, high, jnp.where(lane < 2 * experts, table - high, 0.0))
    out_ref[:, :width] = rows_ref[...]
    out_ref[:, width:] = table.astype(jnp.bfloat16)


def pack(experts, moe_rows, route_ids, route_gates):
    rows, width = moe_rows.shape
    total = width + pl.cdiv(2 * experts, 128) * 128
    return pl.pallas_call(
        functools.partial(pack_kernel, experts),
        out_shape=jax.ShapeDtypeStruct((rows, total), jnp.bfloat16),
        name="pack",
    )(moe_rows, route_ids, route_gates)


def spread(product, outs):
    start = 0
    for out, columns in outs:
        size = out.shape[0]
        out[:, columns] = product[start : start + size]
        start += size


def bring_kernel(source, target, sems):
    rows = source.shape[0] // sems.shape[0]
    copies = []
    for k in range(sems.shape[0]):
        part = pl.ds(k * rows, rows)
        copies.append(pltpu.make_async_copy(source.at[part], target.at[part], sems.at[k]))
    for copy in copies:
        copy.start()
    for copy in copies:
        copy.wait()


def bring(weight, name):
    return pl.pallas_call(
        bring_kernel,
        in_specs=[pl.BlockSpec(memory_space=pltpu.HBM)],
        out_specs=pl.BlockSpec(memory_space=pltpu.VMEM),
        out_shape=pltpu.VMEM(weight.shape, weight.dtype),
        scratch_shapes=[pltpu.SemaphoreType.DMA((4,))],
        cost_estimate=pl.CostEstimate(
            flops=0, bytes_accessed=2 * weight.size, transcendentals=0
        ),
        compiler_params=pltpu.CompilerParams(vmem_limit_bytes=MEBI),
        name=name,
    )(pltpu.with_memory_space_constraint(weight, pltpu.HBM))


def expert_kernel(count, experts, tile, down_tile, node_ref, *refs):
    blocks = refs[:count]
    gate, up, down, hidden_ref, share_ref = refs[count : count + 5]
    outs = refs[count + 5 : -2]
    gate_sum, up_sum = refs[-2:]
    width = gate.shape[0]
    columns = outs[0].shape[1]

    table = jnp.concatenate([block[:, width:] for block in blocks], axis=0).astype(jnp.float32)
    lane = lax.broadcasted_iota(jnp.int32, table.shape, 1)
    mine = (lane == node_ref[0]) | (lane == node_ref[0] + experts)
    share = jnp.sum(jnp.where(mine, table, 0.0), axis=1, keepdims=True)
    share_ref[...] = jnp.broadcast_to(share, share_ref.shape)

    for k in range(0, width, tile):
        part = pl.ds(k, tile)
        rows = jnp.concatenate([block[:, part] for block in blocks], axis=0)
        for weight, total in ((gate, gate_sum), (up, up_sum)):
            product = jnp.dot(rows, weight[part], preferred_element_type=jnp.float32)
            if k == 0:
                total[...] = product
            else:
                total[...] += product
    hidden_ref[...] = (jax.nn.silu(gate_sum[...]) * up_sum[...]).astype(jnp.bfloat16)
    for k in range(0, columns, down_tile):
        part = pl.ds(k, down_tile)
        product = jnp.dot(hidden_ref[...], down[:, part], preferred_element_type=jnp.float32)
        product = (product * share_ref[:, :1]).astype(jnp.bfloat16)
        spread(product, [(out, part) for out in outs])


def expert(blocks, w_gate, w_up, w_down, experts, node, sizes, columns):
    width, units = w_gate.shape
    rows = sum(sizes)
    return pl.pallas_call(
        functools.partial(expert_kernel, len(blocks), experts, 1024, 512),
        in_specs=[pl.BlockSpec(memory_space=pltpu.SMEM)]
        + [pl.BlockSpec(memory_space=pltpu.VMEM)] * (len(blocks) + 3),
        out_specs=[pl.BlockSpec(memory_space=pltpu.VMEM)] * (2 + len(sizes)),
        out_shape=[
            jax.ShapeDtypeStruct((rows, units), jnp.bfloat16),
            jax.ShapeDtypeStruct((rows, 128), jnp.float32),
        ]
        + [jax.ShapeDtypeStruct((size, columns), jnp.bfloat16) for size in sizes],
        scratch_shapes=[pltpu.VMEM((rows, units), jnp.float32)] * 2,
        cost_estimate=pl.CostEstimate(
            flops=4 * rows * width * units + 2 * rows * columns * units,
            bytes_accessed=4 * width * units + 2 * units * columns,
            transcendentals=rows * units,
        ),
        compiler_params=pltpu.CompilerParams(vmem_limit_bytes=8 * MEBI),
        name="expert",
    )(node, *blocks, w_gate, w_up, w_down)


def down_kernel(start, tile, hidden_ref, share_ref, down_ref, *outs):
    for k in range(0, outs[0].shape[1], tile):
        weight = down_ref[:, pl.ds(start + k, tile)]
        product = jnp.dot(hidden_ref[...], weight, preferred_element_type=jnp.float32)
        product = (product * share_ref[:, :1]).astype(jnp.bfloat16)
        spread(product, [(out, pl.ds(k, tile)) for out in outs])


def down_of(hidden, share, w_down, sizes, start):
    rows, units = hidden.shape
    columns = w_down.shape[1] - start
    return pl.pallas_call(
        functools.partial(down_kernel, start, 512),
        in_specs=[pl.BlockSpec(memory_space=pltpu.VMEM)] * 3,
        out_specs=[pl.BlockSpec(memory_space=pltpu.VMEM)] * len(sizes),
        out_shape=[jax.ShapeDtypeStruct((size, columns), jnp.bfloat16) for size in sizes],
        cost_estimate=pl.CostEstimate(
            flops=2 * rows * columns * units,
            bytes_accessed=2 * columns * (units + rows),
            transcendentals=0,
        ),
        compiler_params=pltpu.CompilerParams(vmem_limit_bytes=8 * MEBI),
        name="down",
    )(hidden, share, w_down)


def body(
    moe_rows,
    route_ids,
    route_gates,
    w_gate,
    w_up,
    w_down,
    query_latent,
    query_rope,
    cache_latent,
    cache_rope,
    cache_lengths,
):
    grid = Grid()
    high, middle, cores, _ = grid.sizes
    experts = high * middle * cores
    tokens, width = moe_rows.shape
    node = lax.axis_index(("high", "middle", "core")).astype(jnp.int32).reshape(1)
    weights = bring(w_gate[0], "gate"), bring(w_up[0], "up"), bring(w_down[0], "down_in")
    outgoing = pack(experts, moe_rows, route_ids, route_gates)
    attn_latent = attention(query_latent, query_rope, cache_latent, cache_rope, cache_lengths)
    places, (gate, up, (down, attn_latent)) = grid.gather(
        outgoing, weights[:2] + ((weights[2], attn_latent),)
    )
    size = high * tokens
    count = len(places) // 2
    sizes = [size] * count + [size, size * (count - 1)]
    places = places[:count] + places[-1:] + places[count:-1]
    blocks = [block for place in places for block in place]
    split = width * 4 // 7
    hidden, share, *products = expert(blocks, gate, up, down, experts, node, sizes, split)
    lower, lower_other = products[:count], products[count:]
    last = grid.last_sum(lower, lower_other)
    hidden, last = lax.optimization_barrier((hidden, last))
    products = down_of(hidden, share, down, sizes, split)
    upper, upper_other = products[:count], products[count:]
    sums = grid.rest_sums(lower, lower_other) + [last]
    came = grid.back(sums, count - 1)
    last = grid.last_sum(upper, upper_other)
    last, came = lax.optimization_barrier((last, came))
    line = grid.line_sum(sums, came)
    sums = grid.rest_sums(upper, upper_other)
    came = grid.back(sums + [last], count - 1)
    sums, came, line = lax.optimization_barrier((sums, came, line))
    lower = grid.high_sum(line)
    upper = grid.high_sum(grid.line_sum(sums + [last], came))
    return (jnp.concatenate([lower, upper], axis=1), attn_latent)


def solution(mesh):
    groups, nodes, local = mesh.devices.shape
    split = Mesh(mesh.devices.reshape(groups, nodes // 4, 2, 2, local), ("group",) + everyone)
    node = ("high", "middle", "core")
    whole = ("group",) + everyone
    rows = P(whole, None)
    blocks = P(whole, None, None)
    return jax.shard_map(
        body,
        mesh=split,
        in_specs=(
            rows,
            rows,
            rows,
            P(node, None, "local"),
            P(node, None, "local"),
            P(node, "local", None),
            blocks,
            blocks,
            blocks,
            blocks,
            P(whole),
        ),
        out_specs=(rows, blocks),
        check_vma=False,
    )
```

```python
import functools

import jax
import jax.numpy as jnp
import numpy as np
from jax import lax
from jax.experimental import pallas as pl
from jax.experimental.pallas import tpu as pltpu
from jax.sharding import Mesh
from jax.sharding import PartitionSpec as P

score_scale = 192.0 ** (-0.5)
everyone = ("high", "middle", "core", "local")
MEBI = 1024 * 1024


def attention_kernel(lengths_ref, query_ref, query_rope_ref, cache_ref, cache_rope_ref, out_ref):
    for row in range(query_ref.shape[0]):
        cache = cache_ref[row]
        scores = lax.dot_general(
            query_ref[row], cache, (((1,), (1,)), ((), ())), preferred_element_type=jnp.float32
        )
        scores += jnp.dot(
            query_rope_ref[row], cache_rope_ref[row], preferred_element_type=jnp.float32
        )
        slot = lax.broadcasted_iota(jnp.int32, scores.shape, 1)
        in_range = slot < lengths_ref[row]
        scores = jnp.where(in_range, scores * score_scale, -jnp.inf)
        row_peak = jnp.max(scores, axis=1, keepdims=True)
        lifted = jnp.where(in_range, jnp.exp(scores - row_peak), 0.0)
        weights = (lifted / jnp.sum(lifted, axis=1, keepdims=True)).astype(jnp.bfloat16)
        value = jnp.dot(weights, cache, preferred_element_type=jnp.float32)
        out_ref[row] = value.astype(jnp.bfloat16)


def attention(query_latent, query_rope, cache_latent, cache_rope, cache_lengths):
    rows, heads, latent = query_latent.shape
    slots = cache_latent.shape[1]
    return pl.pallas_call(
        attention_kernel,
        in_specs=[pl.BlockSpec(memory_space=pltpu.SMEM)]
        + [pl.BlockSpec(memory_space=pltpu.VMEM)] * 4,
        out_specs=pl.BlockSpec(memory_space=pltpu.VMEM),
        out_shape=jax.ShapeDtypeStruct(query_latent.shape, jnp.bfloat16),
        cost_estimate=pl.CostEstimate(
            flops=4 * rows * heads * slots * latent,
            bytes_accessed=2 * rows * slots * latent,
            transcendentals=rows * heads * slots,
        ),
        compiler_params=pltpu.CompilerParams(vmem_limit_bytes=8 * MEBI),
        name="attention",
    )(cache_lengths, query_latent, query_rope, cache_latent, cache_rope)


class Grid:
    def __init__(self):
        self.sizes = tuple(lax.axis_size(name) for name in everyone)
        self.mixed = self.sizes[1] == self.sizes[3]

    def swap(self, value, pick, mask):
        pairs = []
        for place in np.ndindex(*self.sizes):
            other = list(place)
            other[pick(place[2])] ^= mask
            pairs.append(
                (
                    int(np.ravel_multi_index(place, self.sizes)),
                    int(np.ravel_multi_index(other, self.sizes)),
                )
            )
        return lax.ppermute(value, everyone, pairs)

    def high(self, core):
        return 0

    def core(self, core):
        return 2

    def first(self, core):
        return 1 if self.mixed and core == 1 else 3

    def second(self, core):
        return 3 if self.mixed and core == 1 else 1

    def extent(self, pick):
        return self.sizes[pick(0)]

    def masks(self):
        masks, m = [], self.extent(self.high) // 2
        while m:
            masks.append(m)
            m //= 2
        return masks

    def near(self, line):
        return [line] + [self.swap(line, self.first, m) for m in range(1, self.extent(self.first))]

    def far(self, near):
        return [
            self.swap(block, self.second, m)
            for m in range(1, self.extent(self.second))
            for block in near
        ]

    def other(self, mine):
        return [self.swap(block, self.core, 1) for block in mine]

    def last_sum(self, mine, other):
        return add([mine[-1], self.swap(other[0], self.core, 1)])

    def rest_sums(self, mine, other):
        size = mine[0].shape[0]
        rest = self.swap(other[1], self.core, 1)
        return [
            add([part, rest[i * size : (i + 1) * size]]) for i, part in enumerate(mine[:-1])
        ]

    def back(self, sums, place):
        return self.swap(sums[place], self.second, place // self.extent(self.first))

    def line_sum(self, sums, last):
        wide = self.extent(self.first)
        near = [[part] for part in sums[:wide]]
        for place in range(wide, len(sums)):
            moved = last if place == len(sums) - 1 else self.back(sums, place)
            near[place % wide].append(moved)
        near = [add(parts) for parts in near]
        return add([near[0]] + [self.swap(near[m], self.first, m) for m in range(1, wide)])

    def high_sum(self, line):
        for m in reversed(self.masks()):
            half = line.shape[0] // 2
            line = add([line[:half], self.swap(line[half:], self.high, m)])
        return line


def add(parts):
    total = parts[0].astype(jnp.float32)
    for part in parts[1:]:
        total = total + part.astype(jnp.float32)
    return total.astype(parts[0].dtype)


def join_kernel(*refs):
    refs[-1][...] = jnp.concatenate([ref[...] for ref in refs[:-1]], axis=0)


def join(parts):
    rows = sum(part.shape[0] for part in parts)
    return pl.pallas_call(
        join_kernel,
        in_specs=[pl.BlockSpec(memory_space=pltpu.VMEM)] * len(parts),
        out_specs=pl.BlockSpec(memory_space=pltpu.VMEM),
        out_shape=jax.ShapeDtypeStruct((rows, parts[0].shape[1]), parts[0].dtype),
        compiler_params=pltpu.CompilerParams(vmem_limit_bytes=2 * MEBI),
        name="join",
    )(*parts)


def cut_kernel(rows_ref, out_ref):
    out_ref[...] = rows_ref[:, : out_ref.shape[1]]


def cut(columns, moe_rows):
    return pl.pallas_call(
        cut_kernel,
        out_shape=jax.ShapeDtypeStruct((moe_rows.shape[0], columns), moe_rows.dtype),
        compiler_params=pltpu.CompilerParams(vmem_limit_bytes=2 * MEBI),
        name="cut",
    )(moe_rows)


def pack_kernel(experts, rows_ref, ids_ref, gates_ref, out_ref):
    extra = table_width(experts)
    width = out_ref.shape[1] - extra
    gates = gates_ref[...]
    shares = 2.5 * gates / jnp.sum(gates, axis=1, keepdims=True)
    ids = ids_ref[...]
    lane = lax.broadcasted_iota(jnp.int32, (ids.shape[0], extra), 1)
    expert = jnp.where(lane < experts, lane, lane - experts)
    table = jnp.zeros(lane.shape, jnp.float32)
    for k in range(ids.shape[1]):
        table += jnp.where(expert == ids[:, k : k + 1], shares[:, k : k + 1], 0.0)
    high = table.astype(jnp.bfloat16).astype(jnp.float32)
    table = jnp.where(lane < experts, high, jnp.where(lane < 2 * experts, table - high, 0.0))
    out_ref[:, :width] = rows_ref[:, rows_ref.shape[1] - width :]
    out_ref[:, width:] = table.astype(jnp.bfloat16)


def table_width(experts):
    return pl.cdiv(2 * experts, 128) * 128


def pack(columns, experts, moe_rows, route_ids, route_gates):
    total = columns + table_width(experts)
    return pl.pallas_call(
        functools.partial(pack_kernel, experts),
        out_shape=jax.ShapeDtypeStruct((moe_rows.shape[0], total), jnp.bfloat16),
        compiler_params=pltpu.CompilerParams(vmem_limit_bytes=2 * MEBI),
        name="pack",
    )(moe_rows, route_ids, route_gates)


def spread(product, outs):
    start = 0
    for out, columns in outs:
        size = out.shape[0]
        out[:, columns] = product[start : start + size]
        start += size


def in_hbm(weight):
    return pltpu.with_memory_space_constraint(weight, pltpu.HBM)


def fetch(source, target, sems, start, tile, dim):
    copies = []
    for k in range(0, target.shape[dim], tile):
        inside, outside = pl.ds(k, tile), pl.ds(start + k, tile)
        if dim == 1:
            inside, outside = (slice(None), inside), (slice(None), outside)
        copy = pltpu.make_async_copy(source.at[outside], target.at[inside], sems.at[k // tile])
        copy.start()
        copies.append(copy)
    return copies


def fetch_both(gate_hbm, up_hbm, gate, up, gate_sem, up_sem, start, tile):
    copies = []
    for k in range(0, gate.shape[0], tile):
        inside, outside = pl.ds(k, tile), pl.ds(start + k, tile)
        pair = (
            pltpu.make_async_copy(gate_hbm.at[outside], gate.at[inside], gate_sem.at[k // tile]),
            pltpu.make_async_copy(up_hbm.at[outside], up.at[inside], up_sem.at[k // tile]),
        )
        for copy in pair:
            copy.start()
        copies.append(pair)
    return copies


def project(blocks, copies, gate, up, gate_sum, up_sum, tile, fresh):
    for k, pair in enumerate(copies):
        part = pl.ds(k * tile, tile)
        rows = jnp.concatenate([block[:, part] for block in blocks], axis=0)
        for copy, weight, total in zip(pair, (gate, up), (gate_sum, up_sum)):
            copy.wait()
            product = jnp.dot(rows, weight[part], preferred_element_type=jnp.float32)
            if fresh and k == 0:
                total[...] = product
            else:
                total[...] += product


def first_kernel(count, tile, *refs):
    blocks = refs[:count]
    gate_hbm, up_hbm, gate_sum, up_sum, gate, up, gate_sem, up_sem = refs[count:]
    copies = fetch_both(gate_hbm, up_hbm, gate, up, gate_sem, up_sem, 0, tile)
    project(blocks, copies, gate, up, gate_sum, up_sum, tile, True)


def first_sums(blocks, w_gate, w_up):
    units = w_gate.shape[1]
    rows = sum(block.shape[0] for block in blocks)
    columns = blocks[0].shape[1]
    tile = 1024
    return pl.pallas_call(
        functools.partial(first_kernel, len(blocks), tile),
        in_specs=[pl.BlockSpec(memory_space=pltpu.VMEM)] * len(blocks)
        + [pl.BlockSpec(memory_space=pltpu.HBM)] * 2,
        out_specs=[pl.BlockSpec(memory_space=pltpu.VMEM)] * 2,
        out_shape=[jax.ShapeDtypeStruct((rows, units), jnp.float32)] * 2,
        scratch_shapes=[pltpu.VMEM((columns, units), jnp.bfloat16)] * 2
        + [pltpu.SemaphoreType.DMA((columns // tile,))] * 2,
        cost_estimate=pl.CostEstimate(
            flops=4 * rows * columns * units,
            bytes_accessed=4 * columns * units,
            transcendentals=0,
        ),
        compiler_params=pltpu.CompilerParams(vmem_limit_bytes=20 * MEBI),
        name="first_sums",
    )(*blocks, in_hbm(w_gate), in_hbm(w_up))


def expert_kernel(count, experts, tile, down_tile, node_ref, *refs):
    blocks = refs[:count]
    gate_in, up_in, gate_hbm, up_hbm, down_hbm, hidden_ref, share_ref = refs[count : count + 7]
    outs = refs[count + 7 : -8]
    gate, up, down, gate_sum, up_sum, gate_sem, up_sem, down_sem = refs[-8:]
    start = gate_hbm.shape[0] - gate.shape[0]
    copies = fetch_both(gate_hbm, up_hbm, gate, up, gate_sem, up_sem, start, tile)
    down_copies = fetch(down_hbm, down, down_sem, 0, down_tile, 1)

    table = jnp.concatenate([block[:, gate.shape[0] :] for block in blocks], axis=0)
    table = table.astype(jnp.float32)
    lane = lax.broadcasted_iota(jnp.int32, table.shape, 1)
    mine = (lane == node_ref[0]) | (lane == node_ref[0] + experts)
    share = jnp.sum(jnp.where(mine, table, 0.0), axis=1, keepdims=True)
    share_ref[...] = jnp.broadcast_to(share, share_ref.shape)
    gate_sum[...] = gate_in[...]
    up_sum[...] = up_in[...]
    project(blocks, copies, gate, up, gate_sum, up_sum, tile, False)
    hidden_ref[...] = (jax.nn.silu(gate_sum[...]) * up_sum[...]).astype(jnp.bfloat16)
    for k, copy in enumerate(down_copies):
        part = pl.ds(k * down_tile, down_tile)
        copy.wait()
        product = jnp.dot(hidden_ref[...], down[:, part], preferred_element_type=jnp.float32)
        product = (product * share_ref[:, :1]).astype(jnp.bfloat16)
        spread(product, [(out, part) for out in outs])


def expert(blocks, sums, w_gate, w_up, w_down, experts, node, sizes, columns):
    units = w_gate.shape[1]
    rows = sum(sizes)
    tail = blocks[0].shape[1] - table_width(experts)
    tile, down_tile = 1024, 512
    return pl.pallas_call(
        functools.partial(expert_kernel, len(blocks), experts, tile, down_tile),
        in_specs=[pl.BlockSpec(memory_space=pltpu.SMEM)]
        + [pl.BlockSpec(memory_space=pltpu.VMEM)] * (len(blocks) + 2)
        + [pl.BlockSpec(memory_space=pltpu.HBM)] * 3,
        out_specs=[pl.BlockSpec(memory_space=pltpu.VMEM)] * (2 + len(sizes)),
        out_shape=[
            jax.ShapeDtypeStruct((rows, units), jnp.bfloat16),
            jax.ShapeDtypeStruct((rows, 128), jnp.float32),
        ]
        + [jax.ShapeDtypeStruct((size, columns), jnp.bfloat16) for size in sizes],
        scratch_shapes=[
            pltpu.VMEM((tail, units), jnp.bfloat16),
            pltpu.VMEM((tail, units), jnp.bfloat16),
            pltpu.VMEM((units, columns), jnp.bfloat16),
            pltpu.VMEM((rows, units), jnp.float32),
            pltpu.VMEM((rows, units), jnp.float32),
            pltpu.SemaphoreType.DMA((tail // tile,)),
            pltpu.SemaphoreType.DMA((tail // tile,)),
            pltpu.SemaphoreType.DMA((columns // down_tile,)),
        ],
        cost_estimate=pl.CostEstimate(
            flops=4 * rows * tail * units + 2 * rows * columns * units,
            bytes_accessed=4 * tail * units + 2 * units * columns,
            transcendentals=rows * units,
        ),
        compiler_params=pltpu.CompilerParams(vmem_limit_bytes=24 * MEBI),
        name="expert",
    )(node, *blocks, *sums, in_hbm(w_gate), in_hbm(w_up), in_hbm(w_down))


def down_kernel(start, tile, hidden_ref, share_ref, down_hbm, *refs):
    outs = refs[:-2]
    down, down_sem = refs[-2:]
    for k, copy in enumerate(fetch(down_hbm, down, down_sem, start, tile, 1)):
        part = pl.ds(k * tile, tile)
        copy.wait()
        product = jnp.dot(hidden_ref[...], down[:, part], preferred_element_type=jnp.float32)
        product = (product * share_ref[:, :1]).astype(jnp.bfloat16)
        spread(product, [(out, part) for out in outs])


def down_of(hidden, share, w_down, sizes, start):
    rows, units = hidden.shape
    columns = w_down.shape[1] - start
    tile = 512
    return pl.pallas_call(
        functools.partial(down_kernel, start, tile),
        in_specs=[pl.BlockSpec(memory_space=pltpu.VMEM)] * 2
        + [pl.BlockSpec(memory_space=pltpu.HBM)],
        out_specs=[pl.BlockSpec(memory_space=pltpu.VMEM)] * len(sizes),
        out_shape=[jax.ShapeDtypeStruct((size, columns), jnp.bfloat16) for size in sizes],
        scratch_shapes=[
            pltpu.VMEM((units, columns), jnp.bfloat16),
            pltpu.SemaphoreType.DMA((columns // tile,)),
        ],
        cost_estimate=pl.CostEstimate(
            flops=2 * rows * columns * units,
            bytes_accessed=2 * columns * (units + rows),
            transcendentals=0,
        ),
        compiler_params=pltpu.CompilerParams(vmem_limit_bytes=12 * MEBI),
        name="down",
    )(hidden, share, in_hbm(w_down))


def body(
    moe_rows,
    route_ids,
    route_gates,
    w_gate,
    w_up,
    w_down,
    query_latent,
    query_rope,
    cache_latent,
    cache_rope,
    cache_lengths,
):
    grid = Grid()
    high, middle, cores, _ = grid.sizes
    experts = high * middle * cores
    tokens, width = moe_rows.shape
    node = lax.axis_index(("high", "middle", "core")).astype(jnp.int32).reshape(1)
    split = width * 4 // 7
    tied = lax.optimization_barrier
    attn_latent = attention(query_latent, query_rope, cache_latent, cache_rope, cache_lengths)

    head = cut(split, moe_rows)
    tail = pack(width - split, experts, moe_rows, route_ids, route_gates)
    masks = grid.masks()
    came = grid.swap(head, grid.high, masks[0])
    tail, came = tied((tail, came))
    head = join([head, came])
    for m in masks[1:]:
        head = join([head, grid.swap(head, grid.high, m)])
    head, attn_latent = tied((head, attn_latent))
    for m in masks:
        tail = join([tail, grid.swap(tail, grid.high, m)])
    head_near = grid.near(head)
    tail, head_near[-1] = tied((tail, head_near[-1]))
    head_far = grid.far(head_near)
    tail_near = grid.near(tail)
    tail_near[-1], head_far[-1] = tied((tail_near[-1], head_far[-1]))
    tail_far = grid.far(tail_near)
    mine = head_near + head_far
    other = grid.other(mine)
    gate_sum, up_sum = first_sums(mine + other[-1:] + other[:-1], w_gate[0], w_up[0])
    tail_far[-1], gate_sum, up_sum = tied((tail_far[-1], gate_sum, up_sum))
    mine = tail_near + tail_far
    other = grid.other(mine)
    size, count = high * tokens, len(mine)
    sizes = [size] * count + [size, size * (count - 1)]
    hidden, share, *products = expert(
        mine + other[-1:] + other[:-1],
        (gate_sum, up_sum),
        w_gate[0],
        w_up[0],
        w_down[0],
        experts,
        node,
        sizes,
        split,
    )

    lower, lower_other = products[:count], products[count:]
    last = grid.last_sum(lower, lower_other)
    hidden, last = tied((hidden, last))
    products = down_of(hidden, share, w_down[0], sizes, split)
    sums = grid.rest_sums(lower, lower_other) + [last]
    came = grid.back(sums, count - 1)
    products, came = tied((products, came))
    upper, upper_other = products[:count], products[count:]
    last = grid.last_sum(upper, upper_other)
    line = grid.line_sum(sums, came)
    sums = grid.rest_sums(upper, upper_other)
    came = grid.back(sums + [last], count - 1)
    sums, came, line = tied((sums, came, line))
    lower = grid.high_sum(line)
    upper = grid.high_sum(grid.line_sum(sums + [last], came))
    return (jnp.concatenate([lower, upper], axis=1), attn_latent)


def solution(mesh):
    groups, nodes, local = mesh.devices.shape
    split = Mesh(mesh.devices.reshape(groups, nodes // 4, 2, 2, local), ("group",) + everyone)
    node = ("high", "middle", "core")
    whole = ("group",) + everyone
    rows = P(whole, None)
    blocks = P(whole, None, None)
    return jax.shard_map(
        body,
        mesh=split,
        in_specs=(
            rows,
            rows,
            rows,
            P(node, None, "local"),
            P(node, None, "local"),
            P(node, "local", None),
            blocks,
            blocks,
            blocks,
            blocks,
            P(whole),
        ),
        out_specs=(rows, blocks),
        check_vma=False,
    )
```

```python
import functools

import jax
import jax.numpy as jnp
import numpy as np
from jax import lax
from jax.experimental import pallas as pl
from jax.experimental.pallas import tpu as pltpu
from jax.sharding import Mesh
from jax.sharding import PartitionSpec as P

score_scale = 192.0 ** (-0.5)
everyone = ("high", "middle", "core", "local")
MEBI = 1024 * 1024


def attention_kernel(lengths_ref, *refs):
    sources, (out_ref, *targets), sems = refs[:4], refs[4:-1], refs[-1]
    query_ref, query_rope_ref, cache_ref, cache_rope_ref = targets
    copies = []
    for row in range(out_ref.shape[0]):
        copies.append(
            [
                pltpu.make_async_copy(source.at[row], target.at[row], sems.at[row, i])
                for i, (source, target) in enumerate(zip(sources, targets))
            ]
        )
        for copy in copies[-1]:
            copy.start()
    for row in range(out_ref.shape[0]):
        for copy in copies[row]:
            copy.wait()
        cache = cache_ref[row]
        scores = lax.dot_general(
            query_ref[row], cache, (((1,), (1,)), ((), ())), preferred_element_type=jnp.float32
        )
        scores += jnp.dot(
            query_rope_ref[row], cache_rope_ref[row], preferred_element_type=jnp.float32
        )
        slot = lax.broadcasted_iota(jnp.int32, scores.shape, 1)
        in_range = slot < lengths_ref[row]
        scores = jnp.where(in_range, scores * score_scale, -jnp.inf)
        row_peak = jnp.max(scores, axis=1, keepdims=True)
        lifted = jnp.where(in_range, jnp.exp(scores - row_peak), 0.0)
        weights = (lifted / jnp.sum(lifted, axis=1, keepdims=True)).astype(jnp.bfloat16)
        value = jnp.dot(weights, cache, preferred_element_type=jnp.float32)
        out_ref[row] = value.astype(jnp.bfloat16)


def attention(query_latent, query_rope, cache_latent, cache_rope, cache_lengths):
    rows, heads, latent = query_latent.shape
    slots = cache_latent.shape[1]
    sources = (query_latent, query_rope, cache_latent, cache_rope)
    return pl.pallas_call(
        attention_kernel,
        in_specs=[pl.BlockSpec(memory_space=pltpu.SMEM)]
        + [pl.BlockSpec(memory_space=pltpu.HBM)] * 4,
        out_specs=pl.BlockSpec(memory_space=pltpu.VMEM),
        out_shape=jax.ShapeDtypeStruct(query_latent.shape, jnp.bfloat16),
        scratch_shapes=[pltpu.VMEM(source.shape, source.dtype) for source in sources]
        + [pltpu.SemaphoreType.DMA((rows, 4))],
        cost_estimate=pl.CostEstimate(
            flops=4 * rows * heads * slots * latent,
            bytes_accessed=2 * rows * slots * latent,
            transcendentals=rows * heads * slots,
        ),
        compiler_params=pltpu.CompilerParams(vmem_limit_bytes=8 * MEBI),
        name="attention",
    )(cache_lengths, *[in_hbm(source) for source in sources])


def in_hbm(array):
    return pltpu.with_memory_space_constraint(array, pltpu.HBM)


class Grid:
    def __init__(self):
        self.sizes = tuple(lax.axis_size(name) for name in everyone)
        self.mixed = self.sizes[1] == self.sizes[3]

    def swap(self, value, pick, mask):
        pairs = []
        for place in np.ndindex(*self.sizes):
            other = list(place)
            other[pick(place[2])] ^= mask
            pairs.append(
                (
                    int(np.ravel_multi_index(place, self.sizes)),
                    int(np.ravel_multi_index(other, self.sizes)),
                )
            )
        return lax.ppermute(value, everyone, pairs)

    def high(self, core):
        return 0

    def core(self, core):
        return 2

    def first(self, core):
        return 1 if self.mixed and core == 1 else 3

    def second(self, core):
        return 3 if self.mixed and core == 1 else 1

    def extent(self, pick):
        return self.sizes[pick(0)]

    def masks(self):
        masks, m = [], self.extent(self.high) // 2
        while m:
            masks.append(m)
            m //= 2
        return masks

    def over_first(self, line):
        return [line] + [self.swap(line, self.first, m) for m in range(1, self.extent(self.first))]

    def over_second(self, near):
        return [near] + [self.swap(near, self.second, m) for m in range(1, self.extent(self.second))]

    def second_sum(self, parts):
        return add(parts[:1] + [self.swap(parts[m], self.second, m) for m in range(1, len(parts))])

    def first_sum(self, near):
        rows = near.shape[0] // self.extent(self.first)
        parts = [near[:rows]]
        for m in range(1, self.extent(self.first)):
            parts.append(self.swap(near[m * rows : (m + 1) * rows], self.first, m))
        return add(parts)

    def high_sum(self, line):
        for m in reversed(self.masks()):
            half = line.shape[0] // 2
            line = add([line[:half], self.swap(line[half:], self.high, m)])
        return line

    def high_sum_direct(self, line):
        order = [0]
        for m in self.masks():
            order += [m | other for other in order]
        rows = line.shape[0] // len(order)
        parts = [line[:rows]]
        for i in range(1, len(order)):
            parts.append(self.swap(line[i * rows : (i + 1) * rows], self.high, order[i]))
        return add(parts)


def add(parts):
    total = parts[0].astype(jnp.float32)
    for part in parts[1:]:
        total = total + part.astype(jnp.float32)
    return total.astype(parts[0].dtype)


def join_kernel(count, *refs):
    start = 0
    for out in refs[count:]:
        columns = pl.ds(start, out.shape[1])
        out[...] = jnp.concatenate([ref[:, columns] for ref in refs[:count]], axis=0)
        start += out.shape[1]


def join(parts, *widths):
    rows = sum(part.shape[0] for part in parts)
    widths = widths or parts[0].shape[1:]
    outs = pl.pallas_call(
        functools.partial(join_kernel, len(parts)),
        in_specs=[pl.BlockSpec(memory_space=pltpu.VMEM)] * len(parts),
        out_specs=[pl.BlockSpec(memory_space=pltpu.VMEM)] * len(widths),
        out_shape=[jax.ShapeDtypeStruct((rows, width), parts[0].dtype) for width in widths],
        compiler_params=pltpu.CompilerParams(vmem_limit_bytes=2 * MEBI),
        name="join",
    )(*parts)
    return outs if len(widths) > 1 else outs[0]


def pack_kernel(experts, rows_ref, ids_ref, gates_ref, out_ref):
    extra = table_width(experts)
    width = out_ref.shape[1] - extra
    gates = gates_ref[...]
    shares = 2.5 * gates / jnp.sum(gates, axis=1, keepdims=True)
    ids = ids_ref[...]
    lane = lax.broadcasted_iota(jnp.int32, (ids.shape[0], extra), 1)
    expert = jnp.where(lane < experts, lane, lane - experts)
    table = jnp.zeros(lane.shape, jnp.float32)
    for k in range(ids.shape[1]):
        table += jnp.where(expert == ids[:, k : k + 1], shares[:, k : k + 1], 0.0)
    high = table.astype(jnp.bfloat16).astype(jnp.float32)
    table = jnp.where(lane < experts, high, jnp.where(lane < 2 * experts, table - high, 0.0))
    out_ref[:, :width] = rows_ref[...]
    out_ref[:, width:] = table.astype(jnp.bfloat16)


def table_width(experts):
    return pl.cdiv(2 * experts, 128) * 128


def pack(experts, moe_rows, route_ids, route_gates):
    total = moe_rows.shape[1] + table_width(experts)
    return pl.pallas_call(
        functools.partial(pack_kernel, experts),
        out_shape=jax.ShapeDtypeStruct((moe_rows.shape[0], total), jnp.bfloat16),
        compiler_params=pltpu.CompilerParams(vmem_limit_bytes=2 * MEBI),
        name="pack",
    )(moe_rows, route_ids, route_gates)


def spread(product, outs):
    start = 0
    for out, columns in outs:
        size = out.shape[0]
        out[:, columns] = product[start : start + size]
        start += size


def fetch(source, target, sems, start, tile, dim):
    copies = []
    for k in range(0, target.shape[dim], tile):
        inside, outside = pl.ds(k, tile), pl.ds(start + k, tile)
        if dim == 1:
            inside, outside = (slice(None), inside), (slice(None), outside)
        copy = pltpu.make_async_copy(source.at[outside], target.at[inside], sems.at[k // tile])
        copy.start()
        copies.append(copy)
    return copies


def fetch_both(gate_hbm, up_hbm, gate, up, gate_sem, up_sem, start, tile):
    copies = []
    for k in range(0, gate.shape[0], tile):
        inside, outside = pl.ds(k, tile), pl.ds(start + k, tile)
        pair = (
            pltpu.make_async_copy(gate_hbm.at[outside], gate.at[inside], gate_sem.at[k // tile]),
            pltpu.make_async_copy(up_hbm.at[outside], up.at[inside], up_sem.at[k // tile]),
        )
        for copy in pair:
            copy.start()
        copies.append(pair)
    return copies


def project(blocks, copies, gate, up, gate_sum, up_sum, tile, fresh):
    for k, pair in enumerate(copies):
        part = pl.ds(k * tile, tile)
        rows = jnp.concatenate([block[:, part] for block in blocks], axis=0)
        for copy, weight, total in zip(pair, (gate, up), (gate_sum, up_sum)):
            copy.wait()
            product = jnp.dot(rows, weight[part], preferred_element_type=jnp.float32)
            if fresh and k == 0:
                total[...] = product
            else:
                total[...] += product


def first_kernel(count, tile, *refs):
    blocks = refs[:count]
    gate_hbm, up_hbm, gate_sum, up_sum, gate, up, gate_sem, up_sem = refs[count:]
    copies = fetch_both(gate_hbm, up_hbm, gate, up, gate_sem, up_sem, 0, tile)
    project(blocks, copies, gate, up, gate_sum, up_sum, tile, True)


def first_sums(blocks, w_gate, w_up):
    units = w_gate.shape[1]
    rows = sum(block.shape[0] for block in blocks)
    columns = blocks[0].shape[1]
    tile = 1024
    return pl.pallas_call(
        functools.partial(first_kernel, len(blocks), tile),
        in_specs=[pl.BlockSpec(memory_space=pltpu.VMEM)] * len(blocks)
        + [pl.BlockSpec(memory_space=pltpu.HBM)] * 2,
        out_specs=[pl.BlockSpec(memory_space=pltpu.VMEM)] * 2,
        out_shape=[jax.ShapeDtypeStruct((rows, units), jnp.float32)] * 2,
        scratch_shapes=[pltpu.VMEM((columns, units), jnp.bfloat16)] * 2
        + [pltpu.SemaphoreType.DMA((columns // tile,))] * 2,
        cost_estimate=pl.CostEstimate(
            flops=4 * rows * columns * units,
            bytes_accessed=4 * columns * units,
            transcendentals=0,
        ),
        compiler_params=pltpu.CompilerParams(vmem_limit_bytes=20 * MEBI),
        name="first_sums",
    )(*blocks, in_hbm(w_gate), in_hbm(w_up))


def expert_kernel(count, experts, tile, down_tile, node_ref, *refs):
    blocks = refs[:count]
    gate_in, up_in, gate_hbm, up_hbm, down_hbm = refs[count : count + 5]
    outs = refs[count + 5 : -10]
    hidden_ref, share_ref, gate, up, down, gate_sum, up_sum, gate_sem, up_sem, down_sem = refs[-10:]
    start = gate_hbm.shape[0] - gate.shape[0]
    copies = fetch_both(gate_hbm, up_hbm, gate, up, gate_sem, up_sem, start, tile)
    down_copies = fetch(down_hbm, down, down_sem, 0, down_tile, 1)

    table = jnp.concatenate([block[:, gate.shape[0] :] for block in blocks], axis=0)
    table = table.astype(jnp.float32)
    lane = lax.broadcasted_iota(jnp.int32, table.shape, 1)
    mine = (lane == node_ref[0]) | (lane == node_ref[0] + experts)
    share = jnp.sum(jnp.where(mine, table, 0.0), axis=1, keepdims=True)
    share_ref[...] = jnp.broadcast_to(share, share_ref.shape)
    gate_sum[...] = gate_in[...]
    up_sum[...] = up_in[...]
    project(blocks, copies, gate, up, gate_sum, up_sum, tile, False)
    hidden_ref[...] = (jax.nn.silu(gate_sum[...]) * up_sum[...]).astype(jnp.bfloat16)
    for k, copy in enumerate(down_copies):
        part = pl.ds(k * down_tile, down_tile)
        copy.wait()
        product = jnp.dot(hidden_ref[...], down[:, part], preferred_element_type=jnp.float32)
        product = (product * share_ref[:, :1]).astype(jnp.bfloat16)
        start = k * down_tile
        for chunk in (outs[: len(outs) // 2], outs[len(outs) // 2 :]):
            if 0 <= start < chunk[0].shape[1]:
                spread(product, [(out, pl.ds(start, down_tile)) for out in chunk])
            start -= chunk[0].shape[1]


def expert(blocks, sums, w_gate, w_up, w_down, experts, node, split):
    units, columns = w_down.shape
    sizes = [block.shape[0] for block in blocks]
    rows = sum(sizes)
    tail = blocks[0].shape[1] - table_width(experts)
    tile, down_tile = 1024, 512
    return pl.pallas_call(
        functools.partial(expert_kernel, len(blocks), experts, tile, down_tile),
        in_specs=[pl.BlockSpec(memory_space=pltpu.SMEM)]
        + [pl.BlockSpec(memory_space=pltpu.VMEM)] * (len(blocks) + 2)
        + [pl.BlockSpec(memory_space=pltpu.HBM)] * 3,
        out_specs=[pl.BlockSpec(memory_space=pltpu.VMEM)] * (2 * len(sizes)),
        out_shape=[
            jax.ShapeDtypeStruct((size, chunk), jnp.bfloat16)
            for chunk in (split, columns - split)
            for size in sizes
        ],
        scratch_shapes=[
            pltpu.VMEM((rows, units), jnp.bfloat16),
            pltpu.VMEM((rows, 128), jnp.float32),
            pltpu.VMEM((tail, units), jnp.bfloat16),
            pltpu.VMEM((tail, units), jnp.bfloat16),
            pltpu.VMEM((units, columns), jnp.bfloat16),
            pltpu.VMEM((rows, units), jnp.float32),
            pltpu.VMEM((rows, units), jnp.float32),
            pltpu.SemaphoreType.DMA((tail // tile,)),
            pltpu.SemaphoreType.DMA((tail // tile,)),
            pltpu.SemaphoreType.DMA((columns // down_tile,)),
        ],
        cost_estimate=pl.CostEstimate(
            flops=4 * rows * tail * units + 2 * rows * columns * units,
            bytes_accessed=4 * tail * units + 2 * units * columns,
            transcendentals=rows * units,
        ),
        compiler_params=pltpu.CompilerParams(vmem_limit_bytes=24 * MEBI),
        name="expert",
    )(node, *blocks, *sums, in_hbm(w_gate), in_hbm(w_up), in_hbm(w_down))


def body(
    moe_rows,
    route_ids,
    route_gates,
    w_gate,
    w_up,
    w_down,
    query_latent,
    query_rope,
    cache_latent,
    cache_rope,
    cache_lengths,
):
    grid = Grid()
    high, middle, cores, _ = grid.sizes
    experts = high * middle * cores
    tokens, width = moe_rows.shape
    node = lax.axis_index(("high", "middle", "core")).astype(jnp.int32).reshape(1)
    split = width * 4 // 7
    tied = lax.optimization_barrier
    attn_latent = attention(query_latent, query_rope, cache_latent, cache_rope, cache_lengths)

    line = pack(experts, moe_rows, route_ids, route_gates)
    masks = grid.masks()
    for m in masks[:-1]:
        line = join([line, grid.swap(line, grid.high, m)])
    came = grid.swap(line, grid.high, masks[-1])
    came, attn_latent = tied((came, attn_latent))
    head, tail = join([line, came], split, line.shape[1] - split)
    head, tail = grid.over_first(head), grid.over_first(tail)
    head = grid.over_second(join(head))
    tail = join(tail)
    tail, head[0] = tied((tail, head[0]))
    tail = grid.over_second(tail)
    head += [grid.swap(block, grid.core, 1) for block in head]
    gate_sum, up_sum = first_sums(head, w_gate[0], w_up[0])
    tail[-1], gate_sum, up_sum = tied((tail[-1], gate_sum, up_sum))
    tail += [grid.swap(block, grid.core, 1) for block in tail]
    count = len(tail) // 2
    products = expert(
        tail, (gate_sum, up_sum), w_gate[0], w_up[0], w_down[0], experts, node, split
    )

    def core_sum(parts):
        sums = [add([parts[i], grid.swap(parts[count + i], grid.core, 1)]) for i in range(1, count)]
        return [add([parts[0], grid.swap(parts[count], grid.core, 1)])] + sums

    head, tail = products[: 2 * count], products[2 * count :]
    tail, head = tied((tail, core_sum(head)))
    head = grid.second_sum(head)
    tail = grid.second_sum(core_sum(tail))
    head = grid.high_sum(grid.first_sum(head))
    tail = grid.high_sum_direct(grid.first_sum(tail))
    return (jnp.concatenate([head, tail], axis=1), attn_latent)


def solution(mesh):
    groups, nodes, local = mesh.devices.shape
    split = Mesh(mesh.devices.reshape(groups, nodes // 4, 2, 2, local), ("group",) + everyone)
    node = ("high", "middle", "core")
    whole = ("group",) + everyone
    rows = P(whole, None)
    blocks = P(whole, None, None)
    return jax.shard_map(
        body,
        mesh=split,
        in_specs=(
            rows,
            rows,
            rows,
            P(node, None, "local"),
            P(node, None, "local"),
            P(node, "local", None),
            blocks,
            blocks,
            blocks,
            blocks,
            P(whole),
        ),
        out_specs=(rows, blocks),
        check_vma=False,
    )
```

```python
import functools

import jax
import jax.numpy as jnp
import numpy as np
from jax import lax
from jax.experimental import pallas as pl
from jax.experimental.pallas import tpu as pltpu
from jax.sharding import Mesh
from jax.sharding import PartitionSpec as P

score_scale = 192.0 ** (-0.5)
everyone = ("high", "middle", "core", "local")
MEBI = 1024 * 1024


def attention_kernel(lengths_ref, *refs):
    sources, (out_ref, *targets), sems = refs[:4], refs[4:-1], refs[-1]
    query_ref, query_rope_ref, cache_ref, cache_rope_ref = targets
    copies = []
    for row in range(out_ref.shape[0]):
        copies.append(
            [
                pltpu.make_async_copy(source.at[row], target.at[row], sems.at[row, i])
                for i, (source, target) in enumerate(zip(sources, targets))
            ]
        )
        for copy in copies[-1]:
            copy.start()
    for row in range(out_ref.shape[0]):
        for copy in copies[row]:
            copy.wait()
        cache = cache_ref[row]
        scores = lax.dot_general(
            query_ref[row], cache, (((1,), (1,)), ((), ())), preferred_element_type=jnp.float32
        )
        scores += jnp.dot(
            query_rope_ref[row], cache_rope_ref[row], preferred_element_type=jnp.float32
        )
        slot = lax.broadcasted_iota(jnp.int32, scores.shape, 1)
        in_range = slot < lengths_ref[row]
        scores = jnp.where(in_range, scores * score_scale, -jnp.inf)
        row_peak = jnp.max(scores, axis=1, keepdims=True)
        lifted = jnp.where(in_range, jnp.exp(scores - row_peak), 0.0)
        weights = (lifted / jnp.sum(lifted, axis=1, keepdims=True)).astype(jnp.bfloat16)
        value = jnp.dot(weights, cache, preferred_element_type=jnp.float32)
        out_ref[row] = value.astype(jnp.bfloat16)


def attention(query_latent, query_rope, cache_latent, cache_rope, cache_lengths):
    rows, heads, latent = query_latent.shape
    slots = cache_latent.shape[1]
    sources = (query_latent, query_rope, cache_latent, cache_rope)
    return pl.pallas_call(
        attention_kernel,
        in_specs=[pl.BlockSpec(memory_space=pltpu.SMEM)]
        + [pl.BlockSpec(memory_space=pltpu.HBM)] * 4,
        out_specs=pl.BlockSpec(memory_space=pltpu.VMEM),
        out_shape=jax.ShapeDtypeStruct(query_latent.shape, jnp.bfloat16),
        scratch_shapes=[pltpu.VMEM(source.shape, source.dtype) for source in sources]
        + [pltpu.SemaphoreType.DMA((rows, 4))],
        cost_estimate=pl.CostEstimate(
            flops=4 * rows * heads * slots * latent,
            bytes_accessed=2 * rows * slots * latent,
            transcendentals=rows * heads * slots,
        ),
        compiler_params=pltpu.CompilerParams(vmem_limit_bytes=8 * MEBI),
        name="attention",
    )(cache_lengths, *[in_hbm(source) for source in sources])


def in_hbm(array):
    return pltpu.with_memory_space_constraint(array, pltpu.HBM)


HIGH, MIDDLE, CORE, LOCAL = range(4)


class Grid:
    def __init__(self):
        self.sizes = tuple(lax.axis_size(name) for name in everyone)
        self.masks = []
        while self.sizes[HIGH] >> len(self.masks) > 1:
            self.masks.append(self.sizes[HIGH] >> (len(self.masks) + 1))

    def swap(self, value, digit, mask):
        pairs = []
        for place in np.ndindex(*self.sizes):
            other = list(place)
            other[digit] ^= mask
            pairs.append(
                (
                    int(np.ravel_multi_index(place, self.sizes)),
                    int(np.ravel_multi_index(other, self.sizes)),
                )
            )
        return lax.ppermute(value, everyone, pairs)

    def over(self, block, digit):
        return [block] + [self.swap(block, digit, m) for m in range(1, self.sizes[digit])]

    def sum_over(self, parts, digit):
        return add(parts[:1] + [self.swap(parts[m], digit, m) for m in range(1, len(parts))])

    def sum_rows_over(self, block, digit):
        rows = block.shape[0] // self.sizes[digit]
        parts = [block[m * rows : (m + 1) * rows] for m in range(self.sizes[digit])]
        return self.sum_over(parts, digit)

    def high_sum(self, line):
        for m in reversed(self.masks):
            half = line.shape[0] // 2
            line = add([line[:half], self.swap(line[half:], HIGH, m)])
        return line

    def high_sum_direct(self, line):
        order = [0]
        for m in self.masks:
            order += [m | other for other in order]
        rows = line.shape[0] // len(order)
        parts = [line[:rows]]
        for i in range(1, len(order)):
            parts.append(self.swap(line[i * rows : (i + 1) * rows], HIGH, order[i]))
        return add(parts)


def add(parts):
    total = parts[0].astype(jnp.float32)
    for part in parts[1:]:
        total = total + part.astype(jnp.float32)
    return total.astype(parts[0].dtype)


def join_kernel(count, *refs):
    start = 0
    for out in refs[count:]:
        columns = pl.ds(start, out.shape[1])
        out[...] = jnp.concatenate([ref[:, columns] for ref in refs[:count]], axis=0)
        start += out.shape[1]


def join(parts, *widths):
    rows = sum(part.shape[0] for part in parts)
    widths = widths or parts[0].shape[1:]
    outs = pl.pallas_call(
        functools.partial(join_kernel, len(parts)),
        in_specs=[pl.BlockSpec(memory_space=pltpu.VMEM)] * len(parts),
        out_specs=[pl.BlockSpec(memory_space=pltpu.VMEM)] * len(widths),
        out_shape=[jax.ShapeDtypeStruct((rows, width), parts[0].dtype) for width in widths],
        compiler_params=pltpu.CompilerParams(vmem_limit_bytes=2 * MEBI),
        name="join",
    )(*parts)
    return outs if len(widths) > 1 else outs[0]


def table_width(experts):
    return pl.cdiv(2 * experts, 128) * 128


def pack_kernel(experts, rows_ref, ids_ref, gates_ref, head_ref, tail_ref):
    extra = table_width(experts)
    split, width = head_ref.shape[1], tail_ref.shape[1] - extra
    gates = gates_ref[...]
    shares = 2.5 * gates / jnp.sum(gates, axis=1, keepdims=True)
    ids = ids_ref[...]
    lane = lax.broadcasted_iota(jnp.int32, (ids.shape[0], extra), 1)
    expert = jnp.where(lane < experts, lane, lane - experts)
    table = jnp.zeros(lane.shape, jnp.float32)
    for k in range(ids.shape[1]):
        table += jnp.where(expert == ids[:, k : k + 1], shares[:, k : k + 1], 0.0)
    high = table.astype(jnp.bfloat16).astype(jnp.float32)
    table = jnp.where(lane < experts, high, jnp.where(lane < 2 * experts, table - high, 0.0))
    head_ref[...] = rows_ref[:, :split]
    tail_ref[:, :width] = rows_ref[:, split:]
    tail_ref[:, width:] = table.astype(jnp.bfloat16)


def pack(split, experts, moe_rows, route_ids, route_gates):
    rows, width = moe_rows.shape
    return pl.pallas_call(
        functools.partial(pack_kernel, experts),
        out_shape=[
            jax.ShapeDtypeStruct((rows, columns), jnp.bfloat16)
            for columns in (split, width - split + table_width(experts))
        ],
        compiler_params=pltpu.CompilerParams(vmem_limit_bytes=16 * MEBI),
        name="pack",
    )(moe_rows, route_ids, route_gates)


def line_order(sizes):
    _, middle, _, local = sizes
    ways = [[], []]
    for m in range(middle):
        for n in range(local):
            ways[0].append((m, n))
            ways[1].append((n, m))
    return ways


def gathered_rows(arrays, order, size, columns):
    return [arrays[i][line * size : (line + 1) * size, columns] for i, line in order]


def fetch_both(gate_hbm, up_hbm, gate, up, gate_sem, up_sem, start, tile):
    copies = []
    for k in range(0, gate.shape[0], tile):
        inside, outside = pl.ds(k, tile), pl.ds(start + k, tile)
        pair = (
            pltpu.make_async_copy(gate_hbm.at[outside], gate.at[inside], gate_sem.at[k // tile]),
            pltpu.make_async_copy(up_hbm.at[outside], up.at[inside], up_sem.at[k // tile]),
        )
        for copy in pair:
            copy.start()
        copies.append(pair)
    return copies


def both_cores(arrays, way, sizes, columns):
    order = line_order(sizes)[way]
    arrays = arrays[way]
    count = len(arrays) // 2
    size = arrays[0].shape[0] // (1 + max(line for _, line in order))
    rows = gathered_rows(arrays[:count], order, size, columns)
    rows += gathered_rows(arrays[count:], order, size, columns)
    return jnp.concatenate(rows, axis=0)


def project(arrays, sizes, copies, gate, up, gate_sum, up_sum, tile, fresh):
    half = len(copies) // 2
    for k, pair in enumerate(copies):
        rows = both_cores(arrays, k // half, sizes, pl.ds(k % half * tile, tile))
        for copy, weight, total in zip(pair, (gate, up), (gate_sum, up_sum)):
            copy.wait()
            product = jnp.dot(
                rows, weight[pl.ds(k * tile, tile)], preferred_element_type=jnp.float32
            )
            if fresh and k == 0:
                total[...] = product
            else:
                total[...] += product


def by_way(refs, counts):
    return [refs[: counts[0]], refs[counts[0] : sum(counts)]]


def first_kernel(counts, sizes, tile, *refs):
    arrays, refs = by_way(refs, counts), refs[sum(counts) :]
    gate_hbm, up_hbm, gate_sum, up_sum, gate, up, gate_sem, up_sem = refs
    copies = fetch_both(gate_hbm, up_hbm, gate, up, gate_sem, up_sem, 0, tile)
    project(arrays, sizes, copies, gate, up, gate_sum, up_sum, tile, True)


def first_sums(arrays, sizes, rows, w_gate, w_up):
    units = w_gate.shape[1]
    columns = sum(way[0].shape[1] for way in arrays)
    tile = 1024
    counts = tuple(len(way) for way in arrays)
    return pl.pallas_call(
        functools.partial(first_kernel, counts, sizes, tile),
        in_specs=[pl.BlockSpec(memory_space=pltpu.VMEM)] * sum(counts)
        + [pl.BlockSpec(memory_space=pltpu.HBM)] * 2,
        out_specs=[pl.BlockSpec(memory_space=pltpu.VMEM)] * 2,
        out_shape=[jax.ShapeDtypeStruct((rows, units), jnp.float32)] * 2,
        scratch_shapes=[pltpu.VMEM((columns, units), jnp.bfloat16)] * 2
        + [pltpu.SemaphoreType.DMA((columns // tile,))] * 2,
        cost_estimate=pl.CostEstimate(
            flops=4 * rows * columns * units,
            bytes_accessed=4 * columns * units,
            transcendentals=0,
        ),
        compiler_params=pltpu.CompilerParams(vmem_limit_bytes=20 * MEBI),
        name="first_sums",
    )(*arrays[0], *arrays[1], in_hbm(w_gate), in_hbm(w_up))


def expert_kernel(counts, sizes, experts, tile, node_ref, *refs):
    arrays, refs = by_way(refs, counts), refs[sum(counts) :]
    gate_in, up_in, gate_hbm, up_hbm, down_hbm = refs[:5]
    outs = refs[5:-10]
    hidden_ref, share_ref, gate, up, down, gate_sum, up_sum, gate_sem, up_sem, down_sem = refs[-10:]
    start = gate_hbm.shape[0] - gate.shape[0]
    copies = fetch_both(gate_hbm, up_hbm, gate, up, gate_sem, up_sem, start, tile)
    quarters = down_sem.shape[0]
    quarter = down.shape[1] // quarters
    down_copies = []
    for k in range(quarters):
        part = pl.ds(k * quarter, quarter)
        down_copies.append(
            pltpu.make_async_copy(down_hbm.at[:, part], down.at[:, part], down_sem.at[k])
        )
        down_copies[-1].start()

    width = gate.shape[0] // 2
    behind = pl.ds(width, arrays[1][0].shape[1] - width)
    table = both_cores(arrays, 1, sizes, behind).astype(jnp.float32)
    lane = lax.broadcasted_iota(jnp.int32, table.shape, 1)
    mine = (lane == node_ref[0]) | (lane == node_ref[0] + experts)
    share = jnp.sum(jnp.where(mine, table, 0.0), axis=1, keepdims=True)
    share_ref[...] = jnp.broadcast_to(share, share_ref.shape)
    gate_sum[...] = gate_in[...]
    up_sum[...] = up_in[...]
    project(arrays, sizes, copies, gate, up, gate_sum, up_sum, tile, False)
    hidden_ref[...] = (jax.nn.silu(gate_sum[...]) * up_sum[...]).astype(jnp.bfloat16)
    for k, copy in enumerate(down_copies):
        copy.wait()
        order = line_order(sizes)[k % 2]
        each = 2 + max(i for i, _ in order)
        group, outs = outs[:each], outs[each:]
        size = hidden_ref.shape[0] // (2 * len(order))
        for piece in range(0, quarter, quarter // 2):
            part = pl.ds(k * quarter + piece, quarter // 2)
            product = jnp.dot(hidden_ref[...], down[:, part], preferred_element_type=jnp.float32)
            product = (product * share_ref[:, :1]).astype(jnp.bfloat16)
            columns = pl.ds(piece, quarter // 2)
            for i, line in order:
                row = order.index((i, line)) * size
                group[i][line * size : (line + 1) * size, columns] = product[row : row + size]
                row += len(order) * size
                lines = 1 + max(line for _, line in order)
                place = ((i - 1) % (each - 1)) * lines + line
                group[-1][place * size : (place + 1) * size, columns] = product[row : row + size]


def expert(arrays, sizes, rows, sums, w_gate, w_up, w_down, experts, node):
    units, columns = w_down.shape
    tail = sum(way[0].shape[1] for way in arrays) - table_width(experts)
    tile = 512
    counts = tuple(len(way) for way in arrays)
    out_shapes = []
    for k in range(4):
        places = (sizes[MIDDLE], sizes[LOCAL])[k % 2]
        size = rows // 2 // places
        out_shapes += [(size, columns // 4)] * places + [(rows // 2, columns // 4)]
    return pl.pallas_call(
        functools.partial(expert_kernel, counts, sizes, experts, tile),
        in_specs=[pl.BlockSpec(memory_space=pltpu.SMEM)]
        + [pl.BlockSpec(memory_space=pltpu.VMEM)] * (sum(counts) + 2)
        + [pl.BlockSpec(memory_space=pltpu.HBM)] * 3,
        out_specs=[pl.BlockSpec(memory_space=pltpu.VMEM)] * len(out_shapes),
        out_shape=[jax.ShapeDtypeStruct(shape, jnp.bfloat16) for shape in out_shapes],
        scratch_shapes=[
            pltpu.VMEM((rows, units), jnp.bfloat16),
            pltpu.VMEM((rows, 128), jnp.float32),
            pltpu.VMEM((tail, units), jnp.bfloat16),
            pltpu.VMEM((tail, units), jnp.bfloat16),
            pltpu.VMEM((units, columns), jnp.bfloat16),
            pltpu.VMEM((rows, units), jnp.float32),
            pltpu.VMEM((rows, units), jnp.float32),
            pltpu.SemaphoreType.DMA((tail // tile,)),
            pltpu.SemaphoreType.DMA((tail // tile,)),
            pltpu.SemaphoreType.DMA((4,)),
        ],
        cost_estimate=pl.CostEstimate(
            flops=4 * rows * tail * units + 2 * rows * columns * units,
            bytes_accessed=4 * tail * units + 2 * units * columns,
            transcendentals=rows * units,
        ),
        compiler_params=pltpu.CompilerParams(vmem_limit_bytes=24 * MEBI),
        name="expert",
    )(node, *arrays[0], *arrays[1], *sums, in_hbm(w_gate), in_hbm(w_up), in_hbm(w_down))


def body(
    moe_rows,
    route_ids,
    route_gates,
    w_gate,
    w_up,
    w_down,
    query_latent,
    query_rope,
    cache_latent,
    cache_rope,
    cache_lengths,
):
    grid = Grid()
    high, middle, cores, _ = grid.sizes
    experts = high * middle * cores
    tokens, width = moe_rows.shape
    node = lax.axis_index(("high", "middle", "core")).astype(jnp.int32).reshape(1)
    split = width * 4 // 7
    tied = lax.optimization_barrier
    attn_latent = attention(query_latent, query_rope, cache_latent, cache_rope, cache_lengths)

    def join_halves(parts):
        half = (width - split if parts[0].shape[1] < split else split) // 2
        return join(parts, half, parts[0].shape[1] - half)

    def step(blocks):
        return [grid.over(blocks[0], LOCAL), grid.over(blocks[1], MIDDLE)]

    def second_step(blocks):
        return [grid.over(blocks[0], MIDDLE), grid.over(blocks[1], LOCAL)]

    def with_other_core(ways):
        return [way + [grid.swap(block, CORE, 1) for block in way] for way in ways]

    head, tail = pack(split, experts, moe_rows, route_ids, route_gates)
    came = grid.swap(head, HIGH, grid.masks[0])
    tail, came = tied((tail, came))
    head = [head, came]
    for m in grid.masks[1:]:
        line = join(head)
        head = [line, grid.swap(line, HIGH, m)]
    head = join_halves(head)
    came = grid.swap(tail, HIGH, grid.masks[0])
    head, came = tied((head, came))
    tail = [tail, came]
    for m in grid.masks[1:]:
        line = join(tail)
        tail = [line, grid.swap(line, HIGH, m)]
    tail = join_halves(tail)
    head = step(head)
    head, tail, attn_latent = tied(([join(head[0]), join(head[1])], tail, attn_latent))
    head, tail = tied((second_step(head), step(tail)))
    head = with_other_core(head)
    tail = second_step([join(tail[0]), join(tail[1])])
    rows = 2 * grid.sizes[MIDDLE] * grid.sizes[LOCAL] * high * tokens
    sums = first_sums(head, grid.sizes, rows, w_gate[0], w_up[0])
    tail, sums = tied((tail, sums))
    tail = with_other_core(tail)
    products = expert(
        tail, grid.sizes, rows, sums, w_gate[0], w_up[0], w_down[0], experts, node
    )

    digits = (MIDDLE, LOCAL)

    def core_sums(arrays):
        sums = []
        for way in range(2):
            places = grid.sizes[digits[way]]
            mine, other, arrays = arrays[:places], arrays[places], arrays[places + 1 :]
            other = grid.swap(other, CORE, 1)
            size = mine[0].shape[0]
            sums.append(
                [
                    add([mine[i], other[(i - 1) % places * size :][:size]])
                    for i in range(places)
                ]
            )
        return sums

    def second_sums(sums):
        return [grid.sum_over(sums[way], digits[way]) for way in range(2)]

    def first_axis_sums(blocks):
        return jnp.concatenate(
            [grid.sum_rows_over(blocks[way], digits[1 - way]) for way in range(2)], axis=1
        )

    head, tail = products[: len(products) // 2], products[len(products) // 2 :]
    tail, head = tied((tail, core_sums(head)))
    head = first_axis_sums(second_sums(head))
    head, tail = tied((head, second_sums(core_sums(tail))))
    head = grid.high_sum(head)
    tail = grid.high_sum_direct(first_axis_sums(tail))
    return (jnp.concatenate([head, tail], axis=1), attn_latent)


def solution(mesh):
    groups, nodes, local = mesh.devices.shape
    split = Mesh(mesh.devices.reshape(groups, nodes // 4, 2, 2, local), ("group",) + everyone)
    node = ("high", "middle", "core")
    whole = ("group",) + everyone
    rows = P(whole, None)
    blocks = P(whole, None, None)
    return jax.shard_map(
        body,
        mesh=split,
        in_specs=(
            rows,
            rows,
            rows,
            P(node, None, "local"),
            P(node, None, "local"),
            P(node, "local", None),
            blocks,
            blocks,
            blocks,
            blocks,
            P(whole),
        ),
        out_specs=(rows, blocks),
        check_vma=False,
    )
```

```python
import functools

import jax
import jax.numpy as jnp
import numpy as np
from jax import lax
from jax.experimental import pallas as pl
from jax.experimental.pallas import tpu as pltpu
from jax.sharding import Mesh
from jax.sharding import PartitionSpec as P

score_scale = 192.0 ** (-0.5)
everyone = ("high", "middle", "core", "local")
MEBI = 1024 * 1024


def attention_kernel(lengths_ref, *refs):
    sources, (out_ref, *targets), sems = refs[:4], refs[4:-1], refs[-1]
    query_ref, query_rope_ref, cache_ref, cache_rope_ref = targets
    copies = []
    for row in range(out_ref.shape[0]):
        copies.append(
            [
                pltpu.make_async_copy(source.at[row], target.at[row], sems.at[row, i])
                for i, (source, target) in enumerate(zip(sources, targets))
            ]
        )
        for copy in copies[-1]:
            copy.start()
    for row in range(out_ref.shape[0]):
        for copy in copies[row]:
            copy.wait()
        cache = cache_ref[row]
        scores = lax.dot_general(
            query_ref[row], cache, (((1,), (1,)), ((), ())), preferred_element_type=jnp.float32
        )
        scores += jnp.dot(
            query_rope_ref[row], cache_rope_ref[row], preferred_element_type=jnp.float32
        )
        slot = lax.broadcasted_iota(jnp.int32, scores.shape, 1)
        in_range = slot < lengths_ref[row]
        scores = jnp.where(in_range, scores * score_scale, -jnp.inf)
        row_peak = jnp.max(scores, axis=1, keepdims=True)
        lifted = jnp.where(in_range, jnp.exp(scores - row_peak), 0.0)
        weights = (lifted / jnp.sum(lifted, axis=1, keepdims=True)).astype(jnp.bfloat16)
        value = jnp.dot(weights, cache, preferred_element_type=jnp.float32)
        out_ref[row] = value.astype(jnp.bfloat16)


def attention(query_latent, query_rope, cache_latent, cache_rope, cache_lengths):
    rows, heads, latent = query_latent.shape
    slots = cache_latent.shape[1]
    sources = (query_latent, query_rope, cache_latent, cache_rope)
    return pl.pallas_call(
        attention_kernel,
        in_specs=[pl.BlockSpec(memory_space=pltpu.SMEM)]
        + [pl.BlockSpec(memory_space=pltpu.HBM)] * 4,
        out_specs=pl.BlockSpec(memory_space=pltpu.VMEM),
        out_shape=jax.ShapeDtypeStruct(query_latent.shape, jnp.bfloat16),
        scratch_shapes=[pltpu.VMEM(source.shape, source.dtype) for source in sources]
        + [pltpu.SemaphoreType.DMA((rows, 4))],
        cost_estimate=pl.CostEstimate(
            flops=4 * rows * heads * slots * latent,
            bytes_accessed=2 * rows * slots * latent,
            transcendentals=rows * heads * slots,
        ),
        compiler_params=pltpu.CompilerParams(vmem_limit_bytes=8 * MEBI),
        name="attention",
    )(cache_lengths, *[in_hbm(source) for source in sources])


def in_hbm(array):
    return pltpu.with_memory_space_constraint(array, pltpu.HBM)


HIGH, MIDDLE, CORE, LOCAL = range(4)


class Grid:
    def __init__(self):
        self.sizes = tuple(lax.axis_size(name) for name in everyone)
        self.masks = []
        while self.sizes[HIGH] >> len(self.masks) > 1:
            self.masks.append(self.sizes[HIGH] >> (len(self.masks) + 1))

    def swap(self, value, digit, mask):
        pairs = []
        for place in np.ndindex(*self.sizes):
            other = list(place)
            other[digit] ^= mask
            pairs.append(
                (
                    int(np.ravel_multi_index(place, self.sizes)),
                    int(np.ravel_multi_index(other, self.sizes)),
                )
            )
        return lax.ppermute(value, everyone, pairs)

    def over(self, block, digit):
        return [block] + [self.swap(block, digit, m) for m in range(1, self.sizes[digit])]

    def receive(self, parts, digit):
        return parts[:1] + [self.swap(parts[m], digit, m) for m in range(1, len(parts))]

    def receive_rows(self, block, digit):
        rows = block.shape[0] // self.sizes[digit]
        parts = [block[m * rows : (m + 1) * rows] for m in range(self.sizes[digit])]
        return self.receive(parts, digit)

    def receive_half(self, line, mask):
        half = line.shape[0] // 2
        return [line[:half], self.swap(line[half:], HIGH, mask)]

    def receive_high(self, line):
        order = [0]
        for m in self.masks:
            order += [m | other for other in order]
        rows = line.shape[0] // len(order)
        parts = [line[:rows]]
        for i in range(1, len(order)):
            parts.append(self.swap(line[i * rows : (i + 1) * rows], HIGH, order[i]))
        return parts


def add(parts):
    total = parts[0].astype(jnp.float32)
    for part in parts[1:]:
        total = total + part.astype(jnp.float32)
    return total.astype(parts[0].dtype)


def join_kernel(count, *refs):
    start = 0
    for out in refs[count:]:
        columns = pl.ds(start, out.shape[1])
        out[...] = jnp.concatenate([ref[:, columns] for ref in refs[:count]], axis=0)
        start += out.shape[1]


def join(parts, *widths):
    rows = sum(part.shape[0] for part in parts)
    widths = widths or parts[0].shape[1:]
    outs = pl.pallas_call(
        functools.partial(join_kernel, len(parts)),
        in_specs=[pl.BlockSpec(memory_space=pltpu.VMEM)] * len(parts),
        out_specs=[pl.BlockSpec(memory_space=pltpu.VMEM)] * len(widths),
        out_shape=[jax.ShapeDtypeStruct((rows, width), parts[0].dtype) for width in widths],
        compiler_params=pltpu.CompilerParams(vmem_limit_bytes=2 * MEBI),
        name="join",
    )(*parts)
    return outs if len(widths) > 1 else outs[0]


def table_width(experts):
    return pl.cdiv(2 * experts, 128) * 128


def pack_kernel(experts, *refs):
    sources, (head_ref, tail_ref, *targets), sems = refs[:3], refs[3:-1], refs[-1]
    copies = [
        pltpu.make_async_copy(source, target, sems.at[i])
        for i, (source, target) in enumerate(zip(sources, targets))
    ]
    for copy in copies:
        copy.start()
    rows_ref, ids_ref, gates_ref = targets
    for copy in copies[1:]:
        copy.wait()
    extra = table_width(experts)
    split, width = head_ref.shape[1], tail_ref.shape[1] - extra
    gates = gates_ref[...]
    shares = 2.5 * gates / jnp.sum(gates, axis=1, keepdims=True)
    ids = ids_ref[...]
    lane = lax.broadcasted_iota(jnp.int32, (ids.shape[0], extra), 1)
    expert = jnp.where(lane < experts, lane, lane - experts)
    table = jnp.zeros(lane.shape, jnp.float32)
    for k in range(ids.shape[1]):
        table += jnp.where(expert == ids[:, k : k + 1], shares[:, k : k + 1], 0.0)
    high = table.astype(jnp.bfloat16).astype(jnp.float32)
    table = jnp.where(lane < experts, high, jnp.where(lane < 2 * experts, table - high, 0.0))
    copies[0].wait()
    head_ref[...] = rows_ref[:, :split]
    tail_ref[:, :width] = rows_ref[:, split:]
    tail_ref[:, width:] = table.astype(jnp.bfloat16)


def pack(split, experts, moe_rows, route_ids, route_gates):
    rows, width = moe_rows.shape
    sources = (moe_rows, route_ids, route_gates)
    return pl.pallas_call(
        functools.partial(pack_kernel, experts),
        in_specs=[pl.BlockSpec(memory_space=pltpu.HBM)] * 3,
        out_specs=[pl.BlockSpec(memory_space=pltpu.VMEM)] * 2,
        scratch_shapes=[pltpu.VMEM(source.shape, source.dtype) for source in sources]
        + [pltpu.SemaphoreType.DMA((3,))],
        out_shape=[
            jax.ShapeDtypeStruct((rows, columns), jnp.bfloat16)
            for columns in (split, width - split + table_width(experts))
        ],
        compiler_params=pltpu.CompilerParams(vmem_limit_bytes=4 * MEBI),
        name="pack",
    )(*[in_hbm(source) for source in sources])


def line_order(sizes):
    _, middle, _, local = sizes
    ways = [[], []]
    for m in range(middle):
        for n in range(local):
            ways[0].append((m, n))
            ways[1].append((n, m))
    return ways


def gathered_rows(arrays, order, size, columns):
    return [arrays[i][line * size : (line + 1) * size, columns] for i, line in order]


def fetch_both(gate_hbm, up_hbm, gate, up, gate_sem, up_sem, start, tile):
    copies = []
    for k in range(0, gate.shape[0], tile):
        inside, outside = pl.ds(k, tile), pl.ds(start + k, tile)
        pair = (
            pltpu.make_async_copy(gate_hbm.at[outside], gate.at[inside], gate_sem.at[k // tile]),
            pltpu.make_async_copy(up_hbm.at[outside], up.at[inside], up_sem.at[k // tile]),
        )
        for copy in pair:
            copy.start()
        copies.append(pair)
    return copies


def both_cores(arrays, way, sizes, columns):
    order = line_order(sizes)[way]
    arrays = arrays[way]
    count = len(arrays) // 2
    size = arrays[0].shape[0] // (1 + max(line for _, line in order))
    rows = gathered_rows(arrays[:count], order, size, columns)
    rows += gathered_rows(arrays[count:], order, size, columns)
    return jnp.concatenate(rows, axis=0)


def project(arrays, sizes, copies, gate, up, gate_sum, up_sum, tile, fresh):
    half = len(copies) // 2
    for k, pair in enumerate(copies):
        rows = both_cores(arrays, k // half, sizes, pl.ds(k % half * tile, tile))
        for copy, weight, total in zip(pair, (gate, up), (gate_sum, up_sum)):
            copy.wait()
            product = jnp.dot(
                rows, weight[pl.ds(k * tile, tile)], preferred_element_type=jnp.float32
            )
            if fresh and k == 0:
                total[...] = product
            else:
                total[...] += product


def by_way(refs, counts):
    return [refs[: counts[0]], refs[counts[0] : sum(counts)]]


def first_kernel(counts, sizes, tile, *refs):
    arrays, refs = by_way(refs, counts), refs[sum(counts) :]
    gate_hbm, up_hbm, gate_sum, up_sum, gate, up, gate_sem, up_sem = refs
    copies = fetch_both(gate_hbm, up_hbm, gate, up, gate_sem, up_sem, 0, tile)
    project(arrays, sizes, copies, gate, up, gate_sum, up_sum, tile, True)


def first_sums(arrays, sizes, rows, w_gate, w_up):
    units = w_gate.shape[1]
    columns = sum(way[0].shape[1] for way in arrays)
    tile = 1024
    counts = tuple(len(way) for way in arrays)
    return pl.pallas_call(
        functools.partial(first_kernel, counts, sizes, tile),
        in_specs=[pl.BlockSpec(memory_space=pltpu.VMEM)] * sum(counts)
        + [pl.BlockSpec(memory_space=pltpu.HBM)] * 2,
        out_specs=[pl.BlockSpec(memory_space=pltpu.VMEM)] * 2,
        out_shape=[jax.ShapeDtypeStruct((rows, units), jnp.float32)] * 2,
        scratch_shapes=[pltpu.VMEM((columns, units), jnp.bfloat16)] * 2
        + [pltpu.SemaphoreType.DMA((columns // tile,))] * 2,
        cost_estimate=pl.CostEstimate(
            flops=4 * rows * columns * units,
            bytes_accessed=4 * columns * units,
            transcendentals=0,
        ),
        compiler_params=pltpu.CompilerParams(vmem_limit_bytes=20 * MEBI),
        name="first_sums",
    )(*arrays[0], *arrays[1], in_hbm(w_gate), in_hbm(w_up))


def expert_kernel(counts, sizes, experts, tile, node_ref, *refs):
    arrays, refs = by_way(refs, counts), refs[sum(counts) :]
    gate_in, up_in, gate_hbm, up_hbm, down_hbm = refs[:5]
    outs = refs[5:-10]
    hidden_ref, share_ref, gate, up, down, gate_sum, up_sum, gate_sem, up_sem, down_sem = refs[-10:]
    start = gate_hbm.shape[0] - gate.shape[0]
    copies = fetch_both(gate_hbm, up_hbm, gate, up, gate_sem, up_sem, start, tile)
    quarters = down_sem.shape[0]
    quarter = down.shape[1] // quarters
    down_copies = []
    for k in range(quarters):
        part = pl.ds(k * quarter, quarter)
        down_copies.append(
            pltpu.make_async_copy(down_hbm.at[:, part], down.at[:, part], down_sem.at[k])
        )
        down_copies[-1].start()

    width = gate.shape[0] // 2
    behind = pl.ds(width, arrays[1][0].shape[1] - width)
    table = both_cores(arrays, 1, sizes, behind).astype(jnp.float32)
    lane = lax.broadcasted_iota(jnp.int32, table.shape, 1)
    mine = (lane == node_ref[0]) | (lane == node_ref[0] + experts)
    share = jnp.sum(jnp.where(mine, table, 0.0), axis=1, keepdims=True)
    share_ref[...] = jnp.broadcast_to(share, share_ref.shape)
    gate_sum[...] = gate_in[...]
    up_sum[...] = up_in[...]
    project(arrays, sizes, copies, gate, up, gate_sum, up_sum, tile, False)
    hidden_ref[...] = (jax.nn.silu(gate_sum[...]) * up_sum[...]).astype(jnp.bfloat16)
    for k, copy in enumerate(down_copies):
        copy.wait()
        order = line_order(sizes)[k % 2]
        each = 2 + max(i for i, _ in order)
        group, outs = outs[:each], outs[each:]
        size = hidden_ref.shape[0] // (2 * len(order))
        for piece in range(0, quarter, quarter // 2):
            part = pl.ds(k * quarter + piece, quarter // 2)
            product = jnp.dot(hidden_ref[...], down[:, part], preferred_element_type=jnp.float32)
            product = (product * share_ref[:, :1]).astype(jnp.bfloat16)
            columns = pl.ds(piece, quarter // 2)
            for i, line in order:
                row = order.index((i, line)) * size
                group[i][line * size : (line + 1) * size, columns] = product[row : row + size]
                row += len(order) * size
                lines = 1 + max(line for _, line in order)
                place = ((i - 1) % (each - 1)) * lines + line
                group[-1][place * size : (place + 1) * size, columns] = product[row : row + size]


def expert(arrays, sizes, rows, sums, w_gate, w_up, w_down, experts, node):
    units, columns = w_down.shape
    tail = sum(way[0].shape[1] for way in arrays) - table_width(experts)
    tile = 512
    counts = tuple(len(way) for way in arrays)
    out_shapes = []
    for k in range(4):
        places = (sizes[MIDDLE], sizes[LOCAL])[k % 2]
        size = rows // 2 // places
        out_shapes += [(size, columns // 4)] * places + [(rows // 2, columns // 4)]
    return pl.pallas_call(
        functools.partial(expert_kernel, counts, sizes, experts, tile),
        in_specs=[pl.BlockSpec(memory_space=pltpu.SMEM)]
        + [pl.BlockSpec(memory_space=pltpu.VMEM)] * (sum(counts) + 2)
        + [pl.BlockSpec(memory_space=pltpu.HBM)] * 3,
        out_specs=[pl.BlockSpec(memory_space=pltpu.VMEM)] * len(out_shapes),
        out_shape=[jax.ShapeDtypeStruct(shape, jnp.bfloat16) for shape in out_shapes],
        scratch_shapes=[
            pltpu.VMEM((rows, units), jnp.bfloat16),
            pltpu.VMEM((rows, 128), jnp.float32),
            pltpu.VMEM((tail, units), jnp.bfloat16),
            pltpu.VMEM((tail, units), jnp.bfloat16),
            pltpu.VMEM((units, columns), jnp.bfloat16),
            pltpu.VMEM((rows, units), jnp.float32),
            pltpu.VMEM((rows, units), jnp.float32),
            pltpu.SemaphoreType.DMA((tail // tile,)),
            pltpu.SemaphoreType.DMA((tail // tile,)),
            pltpu.SemaphoreType.DMA((4,)),
        ],
        cost_estimate=pl.CostEstimate(
            flops=4 * rows * tail * units + 2 * rows * columns * units,
            bytes_accessed=4 * tail * units + 2 * units * columns,
            transcendentals=rows * units,
        ),
        compiler_params=pltpu.CompilerParams(vmem_limit_bytes=24 * MEBI),
        name="expert",
    )(node, *arrays[0], *arrays[1], *sums, in_hbm(w_gate), in_hbm(w_up), in_hbm(w_down))


def body(
    moe_rows,
    route_ids,
    route_gates,
    w_gate,
    w_up,
    w_down,
    query_latent,
    query_rope,
    cache_latent,
    cache_rope,
    cache_lengths,
):
    grid = Grid()
    high, middle, cores, _ = grid.sizes
    experts = high * middle * cores
    tokens, width = moe_rows.shape
    node = lax.axis_index(("high", "middle", "core")).astype(jnp.int32).reshape(1)
    split = width * 4 // 7
    tied = lax.optimization_barrier
    attn_latent = attention(query_latent, query_rope, cache_latent, cache_rope, cache_lengths)

    def join_halves(parts):
        half = (width - split if parts[0].shape[1] < split else split) // 2
        return join(parts, half, parts[0].shape[1] - half)

    def step(blocks):
        return [grid.over(blocks[0], LOCAL), grid.over(blocks[1], MIDDLE)]

    def second_step(blocks):
        return [grid.over(blocks[0], MIDDLE), grid.over(blocks[1], LOCAL)]

    def with_other_core(ways):
        return [way + [grid.swap(block, CORE, 1) for block in way] for way in ways]

    head, tail = pack(split, experts, moe_rows, route_ids, route_gates)
    came = grid.swap(head, HIGH, grid.masks[0])
    tail, came, attn_latent = tied((tail, came, attn_latent))
    head = [head, came]
    for m in grid.masks[1:]:
        line = join(head)
        head = [line, grid.swap(line, HIGH, m)]
    head = join_halves(head)
    came = grid.swap(tail, HIGH, grid.masks[0])
    head, came = tied((head, came))
    tail = [tail, came]
    for m in grid.masks[1:]:
        line = join(tail)
        tail = [line, grid.swap(line, HIGH, m)]
    tail = join_halves(tail)
    head = step(head)
    head, tail = tied(([join(head[0]), join(head[1])], tail))
    head, tail = tied((second_step(head), step(tail)))
    head = with_other_core(head)
    tail = second_step([join(tail[0]), join(tail[1])])
    rows = 2 * grid.sizes[MIDDLE] * grid.sizes[LOCAL] * high * tokens
    sums = first_sums(head, grid.sizes, rows, w_gate[0], w_up[0])
    tail, sums = tied((tail, sums))
    tail = with_other_core(tail)
    products = expert(
        tail, grid.sizes, rows, sums, w_gate[0], w_up[0], w_down[0], experts, node
    )

    digits = (MIDDLE, LOCAL)

    def core_sums(arrays):
        sums = []
        for way in range(2):
            places = grid.sizes[digits[way]]
            mine, other, arrays = arrays[:places], arrays[places], arrays[places + 1 :]
            other = grid.swap(other, CORE, 1)
            size = mine[0].shape[0]
            sums.append(
                [
                    add([mine[i], other[(i - 1) % places * size :][:size]])
                    for i in range(places)
                ]
            )
        return sums

    def second_axis(ways):
        return [grid.receive(ways[way], digits[way]) for way in range(2)]

    def first_axis(ways):
        return [grid.receive_rows(add(ways[way]), digits[1 - way]) for way in range(2)]

    def line_of(ways):
        return jnp.concatenate([add(way) for way in ways], axis=1)

    head, tail = products[: len(products) // 2], products[len(products) // 2 :]
    tail, head = tied((tail, core_sums(head)))
    head, tail = tied((second_axis(head), core_sums(tail)))
    head, tail = tied((first_axis(head), second_axis(tail)))
    head = line_of(head)
    masks = grid.masks[::-1]
    head, tail = tied((grid.receive_half(head, masks[0]), first_axis(tail)))
    for m in masks[1:]:
        head = grid.receive_half(add(head), m)
    tail = grid.receive_high(line_of(tail))
    head, tail = tied((head, tail))
    return (jnp.concatenate([add(head), add(tail)], axis=1), attn_latent)


def solution(mesh):
    groups, nodes, local = mesh.devices.shape
    split = Mesh(mesh.devices.reshape(groups, nodes // 4, 2, 2, local), ("group",) + everyone)
    node = ("high", "middle", "core")
    whole = ("group",) + everyone
    rows = P(whole, None)
    blocks = P(whole, None, None)
    return jax.shard_map(
        body,
        mesh=split,
        in_specs=(
            rows,
            rows,
            rows,
            P(node, None, "local"),
            P(node, None, "local"),
            P(node, "local", None),
            blocks,
            blocks,
            blocks,
            blocks,
            P(whole),
        ),
        out_specs=(rows, blocks),
        check_vma=False,
    )
```

```python
import functools

import jax
import jax.numpy as jnp
import numpy as np
from jax import lax
from jax.experimental import pallas as pl
from jax.experimental.pallas import tpu as pltpu
from jax.sharding import Mesh
from jax.sharding import PartitionSpec as P

score_scale = 192.0 ** (-0.5)
everyone = ("high", "middle", "core", "local")
MEBI = 1024 * 1024


def attention_kernel(lengths_ref, *refs):
    sources, (out_ref, *targets), sems = refs[:4], refs[4:-1], refs[-1]
    query_ref, query_rope_ref, cache_ref, cache_rope_ref = targets
    copies = []
    for row in range(out_ref.shape[0]):
        copies.append(
            [
                pltpu.make_async_copy(source.at[row], target.at[row], sems.at[row, i])
                for i, (source, target) in enumerate(zip(sources, targets))
            ]
        )
        for copy in copies[-1]:
            copy.start()
    for row in range(out_ref.shape[0]):
        for copy in copies[row]:
            copy.wait()
        cache = cache_ref[row]
        scores = lax.dot_general(
            query_ref[row], cache, (((1,), (1,)), ((), ())), preferred_element_type=jnp.float32
        )
        scores += jnp.dot(
            query_rope_ref[row], cache_rope_ref[row], preferred_element_type=jnp.float32
        )
        slot = lax.broadcasted_iota(jnp.int32, scores.shape, 1)
        in_range = slot < lengths_ref[row]
        scores = jnp.where(in_range, scores * score_scale, -jnp.inf)
        row_peak = jnp.max(scores, axis=1, keepdims=True)
        lifted = jnp.where(in_range, jnp.exp(scores - row_peak), 0.0)
        weights = (lifted / jnp.sum(lifted, axis=1, keepdims=True)).astype(jnp.bfloat16)
        value = jnp.dot(weights, cache, preferred_element_type=jnp.float32)
        out_ref[row] = value.astype(jnp.bfloat16)


def attention(query_latent, query_rope, cache_latent, cache_rope, cache_lengths):
    rows, heads, latent = query_latent.shape
    slots = cache_latent.shape[1]
    sources = (query_latent, query_rope, cache_latent, cache_rope)
    return pl.pallas_call(
        attention_kernel,
        in_specs=[pl.BlockSpec(memory_space=pltpu.SMEM)]
        + [pl.BlockSpec(memory_space=pltpu.HBM)] * 4,
        out_specs=pl.BlockSpec(memory_space=pltpu.VMEM),
        out_shape=jax.ShapeDtypeStruct(query_latent.shape, jnp.bfloat16),
        scratch_shapes=[pltpu.VMEM(source.shape, source.dtype) for source in sources]
        + [pltpu.SemaphoreType.DMA((rows, 4))],
        cost_estimate=pl.CostEstimate(
            flops=4 * rows * heads * slots * latent,
            bytes_accessed=2 * rows * slots * latent,
            transcendentals=rows * heads * slots,
        ),
        compiler_params=pltpu.CompilerParams(vmem_limit_bytes=8 * MEBI),
        name="attention",
    )(cache_lengths, *[in_hbm(source) for source in sources])


def in_hbm(array):
    return pltpu.with_memory_space_constraint(array, pltpu.HBM)


HIGH, MIDDLE, CORE, LOCAL = range(4)


class Grid:
    def __init__(self):
        self.sizes = tuple(lax.axis_size(name) for name in everyone)
        self.masks = []
        while self.sizes[HIGH] >> len(self.masks) > 1:
            self.masks.append(self.sizes[HIGH] >> (len(self.masks) + 1))

    def swap(self, value, digit, mask):
        pairs = []
        for place in np.ndindex(*self.sizes):
            other = list(place)
            other[digit] ^= mask
            pairs.append(
                (
                    int(np.ravel_multi_index(place, self.sizes)),
                    int(np.ravel_multi_index(other, self.sizes)),
                )
            )
        return lax.ppermute(value, everyone, pairs)

    def over(self, block, digit):
        return [block] + [self.swap(block, digit, m) for m in range(1, self.sizes[digit])]

    def receive(self, parts, digit):
        return parts[:1] + [self.swap(parts[m], digit, m) for m in range(1, len(parts))]

    def receive_rows(self, block, digit):
        rows = block.shape[0] // self.sizes[digit]
        parts = [block[m * rows : (m + 1) * rows] for m in range(self.sizes[digit])]
        return self.receive(parts, digit)

    def receive_half(self, line, mask):
        half = line.shape[0] // 2
        return [line[:half], self.swap(line[half:], HIGH, mask)]

    def receive_high(self, line):
        order = [0]
        for m in self.masks:
            order += [m | other for other in order]
        rows = line.shape[0] // len(order)
        parts = [line[:rows]]
        for i in range(1, len(order)):
            parts.append(self.swap(line[i * rows : (i + 1) * rows], HIGH, order[i]))
        return parts


def add(parts):
    total = parts[0].astype(jnp.float32)
    for part in parts[1:]:
        total = total + part.astype(jnp.float32)
    return total.astype(parts[0].dtype)


def join_kernel(count, ranges, *refs):
    for out, parts in zip(refs[count:], ranges):
        start = 0
        for first, size in parts:
            columns = pl.ds(first, size)
            out[:, start : start + size] = jnp.concatenate(
                [ref[:, columns] for ref in refs[:count]], axis=0
            )
            start += size


def join(parts, *ranges):
    rows = sum(part.shape[0] for part in parts)
    ranges = ranges or ([(0, parts[0].shape[1])],)
    outs = pl.pallas_call(
        functools.partial(join_kernel, len(parts), ranges),
        in_specs=[pl.BlockSpec(memory_space=pltpu.VMEM)] * len(parts),
        out_specs=[pl.BlockSpec(memory_space=pltpu.VMEM)] * len(ranges),
        out_shape=[
            jax.ShapeDtypeStruct((rows, sum(size for _, size in columns)), parts[0].dtype)
            for columns in ranges
        ],
        compiler_params=pltpu.CompilerParams(vmem_limit_bytes=4 * MEBI),
        name="join",
    )(*parts)
    return outs if len(ranges) > 1 else outs[0]


def table_width(experts):
    return pl.cdiv(2 * experts, 128) * 128


def pack_kernel(experts, *refs):
    sources, (out_ref, *targets), sems = refs[:3], refs[3:-1], refs[-1]
    copies = [
        pltpu.make_async_copy(source, target, sems.at[i])
        for i, (source, target) in enumerate(zip(sources, targets))
    ]
    for copy in copies:
        copy.start()
    rows_ref, ids_ref, gates_ref = targets
    for copy in copies[1:]:
        copy.wait()
    extra = table_width(experts)
    width = rows_ref.shape[1]
    gates = gates_ref[...]
    shares = 2.5 * gates / jnp.sum(gates, axis=1, keepdims=True)
    ids = ids_ref[...]
    lane = lax.broadcasted_iota(jnp.int32, (ids.shape[0], extra), 1)
    expert = jnp.where(lane < experts, lane, lane - experts)
    table = jnp.zeros(lane.shape, jnp.float32)
    for k in range(ids.shape[1]):
        table += jnp.where(expert == ids[:, k : k + 1], shares[:, k : k + 1], 0.0)
    high = table.astype(jnp.bfloat16).astype(jnp.float32)
    table = jnp.where(lane < experts, high, jnp.where(lane < 2 * experts, table - high, 0.0))
    out_ref[:, width:] = table.astype(jnp.bfloat16)
    copies[0].wait()
    out_ref[:, :width] = rows_ref[...]


def pack(experts, moe_rows, route_ids, route_gates):
    rows, width = moe_rows.shape
    sources = (moe_rows, route_ids, route_gates)
    return pl.pallas_call(
        functools.partial(pack_kernel, experts),
        in_specs=[pl.BlockSpec(memory_space=pltpu.HBM)] * 3,
        out_specs=pl.BlockSpec(memory_space=pltpu.VMEM),
        scratch_shapes=[pltpu.VMEM(source.shape, source.dtype) for source in sources]
        + [pltpu.SemaphoreType.DMA((3,))],
        out_shape=jax.ShapeDtypeStruct((rows, width + table_width(experts)), jnp.bfloat16),
        compiler_params=pltpu.CompilerParams(vmem_limit_bytes=4 * MEBI),
        name="pack",
    )(*[in_hbm(source) for source in sources])


def line_order(sizes):
    _, middle, _, local = sizes
    ways = [[], []]
    for m in range(middle):
        for n in range(local):
            ways[0].append((m, n))
            ways[1].append((n, m))
    return ways


def gathered_rows(arrays, order, size, columns):
    return [arrays[i][line * size : (line + 1) * size, columns] for i, line in order]


def fetch_both(gate_hbm, up_hbm, gate, up, gate_sem, up_sem, start, tile):
    copies = []
    for k in range(0, gate.shape[0], tile):
        inside, outside = pl.ds(k, tile), pl.ds(start + k, tile)
        pair = (
            pltpu.make_async_copy(gate_hbm.at[outside], gate.at[inside], gate_sem.at[k // tile]),
            pltpu.make_async_copy(up_hbm.at[outside], up.at[inside], up_sem.at[k // tile]),
        )
        for copy in pair:
            copy.start()
        copies.append(pair)
    return copies


def both_cores(arrays, way, sizes, columns):
    order = line_order(sizes)[way]
    arrays = arrays[way]
    count = len(arrays) // 2
    size = arrays[0].shape[0] // (1 + max(line for _, line in order))
    rows = gathered_rows(arrays[:count], order, size, columns)
    rows += gathered_rows(arrays[count:], order, size, columns)
    return jnp.concatenate(rows, axis=0)


def project(arrays, sizes, copies, gate, up, gate_sum, up_sum, tile, fresh):
    half = len(copies) // 2
    for k, pair in enumerate(copies):
        rows = both_cores(arrays, k // half, sizes, pl.ds(k % half * tile, tile))
        for copy, weight, total in zip(pair, (gate, up), (gate_sum, up_sum)):
            copy.wait()
            product = jnp.dot(
                rows, weight[pl.ds(k * tile, tile)], preferred_element_type=jnp.float32
            )
            if fresh and k == 0:
                total[...] = product
            else:
                total[...] += product


def by_way(refs, counts):
    return [refs[: counts[0]], refs[counts[0] : sum(counts)]]


def first_kernel(counts, sizes, tile, *refs):
    arrays, refs = by_way(refs, counts), refs[sum(counts) :]
    gate_hbm, up_hbm, gate_sum, up_sum, gate, up, gate_sem, up_sem = refs
    copies = fetch_both(gate_hbm, up_hbm, gate, up, gate_sem, up_sem, 0, tile)
    project(arrays, sizes, copies, gate, up, gate_sum, up_sum, tile, True)


def first_sums(arrays, sizes, rows, w_gate, w_up):
    units = w_gate.shape[1]
    columns = sum(way[0].shape[1] for way in arrays)
    tile = 1024
    counts = tuple(len(way) for way in arrays)
    return pl.pallas_call(
        functools.partial(first_kernel, counts, sizes, tile),
        in_specs=[pl.BlockSpec(memory_space=pltpu.VMEM)] * sum(counts)
        + [pl.BlockSpec(memory_space=pltpu.HBM)] * 2,
        out_specs=[pl.BlockSpec(memory_space=pltpu.VMEM)] * 2,
        out_shape=[jax.ShapeDtypeStruct((rows, units), jnp.float32)] * 2,
        scratch_shapes=[pltpu.VMEM((columns, units), jnp.bfloat16)] * 2
        + [pltpu.SemaphoreType.DMA((columns // tile,))] * 2,
        cost_estimate=pl.CostEstimate(
            flops=4 * rows * columns * units,
            bytes_accessed=4 * columns * units,
            transcendentals=0,
        ),
        compiler_params=pltpu.CompilerParams(vmem_limit_bytes=20 * MEBI),
        name="first_sums",
    )(*arrays[0], *arrays[1], in_hbm(w_gate), in_hbm(w_up))


def expert_kernel(counts, sizes, experts, tile, node_ref, *refs):
    arrays, refs = by_way(refs, counts), refs[sum(counts) :]
    gate_in, up_in, gate_hbm, up_hbm, down_hbm = refs[:5]
    outs = refs[5:-10]
    hidden_ref, share_ref, gate, up, down, gate_sum, up_sum, gate_sem, up_sem, down_sem = refs[-10:]
    start = gate_hbm.shape[0] - gate.shape[0]
    copies = fetch_both(gate_hbm, up_hbm, gate, up, gate_sem, up_sem, start, tile)
    quarters = down_sem.shape[0]
    quarter = down.shape[1] // quarters
    down_copies = []
    for k in range(quarters):
        part = pl.ds(k * quarter, quarter)
        down_copies.append(
            pltpu.make_async_copy(down_hbm.at[:, part], down.at[:, part], down_sem.at[k])
        )
        down_copies[-1].start()

    width = gate.shape[0] // 2
    behind = pl.ds(width, arrays[1][0].shape[1] - width)
    table = both_cores(arrays, 1, sizes, behind).astype(jnp.float32)
    lane = lax.broadcasted_iota(jnp.int32, table.shape, 1)
    mine = (lane == node_ref[0]) | (lane == node_ref[0] + experts)
    share = jnp.sum(jnp.where(mine, table, 0.0), axis=1, keepdims=True)
    share_ref[...] = jnp.broadcast_to(share, share_ref.shape)
    gate_sum[...] = gate_in[...]
    up_sum[...] = up_in[...]
    project(arrays, sizes, copies, gate, up, gate_sum, up_sum, tile, False)
    hidden_ref[...] = (jax.nn.silu(gate_sum[...]) * up_sum[...]).astype(jnp.bfloat16)
    for k, copy in enumerate(down_copies):
        copy.wait()
        order = line_order(sizes)[k % 2]
        each = 2 + max(i for i, _ in order)
        group, outs = outs[:each], outs[each:]
        size = hidden_ref.shape[0] // (2 * len(order))
        for piece in range(0, quarter, quarter // 2):
            part = pl.ds(k * quarter + piece, quarter // 2)
            product = jnp.dot(hidden_ref[...], down[:, part], preferred_element_type=jnp.float32)
            product = (product * share_ref[:, :1]).astype(jnp.bfloat16)
            columns = pl.ds(piece, quarter // 2)
            for i, line in order:
                row = order.index((i, line)) * size
                group[i][line * size : (line + 1) * size, columns] = product[row : row + size]
                row += len(order) * size
                lines = 1 + max(line for _, line in order)
                place = ((i - 1) % (each - 1)) * lines + line
                group[-1][place * size : (place + 1) * size, columns] = product[row : row + size]


def expert(arrays, sizes, rows, sums, w_gate, w_up, w_down, experts, node):
    units, columns = w_down.shape
    tail = sum(way[0].shape[1] for way in arrays) - table_width(experts)
    tile = 512
    counts = tuple(len(way) for way in arrays)
    out_shapes = []
    for k in range(4):
        places = (sizes[MIDDLE], sizes[LOCAL])[k % 2]
        size = rows // 2 // places
        out_shapes += [(size, columns // 4)] * places + [(rows // 2, columns // 4)]
    return pl.pallas_call(
        functools.partial(expert_kernel, counts, sizes, experts, tile),
        in_specs=[pl.BlockSpec(memory_space=pltpu.SMEM)]
        + [pl.BlockSpec(memory_space=pltpu.VMEM)] * (sum(counts) + 2)
        + [pl.BlockSpec(memory_space=pltpu.HBM)] * 3,
        out_specs=[pl.BlockSpec(memory_space=pltpu.VMEM)] * len(out_shapes),
        out_shape=[jax.ShapeDtypeStruct(shape, jnp.bfloat16) for shape in out_shapes],
        scratch_shapes=[
            pltpu.VMEM((rows, units), jnp.bfloat16),
            pltpu.VMEM((rows, 128), jnp.float32),
            pltpu.VMEM((tail, units), jnp.bfloat16),
            pltpu.VMEM((tail, units), jnp.bfloat16),
            pltpu.VMEM((units, columns), jnp.bfloat16),
            pltpu.VMEM((rows, units), jnp.float32),
            pltpu.VMEM((rows, units), jnp.float32),
            pltpu.SemaphoreType.DMA((tail // tile,)),
            pltpu.SemaphoreType.DMA((tail // tile,)),
            pltpu.SemaphoreType.DMA((4,)),
        ],
        cost_estimate=pl.CostEstimate(
            flops=4 * rows * tail * units + 2 * rows * columns * units,
            bytes_accessed=4 * tail * units + 2 * units * columns,
            transcendentals=rows * units,
        ),
        compiler_params=pltpu.CompilerParams(vmem_limit_bytes=24 * MEBI),
        name="expert",
    )(node, *arrays[0], *arrays[1], *sums, in_hbm(w_gate), in_hbm(w_up), in_hbm(w_down))


def body(
    moe_rows,
    route_ids,
    route_gates,
    w_gate,
    w_up,
    w_down,
    query_latent,
    query_rope,
    cache_latent,
    cache_rope,
    cache_lengths,
):
    grid = Grid()
    high, middle, cores, _ = grid.sizes
    experts = high * middle * cores
    tokens, width = moe_rows.shape
    node = lax.axis_index(("high", "middle", "core")).astype(jnp.int32).reshape(1)
    split = width * 4 // 7
    tied = lax.optimization_barrier
    attn_latent = attention(query_latent, query_rope, cache_latent, cache_rope, cache_lengths)

    line = pack(experts, moe_rows, route_ids, route_gates)
    for m in grid.masks[:-1]:
        came = grid.swap(line, HIGH, m)
        came, attn_latent = tied((came, attn_latent))
        line = join([line, came])
    came = grid.swap(line, HIGH, grid.masks[-1])
    half, rest = split // 2, (width - split) // 2
    last = line.shape[1] - split - rest
    ways = join(
        [line, came],
        [(0, half), (split, rest)],
        [(half, half), (split + rest, last)],
    )
    ways = [grid.over(ways[0], LOCAL), grid.over(ways[1], MIDDLE)]
    ways = [join(ways[0], [(0, half)], [(half, rest)]), join(ways[1], [(0, half)], [(half, last)])]
    head = [grid.over(ways[0][0], MIDDLE), grid.over(ways[1][0], LOCAL)]
    tail = [grid.over(ways[0][1], MIDDLE), grid.over(ways[1][1], LOCAL)]

    def with_other_core(ways):
        return [way + [grid.swap(block, CORE, 1) for block in way] for way in ways]

    head = with_other_core(head)
    rows = 2 * grid.sizes[MIDDLE] * grid.sizes[LOCAL] * high * tokens
    sums = first_sums(head, grid.sizes, rows, w_gate[0], w_up[0])
    tail, sums = tied((tail, sums))
    tail = with_other_core(tail)
    products = expert(
        tail, grid.sizes, rows, sums, w_gate[0], w_up[0], w_down[0], experts, node
    )

    digits = (MIDDLE, LOCAL)

    def core_sums(arrays):
        sums = []
        for way in range(2):
            places = grid.sizes[digits[way]]
            mine, other, arrays = arrays[:places], arrays[places], arrays[places + 1 :]
            other = grid.swap(other, CORE, 1)
            size = mine[0].shape[0]
            sums.append(
                [
                    add([mine[i], other[(i - 1) % places * size :][:size]])
                    for i in range(places)
                ]
            )
        return sums

    def second_axis(ways):
        return [grid.receive(ways[way], digits[way]) for way in range(2)]

    def line_of(ways):
        return jnp.concatenate([add(way) for way in ways], axis=1)

    head, tail = products[: len(products) // 2], products[len(products) // 2 :]
    tail, head = tied((tail, core_sums(head)))
    head, tail = second_axis(head), second_axis(core_sums(tail))
    head, tail = tied((head, tail))
    ways = [
        grid.receive_rows(
            jnp.concatenate([add(head[way]), add(tail[way])], axis=1), digits[1 - way]
        )
        for way in range(2)
    ]
    line = line_of(tied(ways))
    for m in grid.masks[::-1]:
        line = add(grid.receive_half(line, m))
    quarter = width // 4
    order = (0, 2, 1, 3)
    moe_out = jnp.concatenate([line[:, i * quarter : (i + 1) * quarter] for i in order], axis=1)
    return (moe_out, attn_latent)


def solution(mesh):
    groups, nodes, local = mesh.devices.shape
    split = Mesh(mesh.devices.reshape(groups, nodes // 4, 2, 2, local), ("group",) + everyone)
    node = ("high", "middle", "core")
    whole = ("group",) + everyone
    rows = P(whole, None)
    blocks = P(whole, None, None)
    return jax.shard_map(
        body,
        mesh=split,
        in_specs=(
            rows,
            rows,
            rows,
            P(node, None, "local"),
            P(node, None, "local"),
            P(node, "local", None),
            blocks,
            blocks,
            blocks,
            blocks,
            P(whole),
        ),
        out_specs=(rows, blocks),
        check_vma=False,
    )
```

```python
import functools

import jax
import jax.numpy as jnp
import numpy as np
from jax import lax
from jax.experimental import pallas as pl
from jax.experimental.pallas import tpu as pltpu
from jax.sharding import Mesh
from jax.sharding import PartitionSpec as P

score_scale = 192.0 ** (-0.5)
everyone = ("high", "middle", "core", "local")
MEBI = 1024 * 1024


def attention_kernel(lengths_ref, *refs):
    sources, (out_ref, *targets), sems = refs[:4], refs[4:-1], refs[-1]
    query_ref, query_rope_ref, cache_ref, cache_rope_ref = targets
    copies = []
    for row in range(out_ref.shape[0]):
        copies.append(
            [
                pltpu.make_async_copy(source.at[row], target.at[row], sems.at[row, i])
                for i, (source, target) in enumerate(zip(sources, targets))
            ]
        )
        for copy in copies[-1]:
            copy.start()
    for row in range(out_ref.shape[0]):
        for copy in copies[row]:
            copy.wait()
        cache = cache_ref[row]
        scores = lax.dot_general(
            query_ref[row], cache, (((1,), (1,)), ((), ())), preferred_element_type=jnp.float32
        )
        scores += jnp.dot(
            query_rope_ref[row], cache_rope_ref[row], preferred_element_type=jnp.float32
        )
        slot = lax.broadcasted_iota(jnp.int32, scores.shape, 1)
        in_range = slot < lengths_ref[row]
        scores = jnp.where(in_range, scores * score_scale, -jnp.inf)
        row_peak = jnp.max(scores, axis=1, keepdims=True)
        lifted = jnp.where(in_range, jnp.exp(scores - row_peak), 0.0)
        weights = (lifted / jnp.sum(lifted, axis=1, keepdims=True)).astype(jnp.bfloat16)
        value = jnp.dot(weights, cache, preferred_element_type=jnp.float32)
        out_ref[row] = value.astype(jnp.bfloat16)


def attention(query_latent, query_rope, cache_latent, cache_rope, cache_lengths):
    rows, heads, latent = query_latent.shape
    slots = cache_latent.shape[1]
    sources = (query_latent, query_rope, cache_latent, cache_rope)
    return pl.pallas_call(
        attention_kernel,
        in_specs=[pl.BlockSpec(memory_space=pltpu.SMEM)]
        + [pl.BlockSpec(memory_space=pltpu.HBM)] * 4,
        out_specs=pl.BlockSpec(memory_space=pltpu.VMEM),
        out_shape=jax.ShapeDtypeStruct(query_latent.shape, jnp.bfloat16),
        scratch_shapes=[pltpu.VMEM(source.shape, source.dtype) for source in sources]
        + [pltpu.SemaphoreType.DMA((rows, 4))],
        cost_estimate=pl.CostEstimate(
            flops=4 * rows * heads * slots * latent,
            bytes_accessed=2 * rows * slots * latent,
            transcendentals=rows * heads * slots,
        ),
        compiler_params=pltpu.CompilerParams(vmem_limit_bytes=8 * MEBI),
        name="attention",
    )(cache_lengths, *[in_hbm(source) for source in sources])


def in_hbm(array):
    return pltpu.with_memory_space_constraint(array, pltpu.HBM)


class Grid:
    def __init__(self):
        self.sizes = tuple(lax.axis_size(name) for name in everyone)
        self.mixed = self.sizes[1] == self.sizes[3]

    def swap(self, value, pick, mask):
        pairs = []
        for place in np.ndindex(*self.sizes):
            other = list(place)
            other[pick(place[2])] ^= mask
            pairs.append(
                (
                    int(np.ravel_multi_index(place, self.sizes)),
                    int(np.ravel_multi_index(other, self.sizes)),
                )
            )
        return lax.ppermute(value, everyone, pairs)

    def high(self, core):
        return 0

    def core(self, core):
        return 2

    def first(self, core):
        return 1 if self.mixed and core == 1 else 3

    def second(self, core):
        return 3 if self.mixed and core == 1 else 1

    def extent(self, pick):
        return self.sizes[pick(0)]

    def lines(self, rows):
        return [rows] + [self.swap(rows, self.high, m) for m in range(1, self.extent(self.high))]

    def near(self, line):
        return [line] + [self.swap(line, self.first, m) for m in range(1, self.extent(self.first))]

    def far(self, near):
        return [
            self.swap(block, self.second, m)
            for m in range(1, self.extent(self.second))
            for block in near
        ]

    def other(self, mine):
        return [self.swap(block, self.core, 1) for block in mine]

    def last_sum(self, mine, other):
        return add([mine[-1], self.swap(other[0], self.core, 1)])

    def rest_sums(self, mine, other):
        size = mine[0].shape[0]
        rest = self.swap(other[1], self.core, 1)
        return [
            add([part, rest[i * size : (i + 1) * size]]) for i, part in enumerate(mine[:-1])
        ]

    def back(self, sums, place):
        return self.swap(sums[place], self.second, place // self.extent(self.first))

    def line_sum(self, sums, last):
        wide = self.extent(self.first)
        near = [[part] for part in sums[:wide]]
        for place in range(wide, len(sums)):
            moved = last if place == len(sums) - 1 else self.back(sums, place)
            near[place % wide].append(moved)
        near = [add(parts) for parts in near]
        return add([near[0]] + [self.swap(near[m], self.first, m) for m in range(1, wide)])

    def high_sum(self, line):
        rows = line.shape[0] // self.extent(self.high)
        parts = [line[:rows]]
        for m in range(1, self.extent(self.high)):
            parts.append(self.swap(line[m * rows : (m + 1) * rows], self.high, m))
        return add(parts)


def add(parts):
    total = parts[0].astype(jnp.float32)
    for part in parts[1:]:
        total = total + part.astype(jnp.float32)
    return total.astype(parts[0].dtype)


def join_kernel(count, ranges, *refs):
    for out, parts in zip(refs[count:], ranges):
        start = 0
        for first, size in parts:
            columns = pl.ds(first, size)
            out[:, start : start + size] = jnp.concatenate(
                [ref[:, columns] for ref in refs[:count]], axis=0
            )
            start += size


def join(parts, *ranges):
    rows = sum(part.shape[0] for part in parts)
    ranges = ranges or ([(0, parts[0].shape[1])],)
    outs = pl.pallas_call(
        functools.partial(join_kernel, len(parts), ranges),
        in_specs=[pl.BlockSpec(memory_space=pltpu.VMEM)] * len(parts),
        out_specs=[pl.BlockSpec(memory_space=pltpu.VMEM)] * len(ranges),
        out_shape=[
            jax.ShapeDtypeStruct((rows, sum(size for _, size in columns)), parts[0].dtype)
            for columns in ranges
        ],
        compiler_params=pltpu.CompilerParams(vmem_limit_bytes=4 * MEBI),
        name="join",
    )(*parts)
    return outs if len(ranges) > 1 else outs[0]


def table_width(experts):
    return pl.cdiv(2 * experts, 128) * 128


def pack_kernel(experts, *refs):
    sources, (out_ref, *targets), sems = refs[:3], refs[3:-1], refs[-1]
    copies = [
        pltpu.make_async_copy(source, target, sems.at[i])
        for i, (source, target) in enumerate(zip(sources, targets))
    ]
    for copy in copies:
        copy.start()
    rows_ref, ids_ref, gates_ref = targets
    for copy in copies[1:]:
        copy.wait()
    extra = table_width(experts)
    width = rows_ref.shape[1]
    gates = gates_ref[...]
    shares = 2.5 * gates / jnp.sum(gates, axis=1, keepdims=True)
    ids = ids_ref[...]
    lane = lax.broadcasted_iota(jnp.int32, (ids.shape[0], extra), 1)
    expert = jnp.where(lane < experts, lane, lane - experts)
    table = jnp.zeros(lane.shape, jnp.float32)
    for k in range(ids.shape[1]):
        table += jnp.where(expert == ids[:, k : k + 1], shares[:, k : k + 1], 0.0)
    high = table.astype(jnp.bfloat16).astype(jnp.float32)
    table = jnp.where(lane < experts, high, jnp.where(lane < 2 * experts, table - high, 0.0))
    out_ref[:, width:] = table.astype(jnp.bfloat16)
    copies[0].wait()
    out_ref[:, :width] = rows_ref[...]


def pack(experts, moe_rows, route_ids, route_gates):
    rows, width = moe_rows.shape
    sources = (moe_rows, route_ids, route_gates)
    return pl.pallas_call(
        functools.partial(pack_kernel, experts),
        in_specs=[pl.BlockSpec(memory_space=pltpu.HBM)] * 3,
        out_specs=pl.BlockSpec(memory_space=pltpu.VMEM),
        scratch_shapes=[pltpu.VMEM(source.shape, source.dtype) for source in sources]
        + [pltpu.SemaphoreType.DMA((3,))],
        out_shape=jax.ShapeDtypeStruct((rows, width + table_width(experts)), jnp.bfloat16),
        compiler_params=pltpu.CompilerParams(vmem_limit_bytes=4 * MEBI),
        name="pack",
    )(*[in_hbm(source) for source in sources])


def spread(product, outs):
    start = 0
    for out, columns in outs:
        size = out.shape[0]
        out[:, columns] = product[start : start + size]
        start += size


def fetch(source, target, sems, start, tile, dim):
    copies = []
    for k in range(0, target.shape[dim], tile):
        inside, outside = pl.ds(k, tile), pl.ds(start + k, tile)
        if dim == 1:
            inside, outside = (slice(None), inside), (slice(None), outside)
        copy = pltpu.make_async_copy(source.at[outside], target.at[inside], sems.at[k // tile])
        copy.start()
        copies.append(copy)
    return copies


def fetch_both(gate_hbm, up_hbm, gate, up, gate_sem, up_sem, start, tile):
    copies = []
    for k in range(0, gate.shape[0], tile):
        inside, outside = pl.ds(k, tile), pl.ds(start + k, tile)
        pair = (
            pltpu.make_async_copy(gate_hbm.at[outside], gate.at[inside], gate_sem.at[k // tile]),
            pltpu.make_async_copy(up_hbm.at[outside], up.at[inside], up_sem.at[k // tile]),
        )
        for copy in pair:
            copy.start()
        copies.append(pair)
    return copies


def project(blocks, copies, gate, up, gate_sum, up_sum, tile, fresh):
    for k, pair in enumerate(copies):
        part = pl.ds(k * tile, tile)
        rows = jnp.concatenate([block[:, part] for block in blocks], axis=0)
        for copy, weight, total in zip(pair, (gate, up), (gate_sum, up_sum)):
            copy.wait()
            product = jnp.dot(rows, weight[part], preferred_element_type=jnp.float32)
            if fresh and k == 0:
                total[...] = product
            else:
                total[...] += product


def first_kernel(count, tile, *refs):
    blocks = refs[:count]
    gate_hbm, up_hbm, gate_sum, up_sum, gate, up, gate_sem, up_sem = refs[count:]
    copies = fetch_both(gate_hbm, up_hbm, gate, up, gate_sem, up_sem, 0, tile)
    project(blocks, copies, gate, up, gate_sum, up_sum, tile, True)


def first_sums(blocks, w_gate, w_up):
    units = w_gate.shape[1]
    rows = sum(block.shape[0] for block in blocks)
    columns = blocks[0].shape[1]
    tile = 1024
    return pl.pallas_call(
        functools.partial(first_kernel, len(blocks), tile),
        in_specs=[pl.BlockSpec(memory_space=pltpu.VMEM)] * len(blocks)
        + [pl.BlockSpec(memory_space=pltpu.HBM)] * 2,
        out_specs=[pl.BlockSpec(memory_space=pltpu.VMEM)] * 2,
        out_shape=[jax.ShapeDtypeStruct((rows, units), jnp.float32)] * 2,
        scratch_shapes=[pltpu.VMEM((columns, units), jnp.bfloat16)] * 2
        + [pltpu.SemaphoreType.DMA((columns // tile,))] * 2,
        cost_estimate=pl.CostEstimate(
            flops=4 * rows * columns * units,
            bytes_accessed=4 * columns * units,
            transcendentals=0,
        ),
        compiler_params=pltpu.CompilerParams(vmem_limit_bytes=20 * MEBI),
        name="first_sums",
    )(*blocks, in_hbm(w_gate), in_hbm(w_up))


def expert_kernel(count, experts, tile, down_tile, split, node_ref, *refs):
    blocks = refs[:count]
    gate_in, up_in, gate_hbm, up_hbm, down_hbm = refs[count : count + 5]
    outs = refs[count + 5 : -10]
    hidden_ref, share_ref, gate, up, down, gate_sum, up_sum, gate_sem, up_sem, down_sem = refs[-10:]
    start = gate_hbm.shape[0] - gate.shape[0]
    copies = fetch_both(gate_hbm, up_hbm, gate, up, gate_sem, up_sem, start, tile)
    down_copies = fetch(down_hbm, down, down_sem, 0, 2 * down_tile, 1)

    table = jnp.concatenate([block[:, gate.shape[0] :] for block in blocks], axis=0)
    table = table.astype(jnp.float32)
    lane = lax.broadcasted_iota(jnp.int32, table.shape, 1)
    mine = (lane == node_ref[0]) | (lane == node_ref[0] + experts)
    share = jnp.sum(jnp.where(mine, table, 0.0), axis=1, keepdims=True)
    share_ref[...] = jnp.broadcast_to(share, share_ref.shape)
    gate_sum[...] = gate_in[...]
    up_sum[...] = up_in[...]
    project(blocks, copies, gate, up, gate_sum, up_sum, tile, False)
    hidden_ref[...] = (jax.nn.silu(gate_sum[...]) * up_sum[...]).astype(jnp.bfloat16)
    for k in range(0, down.shape[1], down_tile):
        if k % (2 * down_tile) == 0:
            down_copies[k // (2 * down_tile)].wait()
        product = jnp.dot(
            hidden_ref[...], down[:, pl.ds(k, down_tile)], preferred_element_type=jnp.float32
        )
        product = (product * share_ref[:, :1]).astype(jnp.bfloat16)
        if k < split:
            spread(product, [(out, pl.ds(k, down_tile)) for out in outs[: len(outs) // 2]])
        else:
            spread(product, [(out, pl.ds(k - split, down_tile)) for out in outs[len(outs) // 2 :]])


def expert(blocks, sums, w_gate, w_up, w_down, experts, node, sizes, split):
    units, columns = w_down.shape
    rows = sum(sizes)
    tail = blocks[0].shape[1] - table_width(experts)
    tile, down_tile = 1024, 512
    return pl.pallas_call(
        functools.partial(expert_kernel, len(blocks), experts, tile, down_tile, split),
        in_specs=[pl.BlockSpec(memory_space=pltpu.SMEM)]
        + [pl.BlockSpec(memory_space=pltpu.VMEM)] * (len(blocks) + 2)
        + [pl.BlockSpec(memory_space=pltpu.HBM)] * 3,
        out_specs=[pl.BlockSpec(memory_space=pltpu.VMEM)] * (2 * len(sizes)),
        out_shape=[
            jax.ShapeDtypeStruct((size, chunk), jnp.bfloat16)
            for chunk in (split, columns - split)
            for size in sizes
        ],
        scratch_shapes=[
            pltpu.VMEM((rows, units), jnp.bfloat16),
            pltpu.VMEM((rows, 128), jnp.float32),
            pltpu.VMEM((tail, units), jnp.bfloat16),
            pltpu.VMEM((tail, units), jnp.bfloat16),
            pltpu.VMEM((units, columns), jnp.bfloat16),
            pltpu.VMEM((rows, units), jnp.float32),
            pltpu.VMEM((rows, units), jnp.float32),
            pltpu.SemaphoreType.DMA((tail // tile,)),
            pltpu.SemaphoreType.DMA((tail // tile,)),
            pltpu.SemaphoreType.DMA((columns // (2 * down_tile),)),
        ],
        cost_estimate=pl.CostEstimate(
            flops=4 * rows * tail * units + 2 * rows * columns * units,
            bytes_accessed=4 * tail * units + 2 * units * columns,
            transcendentals=rows * units,
        ),
        compiler_params=pltpu.CompilerParams(vmem_limit_bytes=24 * MEBI),
        name="expert",
    )(node, *blocks, *sums, in_hbm(w_gate), in_hbm(w_up), in_hbm(w_down))


def body(
    moe_rows,
    route_ids,
    route_gates,
    w_gate,
    w_up,
    w_down,
    query_latent,
    query_rope,
    cache_latent,
    cache_rope,
    cache_lengths,
):
    grid = Grid()
    high, middle, cores, _ = grid.sizes
    experts = high * middle * cores
    tokens, width = moe_rows.shape
    node = lax.axis_index(("high", "middle", "core")).astype(jnp.int32).reshape(1)
    split = width * 4 // 7
    tied = lax.optimization_barrier
    attn_latent = attention(query_latent, query_rope, cache_latent, cache_rope, cache_lengths)

    lines = grid.lines(pack(experts, moe_rows, route_ids, route_gates))
    lines[-1], attn_latent = tied((lines[-1], attn_latent))
    total = lines[0].shape[1]
    head, tail = join(lines, [(0, split)], [(split, total - split)])
    head, tail = grid.near(head), grid.near(tail)
    far = grid.far(head)
    far[-1], tail[-1] = tied((far[-1], tail[-1]))
    head, tail = head + far, tail + grid.far(tail)
    other = grid.other(head)
    sums = first_sums(head + other[-1:] + other[:-1], w_gate[0], w_up[0])
    tail[-1], sums = tied((tail[-1], sums))
    other = grid.other(tail)
    size, count = high * tokens, len(tail)
    sizes = [size] * count + [size, size * (count - 1)]
    products = expert(
        tail + other[-1:] + other[:-1],
        sums,
        w_gate[0],
        w_up[0],
        w_down[0],
        experts,
        node,
        sizes,
        split,
    )

    def returned(parts):
        mine, other = parts[:count], parts[count:]
        last = grid.last_sum(mine, other)
        sums = grid.rest_sums(mine, other) + [last]
        return grid.high_sum(grid.line_sum(sums, grid.back(sums, count - 1)))

    head, tail = returned(products[: len(sizes)]), returned(products[len(sizes) :])
    return (jnp.concatenate([head, tail], axis=1), attn_latent)


def solution(mesh):
    groups, nodes, local = mesh.devices.shape
    split = Mesh(mesh.devices.reshape(groups, nodes // 4, 2, 2, local), ("group",) + everyone)
    node = ("high", "middle", "core")
    whole = ("group",) + everyone
    rows = P(whole, None)
    blocks = P(whole, None, None)
    return jax.shard_map(
        body,
        mesh=split,
        in_specs=(
            rows,
            rows,
            rows,
            P(node, None, "local"),
            P(node, None, "local"),
            P(node, "local", None),
            blocks,
            blocks,
            blocks,
            blocks,
            P(whole),
        ),
        out_specs=(rows, blocks),
        check_vma=False,
    )
```

```python
import functools

import jax
import jax.numpy as jnp
import numpy as np
from jax import lax
from jax.experimental import pallas as pl
from jax.experimental.pallas import tpu as pltpu
from jax.sharding import Mesh
from jax.sharding import PartitionSpec as P

score_scale = 192.0 ** (-0.5)
everyone = ("high", "middle", "core", "local")
MEBI = 1024 * 1024


def attention_kernel(lengths_ref, *refs):
    sources, (out_ref, *targets), sems = refs[:4], refs[4:-1], refs[-1]
    query_ref, query_rope_ref, cache_ref, cache_rope_ref = targets
    copies = []
    for row in range(out_ref.shape[0]):
        copies.append(
            [
                pltpu.make_async_copy(source.at[row], target.at[row], sems.at[row, i])
                for i, (source, target) in enumerate(zip(sources, targets))
            ]
        )
        for copy in copies[-1]:
            copy.start()
    for row in range(out_ref.shape[0]):
        for copy in copies[row]:
            copy.wait()
        cache = cache_ref[row]
        scores = lax.dot_general(
            query_ref[row], cache, (((1,), (1,)), ((), ())), preferred_element_type=jnp.float32
        )
        scores += jnp.dot(
            query_rope_ref[row], cache_rope_ref[row], preferred_element_type=jnp.float32
        )
        slot = lax.broadcasted_iota(jnp.int32, scores.shape, 1)
        in_range = slot < lengths_ref[row]
        scores = jnp.where(in_range, scores * score_scale, -jnp.inf)
        row_peak = jnp.max(scores, axis=1, keepdims=True)
        lifted = jnp.where(in_range, jnp.exp(scores - row_peak), 0.0)
        weights = (lifted / jnp.sum(lifted, axis=1, keepdims=True)).astype(jnp.bfloat16)
        value = jnp.dot(weights, cache, preferred_element_type=jnp.float32)
        out_ref[row] = value.astype(jnp.bfloat16)


def attention(query_latent, query_rope, cache_latent, cache_rope, cache_lengths):
    rows, heads, latent = query_latent.shape
    slots = cache_latent.shape[1]
    sources = (query_latent, query_rope, cache_latent, cache_rope)
    return pl.pallas_call(
        attention_kernel,
        in_specs=[pl.BlockSpec(memory_space=pltpu.SMEM)]
        + [pl.BlockSpec(memory_space=pltpu.HBM)] * 4,
        out_specs=pl.BlockSpec(memory_space=pltpu.VMEM),
        out_shape=jax.ShapeDtypeStruct(query_latent.shape, jnp.bfloat16),
        scratch_shapes=[pltpu.VMEM(source.shape, source.dtype) for source in sources]
        + [pltpu.SemaphoreType.DMA((rows, 4))],
        cost_estimate=pl.CostEstimate(
            flops=4 * rows * heads * slots * latent,
            bytes_accessed=2 * rows * slots * latent,
            transcendentals=rows * heads * slots,
        ),
        compiler_params=pltpu.CompilerParams(vmem_limit_bytes=8 * MEBI),
        name="attention",
    )(cache_lengths, *[in_hbm(source) for source in sources])


def in_hbm(array):
    return pltpu.with_memory_space_constraint(array, pltpu.HBM)


class Grid:
    def __init__(self):
        self.sizes = tuple(lax.axis_size(name) for name in everyone)
        self.mixed = self.sizes[1] == self.sizes[3]

    def swap(self, value, pick, mask):
        pairs = []
        for place in np.ndindex(*self.sizes):
            other = list(place)
            other[pick(place[2])] ^= mask
            pairs.append(
                (
                    int(np.ravel_multi_index(place, self.sizes)),
                    int(np.ravel_multi_index(other, self.sizes)),
                )
            )
        return lax.ppermute(value, everyone, pairs)

    def high(self, core):
        return 0

    def core(self, core):
        return 2

    def first(self, core):
        return 1 if self.mixed and core == 1 else 3

    def second(self, core):
        return 3 if self.mixed and core == 1 else 1

    def extent(self, pick):
        return self.sizes[pick(0)]

    def masks(self):
        masks, m = [], self.extent(self.high) // 2
        while m:
            masks.append(m)
            m //= 2
        return masks

    def lines(self, rows, masks):
        if not masks:
            return [rows]
        came = self.swap(rows, self.high, masks[0])
        return self.lines(rows, masks[1:]) + self.lines(came, masks[1:])

    def line_parts(self, parts, masks):
        if not masks:
            return parts
        half = len(parts) // 2
        far = add(self.line_parts(parts[half:], masks[1:]))
        return self.line_parts(parts[:half], masks[1:]) + [self.swap(far, self.high, masks[0])]

    def near(self, line):
        return [line] + [self.swap(line, self.first, m) for m in range(1, self.extent(self.first))]

    def far(self, near):
        return [
            self.swap(block, self.second, m)
            for m in range(1, self.extent(self.second))
            for block in near
        ]

    def other(self, mine):
        return [self.swap(block, self.core, 1) for block in mine]

    def last_sum(self, mine, other):
        return add([mine[-1], self.swap(other[0], self.core, 1)])

    def rest_sums(self, mine, other):
        size = mine[0].shape[0]
        rest = self.swap(other[1], self.core, 1)
        return [
            add([part, rest[i * size : (i + 1) * size]]) for i, part in enumerate(mine[:-1])
        ]

    def back(self, sums, place):
        return self.swap(sums[place], self.second, place // self.extent(self.first))

    def line_sum(self, sums, last):
        wide = self.extent(self.first)
        near = [[part] for part in sums[:wide]]
        for place in range(wide, len(sums)):
            moved = last if place == len(sums) - 1 else self.back(sums, place)
            near[place % wide].append(moved)
        near = [add(parts) for parts in near]
        return add([near[0]] + [self.swap(near[m], self.first, m) for m in range(1, wide)])

    def high_sum(self, line):
        size = self.extent(self.high)
        rows = line.shape[0] // size
        parts = [line[i * rows : (i + 1) * rows] for i in range(size)]
        return add(self.line_parts(parts, self.masks()))


def add(parts):
    total = parts[0].astype(jnp.float32)
    for part in parts[1:]:
        total = total + part.astype(jnp.float32)
    return total.astype(parts[0].dtype)


def join_kernel(count, ranges, *refs):
    for out, parts in zip(refs[count:], ranges):
        start = 0
        for first, size in parts:
            columns = pl.ds(first, size)
            out[:, start : start + size] = jnp.concatenate(
                [ref[:, columns] for ref in refs[:count]], axis=0
            )
            start += size


def join(parts, *ranges):
    rows = sum(part.shape[0] for part in parts)
    ranges = ranges or ([(0, parts[0].shape[1])],)
    outs = pl.pallas_call(
        functools.partial(join_kernel, len(parts), ranges),
        in_specs=[pl.BlockSpec(memory_space=pltpu.VMEM)] * len(parts),
        out_specs=[pl.BlockSpec(memory_space=pltpu.VMEM)] * len(ranges),
        out_shape=[
            jax.ShapeDtypeStruct((rows, sum(size for _, size in columns)), parts[0].dtype)
            for columns in ranges
        ],
        compiler_params=pltpu.CompilerParams(vmem_limit_bytes=4 * MEBI),
        name="join",
    )(*parts)
    return outs if len(ranges) > 1 else outs[0]


def table_width(experts):
    return pl.cdiv(2 * experts, 128) * 128


def pack_kernel(experts, *refs):
    sources, (out_ref, *targets), sems = refs[:3], refs[3:-1], refs[-1]
    copies = [
        pltpu.make_async_copy(source, target, sems.at[i])
        for i, (source, target) in enumerate(zip(sources, targets))
    ]
    for copy in copies:
        copy.start()
    rows_ref, ids_ref, gates_ref = targets
    for copy in copies[1:]:
        copy.wait()
    extra = table_width(experts)
    width = rows_ref.shape[1]
    gates = gates_ref[...]
    shares = 2.5 * gates / jnp.sum(gates, axis=1, keepdims=True)
    ids = ids_ref[...]
    lane = lax.broadcasted_iota(jnp.int32, (ids.shape[0], extra), 1)
    expert = jnp.where(lane < experts, lane, lane - experts)
    table = jnp.zeros(lane.shape, jnp.float32)
    for k in range(ids.shape[1]):
        table += jnp.where(expert == ids[:, k : k + 1], shares[:, k : k + 1], 0.0)
    high = table.astype(jnp.bfloat16).astype(jnp.float32)
    table = jnp.where(lane < experts, high, jnp.where(lane < 2 * experts, table - high, 0.0))
    out_ref[:, width:] = table.astype(jnp.bfloat16)
    copies[0].wait()
    out_ref[:, :width] = rows_ref[...]


def pack(experts, moe_rows, route_ids, route_gates):
    rows, width = moe_rows.shape
    sources = (moe_rows, route_ids, route_gates)
    return pl.pallas_call(
        functools.partial(pack_kernel, experts),
        in_specs=[pl.BlockSpec(memory_space=pltpu.HBM)] * 3,
        out_specs=pl.BlockSpec(memory_space=pltpu.VMEM),
        scratch_shapes=[pltpu.VMEM(source.shape, source.dtype) for source in sources]
        + [pltpu.SemaphoreType.DMA((3,))],
        out_shape=jax.ShapeDtypeStruct((rows, width + table_width(experts)), jnp.bfloat16),
        compiler_params=pltpu.CompilerParams(vmem_limit_bytes=4 * MEBI),
        name="pack",
    )(*[in_hbm(source) for source in sources])


def spread(product, outs):
    start = 0
    for out, columns in outs:
        size = out.shape[0]
        out[:, columns] = product[start : start + size]
        start += size


def fetch(source, target, sems, start, tile, dim):
    copies = []
    for k in range(0, target.shape[dim], tile):
        inside, outside = pl.ds(k, tile), pl.ds(start + k, tile)
        if dim == 1:
            inside, outside = (slice(None), inside), (slice(None), outside)
        copy = pltpu.make_async_copy(source.at[outside], target.at[inside], sems.at[k // tile])
        copy.start()
        copies.append(copy)
    return copies


def fetch_both(gate_hbm, up_hbm, gate, up, gate_sem, up_sem, start, tile):
    copies = []
    for k in range(0, gate.shape[0], tile):
        inside, outside = pl.ds(k, tile), pl.ds(start + k, tile)
        pair = (
            pltpu.make_async_copy(gate_hbm.at[outside], gate.at[inside], gate_sem.at[k // tile]),
            pltpu.make_async_copy(up_hbm.at[outside], up.at[inside], up_sem.at[k // tile]),
        )
        for copy in pair:
            copy.start()
        copies.append(pair)
    return copies


def project(blocks, copies, gate, up, gate_sum, up_sum, tile, fresh):
    for k, pair in enumerate(copies):
        part = pl.ds(k * tile, tile)
        rows = jnp.concatenate([block[:, part] for block in blocks], axis=0)
        for copy, weight, total in zip(pair, (gate, up), (gate_sum, up_sum)):
            copy.wait()
            product = jnp.dot(rows, weight[part], preferred_element_type=jnp.float32)
            if fresh and k == 0:
                total[...] = product
            else:
                total[...] += product


def first_kernel(count, tile, *refs):
    blocks = refs[:count]
    gate_hbm, up_hbm, gate_sum, up_sum, gate, up, gate_sem, up_sem = refs[count:]
    copies = fetch_both(gate_hbm, up_hbm, gate, up, gate_sem, up_sem, 0, tile)
    project(blocks, copies, gate, up, gate_sum, up_sum, tile, True)


def first_sums(blocks, w_gate, w_up):
    units = w_gate.shape[1]
    rows = sum(block.shape[0] for block in blocks)
    columns = blocks[0].shape[1]
    tile = 1024
    return pl.pallas_call(
        functools.partial(first_kernel, len(blocks), tile),
        in_specs=[pl.BlockSpec(memory_space=pltpu.VMEM)] * len(blocks)
        + [pl.BlockSpec(memory_space=pltpu.HBM)] * 2,
        out_specs=[pl.BlockSpec(memory_space=pltpu.VMEM)] * 2,
        out_shape=[jax.ShapeDtypeStruct((rows, units), jnp.float32)] * 2,
        scratch_shapes=[pltpu.VMEM((columns, units), jnp.bfloat16)] * 2
        + [pltpu.SemaphoreType.DMA((columns // tile,))] * 2,
        cost_estimate=pl.CostEstimate(
            flops=4 * rows * columns * units,
            bytes_accessed=4 * columns * units,
            transcendentals=0,
        ),
        compiler_params=pltpu.CompilerParams(vmem_limit_bytes=20 * MEBI),
        name="first_sums",
    )(*blocks, in_hbm(w_gate), in_hbm(w_up))


def expert_kernel(count, experts, tile, down_tile, split, node_ref, *refs):
    blocks = refs[:count]
    gate_in, up_in, gate_hbm, up_hbm, down_hbm = refs[count : count + 5]
    outs = refs[count + 5 : -10]
    hidden_ref, share_ref, gate, up, down, gate_sum, up_sum, gate_sem, up_sem, down_sem = refs[-10:]
    start = gate_hbm.shape[0] - gate.shape[0]
    copies = fetch_both(gate_hbm, up_hbm, gate, up, gate_sem, up_sem, start, tile)
    down_copies = fetch(down_hbm, down, down_sem, 0, 2 * down_tile, 1)

    table = jnp.concatenate([block[:, gate.shape[0] :] for block in blocks], axis=0)
    table = table.astype(jnp.float32)
    lane = lax.broadcasted_iota(jnp.int32, table.shape, 1)
    mine = (lane == node_ref[0]) | (lane == node_ref[0] + experts)
    share = jnp.sum(jnp.where(mine, table, 0.0), axis=1, keepdims=True)
    share_ref[...] = jnp.broadcast_to(share, share_ref.shape)
    gate_sum[...] = gate_in[...]
    up_sum[...] = up_in[...]
    project(blocks, copies, gate, up, gate_sum, up_sum, tile, False)
    hidden_ref[...] = (jax.nn.silu(gate_sum[...]) * up_sum[...]).astype(jnp.bfloat16)
    for k in range(0, down.shape[1], down_tile):
        if k % (2 * down_tile) == 0:
            down_copies[k // (2 * down_tile)].wait()
        product = jnp.dot(
            hidden_ref[...], down[:, pl.ds(k, down_tile)], preferred_element_type=jnp.float32
        )
        product = (product * share_ref[:, :1]).astype(jnp.bfloat16)
        if k < split:
            spread(product, [(out, pl.ds(k, down_tile)) for out in outs[: len(outs) // 2]])
        else:
            spread(product, [(out, pl.ds(k - split, down_tile)) for out in outs[len(outs) // 2 :]])


def expert(blocks, sums, w_gate, w_up, w_down, experts, node, sizes, split):
    units, columns = w_down.shape
    rows = sum(sizes)
    tail = blocks[0].shape[1] - table_width(experts)
    tile, down_tile = 1024, 512
    return pl.pallas_call(
        functools.partial(expert_kernel, len(blocks), experts, tile, down_tile, split),
        in_specs=[pl.BlockSpec(memory_space=pltpu.SMEM)]
        + [pl.BlockSpec(memory_space=pltpu.VMEM)] * (len(blocks) + 2)
        + [pl.BlockSpec(memory_space=pltpu.HBM)] * 3,
        out_specs=[pl.BlockSpec(memory_space=pltpu.VMEM)] * (2 * len(sizes)),
        out_shape=[
            jax.ShapeDtypeStruct((size, chunk), jnp.bfloat16)
            for chunk in (split, columns - split)
            for size in sizes
        ],
        scratch_shapes=[
            pltpu.VMEM((rows, units), jnp.bfloat16),
            pltpu.VMEM((rows, 128), jnp.float32),
            pltpu.VMEM((tail, units), jnp.bfloat16),
            pltpu.VMEM((tail, units), jnp.bfloat16),
            pltpu.VMEM((units, columns), jnp.bfloat16),
            pltpu.VMEM((rows, units), jnp.float32),
            pltpu.VMEM((rows, units), jnp.float32),
            pltpu.SemaphoreType.DMA((tail // tile,)),
            pltpu.SemaphoreType.DMA((tail // tile,)),
            pltpu.SemaphoreType.DMA((columns // (2 * down_tile),)),
        ],
        cost_estimate=pl.CostEstimate(
            flops=4 * rows * tail * units + 2 * rows * columns * units,
            bytes_accessed=4 * tail * units + 2 * units * columns,
            transcendentals=rows * units,
        ),
        compiler_params=pltpu.CompilerParams(vmem_limit_bytes=24 * MEBI),
        name="expert",
    )(node, *blocks, *sums, in_hbm(w_gate), in_hbm(w_up), in_hbm(w_down))


def body(
    moe_rows,
    route_ids,
    route_gates,
    w_gate,
    w_up,
    w_down,
    query_latent,
    query_rope,
    cache_latent,
    cache_rope,
    cache_lengths,
):
    grid = Grid()
    high, middle, cores, _ = grid.sizes
    experts = high * middle * cores
    tokens, width = moe_rows.shape
    node = lax.axis_index(("high", "middle", "core")).astype(jnp.int32).reshape(1)
    split = width * 4 // 7
    tied = lax.optimization_barrier
    attn_latent = attention(query_latent, query_rope, cache_latent, cache_rope, cache_lengths)

    lines = grid.lines(pack(experts, moe_rows, route_ids, route_gates), grid.masks())
    lines[-1], attn_latent = tied((lines[-1], attn_latent))
    total = lines[0].shape[1]
    head, tail = join(lines, [(0, split)], [(split, total - split)])
    head, tail = grid.near(head), grid.near(tail)
    far = grid.far(head)
    tail_far = grid.far(tail[:1])
    far[-1], tail[-1], tail_far[0] = tied((far[-1], tail[-1], tail_far[0]))
    head, tail = head + far, tail + tail_far + grid.far(tail[1:])
    other = grid.other(head)
    sums = first_sums(head + other[-1:] + other[:-1], w_gate[0], w_up[0])
    tail[-1], sums = tied((tail[-1], sums))
    other = grid.other(tail)
    size, count = high * tokens, len(tail)
    sizes = [size] * count + [size, size * (count - 1)]
    products = expert(
        tail + other[-1:] + other[:-1],
        sums,
        w_gate[0],
        w_up[0],
        w_down[0],
        experts,
        node,
        sizes,
        split,
    )

    def returned(parts):
        mine, other = parts[:count], parts[count:]
        last = grid.last_sum(mine, other)
        sums = grid.rest_sums(mine, other) + [last]
        return grid.high_sum(grid.line_sum(sums, grid.back(sums, count - 1)))

    head, tail = returned(products[: len(sizes)]), returned(products[len(sizes) :])
    return (jnp.concatenate([head, tail], axis=1), attn_latent)


def solution(mesh):
    groups, nodes, local = mesh.devices.shape
    split = Mesh(mesh.devices.reshape(groups, nodes // 4, 2, 2, local), ("group",) + everyone)
    node = ("high", "middle", "core")
    whole = ("group",) + everyone
    rows = P(whole, None)
    blocks = P(whole, None, None)
    return jax.shard_map(
        body,
        mesh=split,
        in_specs=(
            rows,
            rows,
            rows,
            P(node, None, "local"),
            P(node, None, "local"),
            P(node, "local", None),
            blocks,
            blocks,
            blocks,
            blocks,
            P(whole),
        ),
        out_specs=(rows, blocks),
        check_vma=False,
    )
```

```python
import functools

import jax
import jax.numpy as jnp
import numpy as np
from jax import lax
from jax.experimental import pallas as pl
from jax.experimental.pallas import tpu as pltpu
from jax.sharding import Mesh
from jax.sharding import PartitionSpec as P

score_scale = 192.0 ** (-0.5)
everyone = ("high", "middle", "core", "local")
MEBI = 1024 * 1024


def attention_kernel(lengths_ref, *refs):
    sources, (out_ref, *targets), sems = refs[:4], refs[4:-1], refs[-1]
    query_ref, query_rope_ref, cache_ref, cache_rope_ref = targets
    copies = []
    for row in range(out_ref.shape[0]):
        copies.append(
            [
                pltpu.make_async_copy(source.at[row], target.at[row], sems.at[row, i])
                for i, (source, target) in enumerate(zip(sources, targets))
            ]
        )
        for copy in copies[-1]:
            copy.start()
    for row in range(out_ref.shape[0]):
        for copy in copies[row]:
            copy.wait()
        cache = cache_ref[row]
        scores = lax.dot_general(
            query_ref[row], cache, (((1,), (1,)), ((), ())), preferred_element_type=jnp.float32
        )
        scores += jnp.dot(
            query_rope_ref[row], cache_rope_ref[row], preferred_element_type=jnp.float32
        )
        slot = lax.broadcasted_iota(jnp.int32, scores.shape, 1)
        in_range = slot < lengths_ref[row]
        scores = jnp.where(in_range, scores * score_scale, -jnp.inf)
        row_peak = jnp.max(scores, axis=1, keepdims=True)
        lifted = jnp.where(in_range, jnp.exp(scores - row_peak), 0.0)
        weights = (lifted / jnp.sum(lifted, axis=1, keepdims=True)).astype(jnp.bfloat16)
        value = jnp.dot(weights, cache, preferred_element_type=jnp.float32)
        out_ref[row] = value.astype(jnp.bfloat16)


def attention(query_latent, query_rope, cache_latent, cache_rope, cache_lengths):
    rows, heads, latent = query_latent.shape
    slots = cache_latent.shape[1]
    sources = (query_latent, query_rope, cache_latent, cache_rope)
    return pl.pallas_call(
        attention_kernel,
        in_specs=[pl.BlockSpec(memory_space=pltpu.SMEM)]
        + [pl.BlockSpec(memory_space=pltpu.HBM)] * 4,
        out_specs=pl.BlockSpec(memory_space=pltpu.VMEM),
        out_shape=jax.ShapeDtypeStruct(query_latent.shape, jnp.bfloat16),
        scratch_shapes=[pltpu.VMEM(source.shape, source.dtype) for source in sources]
        + [pltpu.SemaphoreType.DMA((rows, 4))],
        cost_estimate=pl.CostEstimate(
            flops=4 * rows * heads * slots * latent,
            bytes_accessed=2 * rows * slots * latent,
            transcendentals=rows * heads * slots,
        ),
        compiler_params=pltpu.CompilerParams(vmem_limit_bytes=8 * MEBI),
        name="attention",
    )(cache_lengths, *[in_hbm(source) for source in sources])


def in_hbm(array):
    return pltpu.with_memory_space_constraint(array, pltpu.HBM)


class Grid:
    def __init__(self):
        self.sizes = tuple(lax.axis_size(name) for name in everyone)
        self.mixed = self.sizes[1] == self.sizes[3]

    def swap(self, value, pick, mask):
        pairs = []
        for place in np.ndindex(*self.sizes):
            other = list(place)
            other[pick(place[2])] ^= mask
            pairs.append(
                (
                    int(np.ravel_multi_index(place, self.sizes)),
                    int(np.ravel_multi_index(other, self.sizes)),
                )
            )
        return lax.ppermute(value, everyone, pairs)

    def high(self, core):
        return 0

    def core(self, core):
        return 2

    def first(self, core):
        return 1 if self.mixed and core == 1 else 3

    def second(self, core):
        return 3 if self.mixed and core == 1 else 1

    def extent(self, pick):
        return self.sizes[pick(0)]

    def masks(self):
        masks, m = [], self.extent(self.high) // 2
        while m:
            masks.append(m)
            m //= 2
        return masks

    def lines(self, rows, masks, beside):
        if not masks:
            return [rows], beside
        came = self.swap(rows, self.high, masks[0])
        near, _ = self.lines(rows, masks[1:], ())
        came, near, beside = lax.optimization_barrier((came, near, beside))
        far, _ = self.lines(came, masks[1:], ())
        return near + far, beside

    def near(self, line):
        return [line] + [self.swap(line, self.first, m) for m in range(1, self.extent(self.first))]

    def far(self, near):
        return [self.swap(block, self.second, 1) for block in near]

    def other(self, mine):
        return [self.swap(block, self.core, 1) for block in mine]

    def last_sum(self, mine, other):
        return add([mine[-1], self.swap(other[0], self.core, 1)])

    def rest_sums(self, mine, other):
        size = mine[0].shape[0]
        rest = self.swap(other[1], self.core, 1)
        return [
            add([part, rest[i * size : (i + 1) * size]]) for i, part in enumerate(mine[:-1])
        ]

    def back(self, sums, place):
        return self.swap(sums[place], self.second, place // self.extent(self.first))

    def line_sum(self, sums, last):
        wide = self.extent(self.first)
        near = [[part] for part in sums[:wide]]
        for place in range(wide, len(sums)):
            moved = last if place == len(sums) - 1 else self.back(sums, place)
            near[place % wide].append(moved)
        near = [add(parts) for parts in near]
        return add([near[0]] + [self.swap(near[m], self.first, m) for m in range(1, wide)])

    def high_sum(self, line):
        rows = line.shape[0] // self.extent(self.high)
        parts = [line[:rows]]
        for m in range(1, self.extent(self.high)):
            parts.append(self.swap(line[m * rows : (m + 1) * rows], self.high, m))
        return add(parts)


def add(parts):
    total = parts[0].astype(jnp.float32)
    for part in parts[1:]:
        total = total + part.astype(jnp.float32)
    return total.astype(parts[0].dtype)


def join_kernel(count, ranges, *refs):
    for out, parts in zip(refs[count:], ranges):
        start = 0
        for first, size in parts:
            columns = pl.ds(first, size)
            out[:, start : start + size] = jnp.concatenate(
                [ref[:, columns] for ref in refs[:count]], axis=0
            )
            start += size


def join(parts, *ranges):
    rows = sum(part.shape[0] for part in parts)
    ranges = ranges or ([(0, parts[0].shape[1])],)
    outs = pl.pallas_call(
        functools.partial(join_kernel, len(parts), ranges),
        in_specs=[pl.BlockSpec(memory_space=pltpu.VMEM)] * len(parts),
        out_specs=[pl.BlockSpec(memory_space=pltpu.VMEM)] * len(ranges),
        out_shape=[
            jax.ShapeDtypeStruct((rows, sum(size for _, size in columns)), parts[0].dtype)
            for columns in ranges
        ],
        compiler_params=pltpu.CompilerParams(vmem_limit_bytes=4 * MEBI),
        name="join",
    )(*parts)
    return outs if len(ranges) > 1 else outs[0]


def table_width(experts):
    return pl.cdiv(2 * experts, 128) * 128


def pack_kernel(experts, *refs):
    sources, (out_ref, *targets), sems = refs[:3], refs[3:-1], refs[-1]
    copies = [
        pltpu.make_async_copy(source, target, sems.at[i])
        for i, (source, target) in enumerate(zip(sources, targets))
    ]
    for copy in copies:
        copy.start()
    rows_ref, ids_ref, gates_ref = targets
    for copy in copies[1:]:
        copy.wait()
    extra = table_width(experts)
    width = rows_ref.shape[1]
    gates = gates_ref[...]
    shares = 2.5 * gates / jnp.sum(gates, axis=1, keepdims=True)
    ids = ids_ref[...]
    lane = lax.broadcasted_iota(jnp.int32, (ids.shape[0], extra), 1)
    expert = jnp.where(lane < experts, lane, lane - experts)
    table = jnp.zeros(lane.shape, jnp.float32)
    for k in range(ids.shape[1]):
        table += jnp.where(expert == ids[:, k : k + 1], shares[:, k : k + 1], 0.0)
    high = table.astype(jnp.bfloat16).astype(jnp.float32)
    table = jnp.where(lane < experts, high, jnp.where(lane < 2 * experts, table - high, 0.0))
    out_ref[:, width:] = table.astype(jnp.bfloat16)
    copies[0].wait()
    out_ref[:, :width] = rows_ref[...]


def pack(experts, moe_rows, route_ids, route_gates):
    rows, width = moe_rows.shape
    sources = (moe_rows, route_ids, route_gates)
    return pl.pallas_call(
        functools.partial(pack_kernel, experts),
        in_specs=[pl.BlockSpec(memory_space=pltpu.HBM)] * 3,
        out_specs=pl.BlockSpec(memory_space=pltpu.VMEM),
        scratch_shapes=[pltpu.VMEM(source.shape, source.dtype) for source in sources]
        + [pltpu.SemaphoreType.DMA((3,))],
        out_shape=jax.ShapeDtypeStruct((rows, width + table_width(experts)), jnp.bfloat16),
        compiler_params=pltpu.CompilerParams(vmem_limit_bytes=4 * MEBI),
        name="pack",
    )(*[in_hbm(source) for source in sources])


def spread(product, outs):
    start = 0
    for out, columns in outs:
        size = out.shape[0]
        out[:, columns] = product[start : start + size]
        start += size


def fetch_columns(source, target, sems):
    columns = target.shape[1] // sems.shape[0]
    copies = []
    for k in range(sems.shape[0]):
        part = pl.ds(k * columns, columns)
        copies.append(pltpu.make_async_copy(source.at[:, part], target.at[:, part], sems.at[k]))
        copies[-1].start()
    return copies


def fetch_both(gate_hbm, up_hbm, gate, up, gate_sem, up_sem, tile):
    copies = []
    for k in range(0, gate.shape[0], tile):
        part = pl.ds(k, tile)
        pair = (
            pltpu.make_async_copy(gate_hbm.at[part], gate.at[part], gate_sem.at[k // tile]),
            pltpu.make_async_copy(up_hbm.at[part], up.at[part], up_sem.at[k // tile]),
        )
        for copy in pair:
            copy.start()
        copies.append(pair)
    return copies


def project(blocks, copies, gate, up, gate_sum, up_sum, tile):
    for k, pair in enumerate(copies):
        part = pl.ds(k * tile, tile)
        rows = jnp.concatenate([block[:, part] for block in blocks], axis=0)
        for copy, weight, total in zip(pair, (gate, up), (gate_sum, up_sum)):
            copy.wait()
            product = jnp.dot(rows, weight[part], preferred_element_type=jnp.float32)
            if k == 0:
                total[...] = product
            else:
                total[...] += product


def expert_kernel(count, experts, tile, down_tile, split, node_ref, *refs):
    blocks = refs[:count]
    gate_hbm, up_hbm, down_hbm = refs[count : count + 3]
    outs = refs[count + 3 : -10]
    hidden_ref, share_ref, gate, up, down, gate_sum, up_sum, gate_sem, up_sem, down_sem = refs[-10:]
    copies = fetch_both(gate_hbm, up_hbm, gate, up, gate_sem, up_sem, tile)
    down_copies = fetch_columns(down_hbm, down, down_sem)

    table = jnp.concatenate([block[:, gate.shape[0] :] for block in blocks], axis=0)
    table = table.astype(jnp.float32)
    lane = lax.broadcasted_iota(jnp.int32, table.shape, 1)
    mine = (lane == node_ref[0]) | (lane == node_ref[0] + experts)
    share = jnp.sum(jnp.where(mine, table, 0.0), axis=1, keepdims=True)
    share_ref[...] = jnp.broadcast_to(share, share_ref.shape)
    project(blocks, copies, gate, up, gate_sum, up_sum, tile)
    hidden_ref[...] = (jax.nn.silu(gate_sum[...]) * up_sum[...]).astype(jnp.bfloat16)
    wide = down.shape[1] // len(down_copies)
    for k in range(0, down.shape[1], down_tile):
        if k % wide == 0:
            down_copies[k // wide].wait()
        product = jnp.dot(
            hidden_ref[...], down[:, pl.ds(k, down_tile)], preferred_element_type=jnp.float32
        )
        product = (product * share_ref[:, :1]).astype(jnp.bfloat16)
        if k < split:
            spread(product, [(out, pl.ds(k, down_tile)) for out in outs[: len(outs) // 2]])
        else:
            spread(product, [(out, pl.ds(k - split, down_tile)) for out in outs[len(outs) // 2 :]])


def expert(blocks, w_gate, w_up, w_down, experts, node, sizes, split):
    width, units = w_gate.shape
    rows = sum(sizes)
    tile, down_tile = 1024, 512
    return pl.pallas_call(
        functools.partial(expert_kernel, len(blocks), experts, tile, down_tile, split),
        in_specs=[pl.BlockSpec(memory_space=pltpu.SMEM)]
        + [pl.BlockSpec(memory_space=pltpu.VMEM)] * len(blocks)
        + [pl.BlockSpec(memory_space=pltpu.HBM)] * 3,
        out_specs=[pl.BlockSpec(memory_space=pltpu.VMEM)] * (2 * len(sizes)),
        out_shape=[
            jax.ShapeDtypeStruct((size, chunk), jnp.bfloat16)
            for chunk in (split, width - split)
            for size in sizes
        ],
        scratch_shapes=[
            pltpu.VMEM((rows, units), jnp.bfloat16),
            pltpu.VMEM((rows, 128), jnp.float32),
            pltpu.VMEM((width, units), jnp.bfloat16),
            pltpu.VMEM((width, units), jnp.bfloat16),
            pltpu.VMEM((units, width), jnp.bfloat16),
            pltpu.VMEM((rows, units), jnp.float32),
            pltpu.VMEM((rows, units), jnp.float32),
            pltpu.SemaphoreType.DMA((width // tile,)),
            pltpu.SemaphoreType.DMA((width // tile,)),
            pltpu.SemaphoreType.DMA((width // (2 * down_tile),)),
        ],
        cost_estimate=pl.CostEstimate(
            flops=6 * rows * width * units,
            bytes_accessed=6 * units * width,
            transcendentals=rows * units,
        ),
        compiler_params=pltpu.CompilerParams(vmem_limit_bytes=32 * MEBI),
        name="expert",
    )(node, *blocks, in_hbm(w_gate), in_hbm(w_up), in_hbm(w_down))


def body(
    moe_rows,
    route_ids,
    route_gates,
    w_gate,
    w_up,
    w_down,
    query_latent,
    query_rope,
    cache_latent,
    cache_rope,
    cache_lengths,
):
    grid = Grid()
    high, middle, cores, _ = grid.sizes
    experts = high * middle * cores
    tokens, width = moe_rows.shape
    node = lax.axis_index(("high", "middle", "core")).astype(jnp.int32).reshape(1)
    tied = lax.optimization_barrier
    attn_latent = attention(query_latent, query_rope, cache_latent, cache_rope, cache_lengths)

    outgoing = pack(experts, moe_rows, route_ids, route_gates)
    lines, attn_latent = grid.lines(outgoing, grid.masks(), attn_latent)
    near = grid.near(join(lines))
    far = grid.far(near[:-1])
    rows = near[-1].shape[0] // 2
    mine = near + far + grid.far([near[-1][:rows], near[-1][rows:]])
    other = grid.other(mine)
    size, count = high * tokens, len(mine) - 1
    sizes = [size] * count + [size, size * (count - 1)]
    split = width * 3 // 7
    products = expert(
        mine + other[-2:] + other[:-2],
        w_gate[0],
        w_up[0],
        w_down[0],
        experts,
        node,
        sizes,
        split,
    )

    def returned(parts, last):
        sums = grid.rest_sums(parts[:count], parts[count:]) + [last]
        return grid.high_sum(grid.line_sum(sums, grid.back(sums, count - 1)))

    small, large = products[: len(sizes)], products[len(sizes) :]
    last = grid.last_sum(large[:count], large[count:])
    small, last = tied((small, last))
    large = returned(large, last)
    small = returned(small, grid.last_sum(small[:count], small[count:]))
    return (jnp.concatenate([small, large], axis=1), attn_latent)


def solution(mesh):
    groups, nodes, local = mesh.devices.shape
    split = Mesh(mesh.devices.reshape(groups, nodes // 4, 2, 2, local), ("group",) + everyone)
    node = ("high", "middle", "core")
    whole = ("group",) + everyone
    rows = P(whole, None)
    blocks = P(whole, None, None)
    return jax.shard_map(
        body,
        mesh=split,
        in_specs=(
            rows,
            rows,
            rows,
            P(node, None, "local"),
            P(node, None, "local"),
            P(node, "local", None),
            blocks,
            blocks,
            blocks,
            blocks,
            P(whole),
        ),
        out_specs=(rows, blocks),
        check_vma=False,
    )
```

```python
import functools

import jax
import jax.numpy as jnp
import numpy as np
from jax import lax
from jax.experimental import pallas as pl
from jax.experimental.pallas import tpu as pltpu
from jax.sharding import Mesh
from jax.sharding import PartitionSpec as P

score_scale = 192.0 ** (-0.5)
everyone = ("high", "middle", "core", "local")
MEBI = 1024 * 1024


def attention_kernel(lengths_ref, *refs):
    sources, (out_ref, *targets), sems = refs[:4], refs[4:-1], refs[-1]
    query_ref, query_rope_ref, cache_ref, cache_rope_ref = targets
    copies = []
    for row in range(out_ref.shape[0]):
        copies.append(
            [
                pltpu.make_async_copy(source.at[row], target.at[row], sems.at[row, i])
                for i, (source, target) in enumerate(zip(sources, targets))
            ]
        )
        for copy in copies[-1]:
            copy.start()
    for row in range(out_ref.shape[0]):
        for copy in copies[row]:
            copy.wait()
        cache = cache_ref[row]
        scores = lax.dot_general(
            query_ref[row], cache, (((1,), (1,)), ((), ())), preferred_element_type=jnp.float32
        )
        scores += jnp.dot(
            query_rope_ref[row], cache_rope_ref[row], preferred_element_type=jnp.float32
        )
        slot = lax.broadcasted_iota(jnp.int32, scores.shape, 1)
        in_range = slot < lengths_ref[row]
        scores = jnp.where(in_range, scores * score_scale, -jnp.inf)
        row_peak = jnp.max(scores, axis=1, keepdims=True)
        lifted = jnp.where(in_range, jnp.exp(scores - row_peak), 0.0)
        weights = (lifted / jnp.sum(lifted, axis=1, keepdims=True)).astype(jnp.bfloat16)
        value = jnp.dot(weights, cache, preferred_element_type=jnp.float32)
        out_ref[row] = value.astype(jnp.bfloat16)


def attention(query_latent, query_rope, cache_latent, cache_rope, cache_lengths):
    rows, heads, latent = query_latent.shape
    slots = cache_latent.shape[1]
    sources = (query_latent, query_rope, cache_latent, cache_rope)
    return pl.pallas_call(
        attention_kernel,
        in_specs=[pl.BlockSpec(memory_space=pltpu.SMEM)]
        + [pl.BlockSpec(memory_space=pltpu.HBM)] * 4,
        out_specs=pl.BlockSpec(memory_space=pltpu.VMEM),
        out_shape=jax.ShapeDtypeStruct(query_latent.shape, jnp.bfloat16),
        scratch_shapes=[pltpu.VMEM(source.shape, source.dtype) for source in sources]
        + [pltpu.SemaphoreType.DMA((rows, 4))],
        cost_estimate=pl.CostEstimate(
            flops=4 * rows * heads * slots * latent,
            bytes_accessed=2 * rows * slots * latent,
            transcendentals=rows * heads * slots,
        ),
        compiler_params=pltpu.CompilerParams(vmem_limit_bytes=8 * MEBI),
        name="attention",
    )(cache_lengths, *[in_hbm(source) for source in sources])


def in_hbm(array):
    return pltpu.with_memory_space_constraint(array, pltpu.HBM)


class Grid:
    def __init__(self):
        self.sizes = tuple(lax.axis_size(name) for name in everyone)
        self.mixed = self.sizes[1] == self.sizes[3]

    def swap(self, value, pick, mask):
        pairs = []
        for place in np.ndindex(*self.sizes):
            other = list(place)
            other[pick(place[2])] ^= mask
            pairs.append(
                (
                    int(np.ravel_multi_index(place, self.sizes)),
                    int(np.ravel_multi_index(other, self.sizes)),
                )
            )
        return lax.ppermute(value, everyone, pairs)

    def high(self, core):
        return 0

    def core(self, core):
        return 2

    def first(self, core):
        return 1 if self.mixed and core == 1 else 3

    def second(self, core):
        return 3 if self.mixed and core == 1 else 1

    def extent(self, pick):
        return self.sizes[pick(0)]

    def masks(self):
        masks, m = [], self.extent(self.high) // 2
        while m:
            masks.append(m)
            m //= 2
        return masks

    def lines(self, rows, masks):
        if not masks:
            return [rows]
        came = self.swap(rows, self.high, masks[0])
        return self.lines(rows, masks[1:]) + self.lines(came, masks[1:])

    def near(self, line):
        return [line] + [self.swap(line, self.first, m) for m in range(1, self.extent(self.first))]

    def far(self, near):
        return [self.swap(block, self.second, 1) for block in near]

    def other(self, mine):
        return [self.swap(block, self.core, 1) for block in mine]

    def last_sum(self, mine, other):
        return add([mine[-1], self.swap(other[0], self.core, 1)])

    def rest_sums(self, mine, other):
        size = mine[0].shape[0]
        rest = self.swap(other[1], self.core, 1)
        return [
            add([part, rest[i * size : (i + 1) * size]]) for i, part in enumerate(mine[:-1])
        ]

    def back(self, sums, place):
        return self.swap(sums[place], self.second, place // self.extent(self.first))

    def line_sum(self, sums, last):
        wide = self.extent(self.first)
        near = [[part] for part in sums[:wide]]
        for place in range(wide, len(sums)):
            moved = last if place == len(sums) - 1 else self.back(sums, place)
            near[place % wide].append(moved)
        near = [add(parts) for parts in near]
        return add([near[0]] + [self.swap(near[m], self.first, m) for m in range(1, wide)])

    def high_sum(self, line):
        rows = line.shape[0] // self.extent(self.high)
        parts = [line[:rows]]
        for m in range(1, self.extent(self.high)):
            parts.append(self.swap(line[m * rows : (m + 1) * rows], self.high, m))
        return add(parts)


def add(parts):
    total = parts[0].astype(jnp.float32)
    for part in parts[1:]:
        total = total + part.astype(jnp.float32)
    return total.astype(parts[0].dtype)


def join_kernel(count, ranges, *refs):
    for out, parts in zip(refs[count:], ranges):
        start = 0
        for first, size in parts:
            columns = pl.ds(first, size)
            out[:, start : start + size] = jnp.concatenate(
                [ref[:, columns] for ref in refs[:count]], axis=0
            )
            start += size


def join(parts, *ranges):
    rows = sum(part.shape[0] for part in parts)
    ranges = ranges or ([(0, parts[0].shape[1])],)
    outs = pl.pallas_call(
        functools.partial(join_kernel, len(parts), ranges),
        in_specs=[pl.BlockSpec(memory_space=pltpu.VMEM)] * len(parts),
        out_specs=[pl.BlockSpec(memory_space=pltpu.VMEM)] * len(ranges),
        out_shape=[
            jax.ShapeDtypeStruct((rows, sum(size for _, size in columns)), parts[0].dtype)
            for columns in ranges
        ],
        compiler_params=pltpu.CompilerParams(vmem_limit_bytes=4 * MEBI),
        name="join",
    )(*parts)
    return outs if len(ranges) > 1 else outs[0]


def table_width(experts):
    return pl.cdiv(2 * experts, 128) * 128


def pack_kernel(experts, *refs):
    sources, (out_ref, *targets), sems = refs[:3], refs[3:-1], refs[-1]
    copies = [
        pltpu.make_async_copy(source, target, sems.at[i])
        for i, (source, target) in enumerate(zip(sources, targets))
    ]
    for copy in copies:
        copy.start()
    rows_ref, ids_ref, gates_ref = targets
    for copy in copies[1:]:
        copy.wait()
    extra = table_width(experts)
    width = rows_ref.shape[1]
    gates = gates_ref[...]
    shares = 2.5 * gates / jnp.sum(gates, axis=1, keepdims=True)
    ids = ids_ref[...]
    lane = lax.broadcasted_iota(jnp.int32, (ids.shape[0], extra), 1)
    expert = jnp.where(lane < experts, lane, lane - experts)
    table = jnp.zeros(lane.shape, jnp.float32)
    for k in range(ids.shape[1]):
        table += jnp.where(expert == ids[:, k : k + 1], shares[:, k : k + 1], 0.0)
    high = table.astype(jnp.bfloat16).astype(jnp.float32)
    table = jnp.where(lane < experts, high, jnp.where(lane < 2 * experts, table - high, 0.0))
    out_ref[:, width:] = table.astype(jnp.bfloat16)
    copies[0].wait()
    out_ref[:, :width] = rows_ref[...]


def pack(experts, moe_rows, route_ids, route_gates):
    rows, width = moe_rows.shape
    sources = (moe_rows, route_ids, route_gates)
    return pl.pallas_call(
        functools.partial(pack_kernel, experts),
        in_specs=[pl.BlockSpec(memory_space=pltpu.HBM)] * 3,
        out_specs=pl.BlockSpec(memory_space=pltpu.VMEM),
        scratch_shapes=[pltpu.VMEM(source.shape, source.dtype) for source in sources]
        + [pltpu.SemaphoreType.DMA((3,))],
        out_shape=jax.ShapeDtypeStruct((rows, width + table_width(experts)), jnp.bfloat16),
        compiler_params=pltpu.CompilerParams(vmem_limit_bytes=4 * MEBI),
        name="pack",
    )(*[in_hbm(source) for source in sources])


def spread(product, outs):
    start = 0
    for out, columns in outs:
        size = out.shape[0]
        out[:, columns] = product[start : start + size]
        start += size


def fetch_columns(source, target, sems):
    columns = target.shape[1] // sems.shape[0]
    copies = []
    for k in range(sems.shape[0]):
        part = pl.ds(k * columns, columns)
        copies.append(pltpu.make_async_copy(source.at[:, part], target.at[:, part], sems.at[k]))
        copies[-1].start()
    return copies


def fetch_both(gate_hbm, up_hbm, gate, up, gate_sem, up_sem, tile):
    copies = []
    for k in range(0, gate.shape[0], tile):
        part = pl.ds(k, tile)
        pair = (
            pltpu.make_async_copy(gate_hbm.at[part], gate.at[part], gate_sem.at[k // tile]),
            pltpu.make_async_copy(up_hbm.at[part], up.at[part], up_sem.at[k // tile]),
        )
        for copy in pair:
            copy.start()
        copies.append(pair)
    return copies


def project(blocks, copies, gate, up, gate_sum, up_sum, tile):
    for k, pair in enumerate(copies):
        part = pl.ds(k * tile, tile)
        rows = jnp.concatenate([block[:, part] for block in blocks], axis=0)
        for copy, weight, total in zip(pair, (gate, up), (gate_sum, up_sum)):
            copy.wait()
            product = jnp.dot(rows, weight[part], preferred_element_type=jnp.float32)
            if k == 0:
                total[...] = product
            else:
                total[...] += product


def expert_kernel(count, experts, tile, down_tile, split, node_ref, *refs):
    blocks = refs[:count]
    gate_hbm, up_hbm, down_hbm = refs[count : count + 3]
    outs = refs[count + 3 : -10]
    hidden_ref, share_ref, gate, up, down, gate_sum, up_sum, gate_sem, up_sem, down_sem = refs[-10:]
    copies = fetch_both(gate_hbm, up_hbm, gate, up, gate_sem, up_sem, tile)
    down_copies = fetch_columns(down_hbm, down, down_sem)

    table = jnp.concatenate([block[:, gate.shape[0] :] for block in blocks], axis=0)
    table = table.astype(jnp.float32)
    lane = lax.broadcasted_iota(jnp.int32, table.shape, 1)
    mine = (lane == node_ref[0]) | (lane == node_ref[0] + experts)
    share = jnp.sum(jnp.where(mine, table, 0.0), axis=1, keepdims=True)
    share_ref[...] = jnp.broadcast_to(share, share_ref.shape)
    project(blocks, copies, gate, up, gate_sum, up_sum, tile)
    hidden_ref[...] = (jax.nn.silu(gate_sum[...]) * up_sum[...]).astype(jnp.bfloat16)
    wide = down.shape[1] // len(down_copies)
    for k in range(0, down.shape[1], down_tile):
        if k % wide == 0:
            down_copies[k // wide].wait()
        product = jnp.dot(
            hidden_ref[...], down[:, pl.ds(k, down_tile)], preferred_element_type=jnp.float32
        )
        product = (product * share_ref[:, :1]).astype(jnp.bfloat16)
        if k < split:
            spread(product, [(out, pl.ds(k, down_tile)) for out in outs[: len(outs) // 2]])
        else:
            spread(product, [(out, pl.ds(k - split, down_tile)) for out in outs[len(outs) // 2 :]])


def expert(blocks, w_gate, w_up, w_down, experts, node, sizes, split):
    width, units = w_gate.shape
    rows = sum(sizes)
    tile, down_tile = 1024, 512
    return pl.pallas_call(
        functools.partial(expert_kernel, len(blocks), experts, tile, down_tile, split),
        in_specs=[pl.BlockSpec(memory_space=pltpu.SMEM)]
        + [pl.BlockSpec(memory_space=pltpu.VMEM)] * len(blocks)
        + [pl.BlockSpec(memory_space=pltpu.HBM)] * 3,
        out_specs=[pl.BlockSpec(memory_space=pltpu.VMEM)] * (2 * len(sizes)),
        out_shape=[
            jax.ShapeDtypeStruct((size, chunk), jnp.bfloat16)
            for chunk in (split, width - split)
            for size in sizes
        ],
        scratch_shapes=[
            pltpu.VMEM((rows, units), jnp.bfloat16),
            pltpu.VMEM((rows, 128), jnp.float32),
            pltpu.VMEM((width, units), jnp.bfloat16),
            pltpu.VMEM((width, units), jnp.bfloat16),
            pltpu.VMEM((units, width), jnp.bfloat16),
            pltpu.VMEM((rows, units), jnp.float32),
            pltpu.VMEM((rows, units), jnp.float32),
            pltpu.SemaphoreType.DMA((width // tile,)),
            pltpu.SemaphoreType.DMA((width // tile,)),
            pltpu.SemaphoreType.DMA((width // (2 * down_tile),)),
        ],
        cost_estimate=pl.CostEstimate(
            flops=6 * rows * width * units,
            bytes_accessed=6 * units * width,
            transcendentals=rows * units,
        ),
        compiler_params=pltpu.CompilerParams(vmem_limit_bytes=32 * MEBI),
        name="expert",
    )(node, *blocks, in_hbm(w_gate), in_hbm(w_up), in_hbm(w_down))


def body(
    moe_rows,
    route_ids,
    route_gates,
    w_gate,
    w_up,
    w_down,
    query_latent,
    query_rope,
    cache_latent,
    cache_rope,
    cache_lengths,
):
    grid = Grid()
    high, middle, cores, _ = grid.sizes
    experts = high * middle * cores
    tokens, width = moe_rows.shape
    node = lax.axis_index(("high", "middle", "core")).astype(jnp.int32).reshape(1)
    tied = lax.optimization_barrier
    attn_latent = attention(query_latent, query_rope, cache_latent, cache_rope, cache_lengths)

    outgoing = pack(experts, moe_rows, route_ids, route_gates)
    masks = grid.masks()
    came = grid.swap(outgoing, grid.high, masks[0])
    near = grid.near(join(grid.lines(outgoing, masks[1:])))
    far = grid.far(near[:-1])
    lines = grid.lines(came, masks[1:])
    lines[-1], near[-1], far[0] = tied((lines[-1], near[-1], far[0]))
    later_near = grid.near(join(lines))
    later_far = grid.far(later_near[:-1])
    far += grid.far(near[-1:])
    far[-1], later_near[-1], later_far[0], attn_latent = tied(
        (far[-1], later_near[-1], later_far[0], attn_latent)
    )
    rows = later_near[-1].shape[0] // 2
    last = grid.far([later_near[-1][:rows], later_near[-1][rows:]])
    mine = [[block] for block in near + far]
    for place, block in zip(mine, later_near + later_far):
        place.append(block)
    mine[-1] += last
    other = [grid.other(place) for place in mine]
    size, count = high * tokens, len(mine)
    sizes = [size] * count + [size, size * (count - 1)]
    split = width // 2
    places = mine + other[-1:] + other[:-1]
    products = expert(
        [block for place in places for block in place],
        w_gate[0],
        w_up[0],
        w_down[0],
        experts,
        node,
        sizes,
        split,
    )

    def returned(parts):
        last = grid.last_sum(parts[:count], parts[count:])
        sums = grid.rest_sums(parts[:count], parts[count:]) + [last]
        return grid.high_sum(grid.line_sum(sums, grid.back(sums, count - 1)))

    head, tail = returned(products[: len(sizes)]), returned(products[len(sizes) :])
    return (jnp.concatenate([head, tail], axis=1), attn_latent)


def solution(mesh):
    groups, nodes, local = mesh.devices.shape
    split = Mesh(mesh.devices.reshape(groups, nodes // 4, 2, 2, local), ("group",) + everyone)
    node = ("high", "middle", "core")
    whole = ("group",) + everyone
    rows = P(whole, None)
    blocks = P(whole, None, None)
    return jax.shard_map(
        body,
        mesh=split,
        in_specs=(
            rows,
            rows,
            rows,
            P(node, None, "local"),
            P(node, None, "local"),
            P(node, "local", None),
            blocks,
            blocks,
            blocks,
            blocks,
            P(whole),
        ),
        out_specs=(rows, blocks),
        check_vma=False,
    )
```

```python
import functools

import jax
import jax.numpy as jnp
import numpy as np
from jax import lax
from jax.experimental import pallas as pl
from jax.experimental.pallas import tpu as pltpu
from jax.sharding import Mesh
from jax.sharding import PartitionSpec as P

score_scale = 192.0 ** (-0.5)
everyone = ("high", "middle", "core", "local")
MEBI = 1024 * 1024


def attention_kernel(lengths_ref, *refs):
    sources, (out_ref, *targets), sems = refs[:4], refs[4:-1], refs[-1]
    query_ref, query_rope_ref, cache_ref, cache_rope_ref = targets
    copies = []
    for row in range(out_ref.shape[0]):
        copies.append(
            [
                pltpu.make_async_copy(source.at[row], target.at[row], sems.at[row, i])
                for i, (source, target) in enumerate(zip(sources, targets))
            ]
        )
        for copy in copies[-1]:
            copy.start()
    for row in range(out_ref.shape[0]):
        for copy in copies[row]:
            copy.wait()
        cache = cache_ref[row]
        scores = lax.dot_general(
            query_ref[row], cache, (((1,), (1,)), ((), ())), preferred_element_type=jnp.float32
        )
        scores += jnp.dot(
            query_rope_ref[row], cache_rope_ref[row], preferred_element_type=jnp.float32
        )
        slot = lax.broadcasted_iota(jnp.int32, scores.shape, 1)
        in_range = slot < lengths_ref[row]
        scores = jnp.where(in_range, scores * score_scale, -jnp.inf)
        row_peak = jnp.max(scores, axis=1, keepdims=True)
        lifted = jnp.where(in_range, jnp.exp(scores - row_peak), 0.0)
        weights = (lifted / jnp.sum(lifted, axis=1, keepdims=True)).astype(jnp.bfloat16)
        value = jnp.dot(weights, cache, preferred_element_type=jnp.float32)
        out_ref[row] = value.astype(jnp.bfloat16)


def attention(query_latent, query_rope, cache_latent, cache_rope, cache_lengths):
    rows, heads, latent = query_latent.shape
    slots = cache_latent.shape[1]
    sources = (query_latent, query_rope, cache_latent, cache_rope)
    return pl.pallas_call(
        attention_kernel,
        in_specs=[pl.BlockSpec(memory_space=pltpu.SMEM)]
        + [pl.BlockSpec(memory_space=pltpu.HBM)] * 4,
        out_specs=pl.BlockSpec(memory_space=pltpu.VMEM),
        out_shape=jax.ShapeDtypeStruct(query_latent.shape, jnp.bfloat16),
        scratch_shapes=[pltpu.VMEM(source.shape, source.dtype) for source in sources]
        + [pltpu.SemaphoreType.DMA((rows, 4))],
        cost_estimate=pl.CostEstimate(
            flops=4 * rows * heads * slots * latent,
            bytes_accessed=2 * rows * slots * latent,
            transcendentals=rows * heads * slots,
        ),
        compiler_params=pltpu.CompilerParams(vmem_limit_bytes=8 * MEBI),
        name="attention",
    )(cache_lengths, *[in_hbm(source) for source in sources])


def in_hbm(array):
    return pltpu.with_memory_space_constraint(array, pltpu.HBM)


class Grid:
    def __init__(self):
        self.sizes = tuple(lax.axis_size(name) for name in everyone)
        self.mixed = self.sizes[1] == self.sizes[3]

    def swap(self, value, pick, mask):
        pairs = []
        for place in np.ndindex(*self.sizes):
            other = list(place)
            other[pick(place[2])] ^= mask
            pairs.append(
                (
                    int(np.ravel_multi_index(place, self.sizes)),
                    int(np.ravel_multi_index(other, self.sizes)),
                )
            )
        return lax.ppermute(value, everyone, pairs)

    def high(self, core):
        return 0

    def core(self, core):
        return 2

    def first(self, core):
        return 1 if self.mixed and core == 1 else 3

    def second(self, core):
        return 3 if self.mixed and core == 1 else 1

    def extent(self, pick):
        return self.sizes[pick(0)]

    def masks(self):
        masks, m = [], self.extent(self.high) // 2
        while m:
            masks.append(m)
            m //= 2
        return masks

    def lines(self, rows, masks):
        if not masks:
            return [rows]
        came = self.swap(rows, self.high, masks[0])
        return self.lines(rows, masks[1:]) + self.lines(came, masks[1:])

    def near(self, line):
        return [line] + [self.swap(line, self.first, m) for m in range(1, self.extent(self.first))]

    def far(self, near):
        return [self.swap(block, self.second, 1) for block in near]

    def other(self, mine):
        return [self.swap(block, self.core, 1) for block in mine]

    def last_sum(self, mine, other):
        return add([mine[-1], self.swap(other[0], self.core, 1)])

    def rest_sums(self, mine, other):
        size = mine[0].shape[0]
        rest = self.swap(other[1], self.core, 1)
        return [
            add([part, rest[i * size : (i + 1) * size]]) for i, part in enumerate(mine[:-1])
        ]

    def back(self, sums, place):
        return self.swap(sums[place], self.second, place // self.extent(self.first))

    def line_sum(self, sums, came):
        near = [add(list(parts)) for parts in zip(sums, came)]
        return add([near[0]] + [self.swap(near[m], self.first, m) for m in range(1, len(near))])

    def high_sum(self, line):
        rows = line.shape[0] // self.extent(self.high)
        parts = [line[:rows]]
        for m in range(1, self.extent(self.high)):
            parts.append(self.swap(line[m * rows : (m + 1) * rows], self.high, m))
        return add(parts)


def add(parts):
    total = parts[0].astype(jnp.float32)
    for part in parts[1:]:
        total = total + part.astype(jnp.float32)
    return total.astype(parts[0].dtype)


def join_kernel(count, ranges, *refs):
    for out, parts in zip(refs[count:], ranges):
        start = 0
        for first, size in parts:
            columns = pl.ds(first, size)
            out[:, start : start + size] = jnp.concatenate(
                [ref[:, columns] for ref in refs[:count]], axis=0
            )
            start += size


def join(parts, *ranges):
    rows = sum(part.shape[0] for part in parts)
    ranges = ranges or ([(0, parts[0].shape[1])],)
    outs = pl.pallas_call(
        functools.partial(join_kernel, len(parts), ranges),
        in_specs=[pl.BlockSpec(memory_space=pltpu.VMEM)] * len(parts),
        out_specs=[pl.BlockSpec(memory_space=pltpu.VMEM)] * len(ranges),
        out_shape=[
            jax.ShapeDtypeStruct((rows, sum(size for _, size in columns)), parts[0].dtype)
            for columns in ranges
        ],
        compiler_params=pltpu.CompilerParams(vmem_limit_bytes=4 * MEBI),
        name="join",
    )(*parts)
    return outs if len(ranges) > 1 else outs[0]


def table_width(experts):
    return pl.cdiv(2 * experts, 128) * 128


def pack_kernel(experts, *refs):
    sources, (out_ref, *targets), sems = refs[:3], refs[3:-1], refs[-1]
    copies = [
        pltpu.make_async_copy(source, target, sems.at[i])
        for i, (source, target) in enumerate(zip(sources, targets))
    ]
    for copy in copies:
        copy.start()
    rows_ref, ids_ref, gates_ref = targets
    for copy in copies[1:]:
        copy.wait()
    extra = table_width(experts)
    width = rows_ref.shape[1]
    gates = gates_ref[...]
    shares = 2.5 * gates / jnp.sum(gates, axis=1, keepdims=True)
    ids = ids_ref[...]
    lane = lax.broadcasted_iota(jnp.int32, (ids.shape[0], extra), 1)
    expert = jnp.where(lane < experts, lane, lane - experts)
    table = jnp.zeros(lane.shape, jnp.float32)
    for k in range(ids.shape[1]):
        table += jnp.where(expert == ids[:, k : k + 1], shares[:, k : k + 1], 0.0)
    high = table.astype(jnp.bfloat16).astype(jnp.float32)
    table = jnp.where(lane < experts, high, jnp.where(lane < 2 * experts, table - high, 0.0))
    out_ref[:, width:] = table.astype(jnp.bfloat16)
    copies[0].wait()
    out_ref[:, :width] = rows_ref[...]


def pack(experts, moe_rows, route_ids, route_gates):
    rows, width = moe_rows.shape
    sources = (moe_rows, route_ids, route_gates)
    return pl.pallas_call(
        functools.partial(pack_kernel, experts),
        in_specs=[pl.BlockSpec(memory_space=pltpu.HBM)] * 3,
        out_specs=pl.BlockSpec(memory_space=pltpu.VMEM),
        scratch_shapes=[pltpu.VMEM(source.shape, source.dtype) for source in sources]
        + [pltpu.SemaphoreType.DMA((3,))],
        out_shape=jax.ShapeDtypeStruct((rows, width + table_width(experts)), jnp.bfloat16),
        compiler_params=pltpu.CompilerParams(vmem_limit_bytes=4 * MEBI),
        name="pack",
    )(*[in_hbm(source) for source in sources])


def spread(product, outs):
    start = 0
    for out, columns in outs:
        size = out.shape[0]
        out[:, columns] = product[start : start + size]
        start += size


def fetch_columns(source, target, sems):
    columns = target.shape[1] // sems.shape[0]
    copies = []
    for k in range(sems.shape[0]):
        part = pl.ds(k * columns, columns)
        copies.append(pltpu.make_async_copy(source.at[:, part], target.at[:, part], sems.at[k]))
        copies[-1].start()
    return copies


def fetch_both(gate_hbm, up_hbm, gate, up, gate_sem, up_sem, tile):
    copies = []
    for k in range(0, gate.shape[0], tile):
        part = pl.ds(k, tile)
        pair = (
            pltpu.make_async_copy(gate_hbm.at[part], gate.at[part], gate_sem.at[k // tile]),
            pltpu.make_async_copy(up_hbm.at[part], up.at[part], up_sem.at[k // tile]),
        )
        for copy in pair:
            copy.start()
        copies.append(pair)
    return copies


def project(blocks, copies, gate, up, gate_sum, up_sum, tile):
    for k, pair in enumerate(copies):
        part = pl.ds(k * tile, tile)
        rows = jnp.concatenate([block[:, part] for block in blocks], axis=0)
        for copy, weight, total in zip(pair, (gate, up), (gate_sum, up_sum)):
            copy.wait()
            product = jnp.dot(rows, weight[part], preferred_element_type=jnp.float32)
            if k == 0:
                total[...] = product
            else:
                total[...] += product


def expert_kernel(count, experts, tile, down_tile, split, node_ref, *refs):
    blocks = refs[:count]
    gate_hbm, up_hbm, down_hbm = refs[count : count + 3]
    outs = refs[count + 3 : -10]
    hidden_ref, share_ref, gate, up, down, gate_sum, up_sum, gate_sem, up_sem, down_sem = refs[-10:]
    copies = fetch_both(gate_hbm, up_hbm, gate, up, gate_sem, up_sem, tile)
    down_copies = fetch_columns(down_hbm, down, down_sem)

    table = jnp.concatenate([block[:, gate.shape[0] :] for block in blocks], axis=0)
    table = table.astype(jnp.float32)
    lane = lax.broadcasted_iota(jnp.int32, table.shape, 1)
    mine = (lane == node_ref[0]) | (lane == node_ref[0] + experts)
    share = jnp.sum(jnp.where(mine, table, 0.0), axis=1, keepdims=True)
    share_ref[...] = jnp.broadcast_to(share, share_ref.shape)
    project(blocks, copies, gate, up, gate_sum, up_sum, tile)
    hidden_ref[...] = (jax.nn.silu(gate_sum[...]) * up_sum[...]).astype(jnp.bfloat16)
    wide = down.shape[1] // len(down_copies)
    for k in range(0, down.shape[1], down_tile):
        if k % wide == 0:
            down_copies[k // wide].wait()
        product = jnp.dot(
            hidden_ref[...], down[:, pl.ds(k, down_tile)], preferred_element_type=jnp.float32
        )
        product = (product * share_ref[:, :1]).astype(jnp.bfloat16)
        if k < split:
            spread(product, [(out, pl.ds(k, down_tile)) for out in outs[: len(outs) // 2]])
        else:
            spread(product, [(out, pl.ds(k - split, down_tile)) for out in outs[len(outs) // 2 :]])


def expert(blocks, w_gate, w_up, w_down, experts, node, sizes, split):
    width, units = w_gate.shape
    rows = sum(sizes)
    tile, down_tile = 1024, 512
    return pl.pallas_call(
        functools.partial(expert_kernel, len(blocks), experts, tile, down_tile, split),
        in_specs=[pl.BlockSpec(memory_space=pltpu.SMEM)]
        + [pl.BlockSpec(memory_space=pltpu.VMEM)] * len(blocks)
        + [pl.BlockSpec(memory_space=pltpu.HBM)] * 3,
        out_specs=[pl.BlockSpec(memory_space=pltpu.VMEM)] * (2 * len(sizes)),
        out_shape=[
            jax.ShapeDtypeStruct((size, chunk), jnp.bfloat16)
            for chunk in (split, width - split)
            for size in sizes
        ],
        scratch_shapes=[
            pltpu.VMEM((rows, units), jnp.bfloat16),
            pltpu.VMEM((rows, 128), jnp.float32),
            pltpu.VMEM((width, units), jnp.bfloat16),
            pltpu.VMEM((width, units), jnp.bfloat16),
            pltpu.VMEM((units, width), jnp.bfloat16),
            pltpu.VMEM((rows, units), jnp.float32),
            pltpu.VMEM((rows, units), jnp.float32),
            pltpu.SemaphoreType.DMA((width // tile,)),
            pltpu.SemaphoreType.DMA((width // tile,)),
            pltpu.SemaphoreType.DMA((width // (2 * down_tile),)),
        ],
        cost_estimate=pl.CostEstimate(
            flops=6 * rows * width * units,
            bytes_accessed=6 * units * width,
            transcendentals=rows * units,
        ),
        compiler_params=pltpu.CompilerParams(vmem_limit_bytes=32 * MEBI),
        name="expert",
    )(node, *blocks, in_hbm(w_gate), in_hbm(w_up), in_hbm(w_down))


def body(
    moe_rows,
    route_ids,
    route_gates,
    w_gate,
    w_up,
    w_down,
    query_latent,
    query_rope,
    cache_latent,
    cache_rope,
    cache_lengths,
):
    grid = Grid()
    high, middle, cores, _ = grid.sizes
    experts = high * middle * cores
    tokens, width = moe_rows.shape
    node = lax.axis_index(("high", "middle", "core")).astype(jnp.int32).reshape(1)
    tied = lax.optimization_barrier
    attn_latent = attention(query_latent, query_rope, cache_latent, cache_rope, cache_lengths)

    outgoing = pack(experts, moe_rows, route_ids, route_gates)
    masks = grid.masks()
    came = grid.swap(outgoing, grid.high, masks[0])
    near = grid.near(join(grid.lines(outgoing, masks[1:])))
    far = grid.far(near[:-1])
    lines = grid.lines(came, masks[1:])
    lines[-1], near[-1], far[0] = tied((lines[-1], near[-1], far[0]))
    later_near = grid.near(join(lines))
    later_far = grid.far(later_near[:-1])
    early = grid.other(near + far)
    far += grid.far(near[-1:])
    far[-1], later_near[-1], later_far[0], early, attn_latent = tied(
        (far[-1], later_near[-1], later_far[0], early, attn_latent)
    )
    rows = later_near[-1].shape[0] // 2
    last = grid.far([later_near[-1][:rows], later_near[-1][rows:]])
    mine = [[block] for block in near + far]
    for place, block in zip(mine, later_near + later_far):
        place.append(block)
    mine[-1] += last
    other = [[block] + grid.other(place[1:]) for block, place in zip(early, mine)]
    other.append(grid.other(mine[-1]))
    size, count = high * tokens, len(mine)
    sizes = [size] * count + [size, size * (count - 1)]
    split = width // 2
    places = mine + other[-1:] + other[:-1]
    products = expert(
        [block for place in places for block in place],
        w_gate[0],
        w_up[0],
        w_down[0],
        experts,
        node,
        sizes,
        split,
    )

    def returned(parts, together):
        last = grid.last_sum(parts[:count], parts[count:])
        sums = grid.rest_sums(parts[:count], parts[count:]) + [last]
        came = [grid.back(sums, place) for place in range(count // 2, count)]
        if together:
            came = tied(came)
        return grid.high_sum(grid.line_sum(sums[: count // 2], came))

    head = returned(products[: len(sizes)], False)
    tail = returned(products[len(sizes) :], True)
    return (jnp.concatenate([head, tail], axis=1), attn_latent)


def solution(mesh):
    groups, nodes, local = mesh.devices.shape
    split = Mesh(mesh.devices.reshape(groups, nodes // 4, 2, 2, local), ("group",) + everyone)
    node = ("high", "middle", "core")
    whole = ("group",) + everyone
    rows = P(whole, None)
    blocks = P(whole, None, None)
    return jax.shard_map(
        body,
        mesh=split,
        in_specs=(
            rows,
            rows,
            rows,
            P(node, None, "local"),
            P(node, None, "local"),
            P(node, "local", None),
            blocks,
            blocks,
            blocks,
            blocks,
            P(whole),
        ),
        out_specs=(rows, blocks),
        check_vma=False,
    )
```

```python
import functools

import jax
import jax.numpy as jnp
import numpy as np
from jax import lax
from jax.experimental import pallas as pl
from jax.experimental.pallas import tpu as pltpu
from jax.sharding import Mesh
from jax.sharding import PartitionSpec as P

score_scale = 192.0 ** (-0.5)
everyone = ("high", "middle", "core", "local")
MEBI = 1024 * 1024


def attention_kernel(lengths_ref, *refs):
    sources, (out_ref, *targets), sems = refs[:4], refs[4:-1], refs[-1]
    query_ref, query_rope_ref, cache_ref, cache_rope_ref = targets
    copies = []
    for row in range(out_ref.shape[0]):
        copies.append(
            [
                pltpu.make_async_copy(source.at[row], target.at[row], sems.at[row, i])
                for i, (source, target) in enumerate(zip(sources, targets))
            ]
        )
        for copy in copies[-1]:
            copy.start()
    for row in range(out_ref.shape[0]):
        for copy in copies[row]:
            copy.wait()
        cache = cache_ref[row]
        scores = lax.dot_general(
            query_ref[row], cache, (((1,), (1,)), ((), ())), preferred_element_type=jnp.float32
        )
        scores += jnp.dot(
            query_rope_ref[row], cache_rope_ref[row], preferred_element_type=jnp.float32
        )
        slot = lax.broadcasted_iota(jnp.int32, scores.shape, 1)
        in_range = slot < lengths_ref[row]
        scores = jnp.where(in_range, scores * score_scale, -jnp.inf)
        row_peak = jnp.max(scores, axis=1, keepdims=True)
        lifted = jnp.where(in_range, jnp.exp(scores - row_peak), 0.0)
        weights = (lifted / jnp.sum(lifted, axis=1, keepdims=True)).astype(jnp.bfloat16)
        value = jnp.dot(weights, cache, preferred_element_type=jnp.float32)
        out_ref[row] = value.astype(jnp.bfloat16)


def attention(query_latent, query_rope, cache_latent, cache_rope, cache_lengths):
    rows, heads, latent = query_latent.shape
    slots = cache_latent.shape[1]
    sources = (query_latent, query_rope, cache_latent, cache_rope)
    return pl.pallas_call(
        attention_kernel,
        in_specs=[pl.BlockSpec(memory_space=pltpu.SMEM)]
        + [pl.BlockSpec(memory_space=pltpu.HBM)] * 4,
        out_specs=pl.BlockSpec(memory_space=pltpu.VMEM),
        out_shape=jax.ShapeDtypeStruct(query_latent.shape, jnp.bfloat16),
        scratch_shapes=[pltpu.VMEM(source.shape, source.dtype) for source in sources]
        + [pltpu.SemaphoreType.DMA((rows, 4))],
        cost_estimate=pl.CostEstimate(
            flops=4 * rows * heads * slots * latent,
            bytes_accessed=2 * rows * slots * latent,
            transcendentals=rows * heads * slots,
        ),
        compiler_params=pltpu.CompilerParams(vmem_limit_bytes=8 * MEBI),
        name="attention",
    )(cache_lengths, *[in_hbm(source) for source in sources])


def in_hbm(array):
    return pltpu.with_memory_space_constraint(array, pltpu.HBM)


class Grid:
    def __init__(self):
        self.sizes = tuple(lax.axis_size(name) for name in everyone)
        self.mixed = self.sizes[1] == self.sizes[3]

    def swap(self, value, pick, mask):
        pairs = []
        for place in np.ndindex(*self.sizes):
            other = list(place)
            other[pick(place[2])] ^= mask
            pairs.append(
                (
                    int(np.ravel_multi_index(place, self.sizes)),
                    int(np.ravel_multi_index(other, self.sizes)),
                )
            )
        return lax.ppermute(value, everyone, pairs)

    def high(self, core):
        return 0

    def core(self, core):
        return 2

    def first(self, core):
        return 1 if self.mixed and core == 1 else 3

    def second(self, core):
        return 3 if self.mixed and core == 1 else 1

    def extent(self, pick):
        return self.sizes[pick(0)]

    def masks(self):
        masks, m = [], self.extent(self.high) // 2
        while m:
            masks.append(m)
            m //= 2
        return masks

    def lines(self, rows, masks):
        if not masks:
            return [rows]
        came = self.swap(rows, self.high, masks[0])
        return self.lines(rows, masks[1:]) + self.lines(came, masks[1:])

    def near(self, line):
        return [line] + [self.swap(line, self.first, m) for m in range(1, self.extent(self.first))]

    def far(self, near):
        return [self.swap(block, self.second, 1) for block in near]

    def other(self, mine):
        return [self.swap(block, self.core, 1) for block in mine]

    def last_sum(self, mine, other):
        return add([mine[-1], self.swap(other[0], self.core, 1)])

    def rest_sums(self, mine, other):
        size = mine[0].shape[0]
        rest = self.swap(other[1], self.core, 1)
        return [
            add([part, rest[i * size : (i + 1) * size]]) for i, part in enumerate(mine[:-1])
        ]

    def back(self, sums, place):
        return self.swap(sums[place], self.second, place // self.extent(self.first))

    def line_sum(self, sums, last):
        wide = self.extent(self.first)
        near = [[part] for part in sums[:wide]]
        for place in range(wide, len(sums)):
            moved = last if place == len(sums) - 1 else self.back(sums, place)
            near[place % wide].append(moved)
        near = [add(parts) for parts in near]
        return add([near[0]] + [self.swap(near[m], self.first, m) for m in range(1, wide)])

    def high_sum(self, line):
        rows = line.shape[0] // self.extent(self.high)
        parts = [line[:rows]]
        for m in range(1, self.extent(self.high)):
            parts.append(self.swap(line[m * rows : (m + 1) * rows], self.high, m))
        return add(parts)


def add(parts):
    total = parts[0].astype(jnp.float32)
    for part in parts[1:]:
        total = total + part.astype(jnp.float32)
    return total.astype(parts[0].dtype)


def join_kernel(count, ranges, *refs):
    for out, parts in zip(refs[count:], ranges):
        start = 0
        for first, size in parts:
            columns = pl.ds(first, size)
            out[:, start : start + size] = jnp.concatenate(
                [ref[:, columns] for ref in refs[:count]], axis=0
            )
            start += size


def join(parts, *ranges):
    rows = sum(part.shape[0] for part in parts)
    ranges = ranges or ([(0, parts[0].shape[1])],)
    outs = pl.pallas_call(
        functools.partial(join_kernel, len(parts), ranges),
        in_specs=[pl.BlockSpec(memory_space=pltpu.VMEM)] * len(parts),
        out_specs=[pl.BlockSpec(memory_space=pltpu.VMEM)] * len(ranges),
        out_shape=[
            jax.ShapeDtypeStruct((rows, sum(size for _, size in columns)), parts[0].dtype)
            for columns in ranges
        ],
        compiler_params=pltpu.CompilerParams(vmem_limit_bytes=4 * MEBI),
        name="join",
    )(*parts)
    return outs if len(ranges) > 1 else outs[0]


def table_width(experts):
    return pl.cdiv(2 * experts, 128) * 128


def pack_kernel(experts, *refs):
    sources, (out_ref, *targets), sems = refs[:3], refs[3:-1], refs[-1]
    copies = [
        pltpu.make_async_copy(source, target, sems.at[i])
        for i, (source, target) in enumerate(zip(sources, targets))
    ]
    for copy in copies:
        copy.start()
    rows_ref, ids_ref, gates_ref = targets
    for copy in copies[1:]:
        copy.wait()
    extra = table_width(experts)
    width = rows_ref.shape[1]
    gates = gates_ref[...]
    shares = 2.5 * gates / jnp.sum(gates, axis=1, keepdims=True)
    ids = ids_ref[...]
    lane = lax.broadcasted_iota(jnp.int32, (ids.shape[0], extra), 1)
    expert = jnp.where(lane < experts, lane, lane - experts)
    table = jnp.zeros(lane.shape, jnp.float32)
    for k in range(ids.shape[1]):
        table += jnp.where(expert == ids[:, k : k + 1], shares[:, k : k + 1], 0.0)
    high = table.astype(jnp.bfloat16).astype(jnp.float32)
    table = jnp.where(lane < experts, high, jnp.where(lane < 2 * experts, table - high, 0.0))
    out_ref[:, width:] = table.astype(jnp.bfloat16)
    copies[0].wait()
    out_ref[:, :width] = rows_ref[...]


def pack(experts, moe_rows, route_ids, route_gates):
    rows, width = moe_rows.shape
    sources = (moe_rows, route_ids, route_gates)
    return pl.pallas_call(
        functools.partial(pack_kernel, experts),
        in_specs=[pl.BlockSpec(memory_space=pltpu.HBM)] * 3,
        out_specs=pl.BlockSpec(memory_space=pltpu.VMEM),
        scratch_shapes=[pltpu.VMEM(source.shape, source.dtype) for source in sources]
        + [pltpu.SemaphoreType.DMA((3,))],
        out_shape=jax.ShapeDtypeStruct((rows, width + table_width(experts)), jnp.bfloat16),
        compiler_params=pltpu.CompilerParams(vmem_limit_bytes=4 * MEBI),
        name="pack",
    )(*[in_hbm(source) for source in sources])


def spread(product, outs):
    start = 0
    for out, columns in outs:
        size = out.shape[0]
        out[:, columns] = product[start : start + size]
        start += size


def fetch_both(gate_hbm, up_hbm, gate, up, gate_sem, up_sem, tile):
    copies = []
    for k in range(0, gate.shape[0], tile):
        part = pl.ds(k, tile)
        pair = (
            pltpu.make_async_copy(gate_hbm.at[part], gate.at[part], gate_sem.at[k // tile]),
            pltpu.make_async_copy(up_hbm.at[part], up.at[part], up_sem.at[k // tile]),
        )
        for copy in pair:
            copy.start()
        copies.append(pair)
    return copies


def project(blocks, copies, gate, up, gate_sum, up_sum, tile):
    for k, pair in enumerate(copies):
        part = pl.ds(k * tile, tile)
        rows = jnp.concatenate([block[:, part] for block in blocks], axis=0)
        for copy, weight, total in zip(pair, (gate, up), (gate_sum, up_sum)):
            copy.wait()
            product = jnp.dot(rows, weight[part], preferred_element_type=jnp.float32)
            if k == 0:
                total[...] = product
            else:
                total[...] += product


def expert_kernel(count, experts, tile, down_tile, split, node_ref, *refs):
    blocks = refs[:count]
    gate_hbm, up_hbm, down = refs[count : count + 3]
    outs = refs[count + 3 : -8]
    hidden_ref, share_ref, gate, up, gate_sum, up_sum, gate_sem, up_sem = refs[-8:]
    copies = fetch_both(gate_hbm, up_hbm, gate, up, gate_sem, up_sem, tile)

    table = jnp.concatenate([block[:, gate.shape[0] :] for block in blocks], axis=0)
    table = table.astype(jnp.float32)
    lane = lax.broadcasted_iota(jnp.int32, table.shape, 1)
    mine = (lane == node_ref[0]) | (lane == node_ref[0] + experts)
    share = jnp.sum(jnp.where(mine, table, 0.0), axis=1, keepdims=True)
    share_ref[...] = jnp.broadcast_to(share, share_ref.shape)
    project(blocks, copies, gate, up, gate_sum, up_sum, tile)
    hidden_ref[...] = (jax.nn.silu(gate_sum[...]) * up_sum[...]).astype(jnp.bfloat16)
    for k in range(0, down.shape[1], down_tile):
        product = jnp.dot(
            hidden_ref[...], down[:, pl.ds(k, down_tile)], preferred_element_type=jnp.float32
        )
        product = (product * share_ref[:, :1]).astype(jnp.bfloat16)
        if k < split:
            spread(product, [(out, pl.ds(k, down_tile)) for out in outs[: len(outs) // 2]])
        else:
            spread(product, [(out, pl.ds(k - split, down_tile)) for out in outs[len(outs) // 2 :]])


def expert(blocks, w_gate, w_up, w_down, experts, node, sizes, split):
    width, units = w_gate.shape
    rows = sum(sizes)
    tile, down_tile = 1024, 512
    return pl.pallas_call(
        functools.partial(expert_kernel, len(blocks), experts, tile, down_tile, split),
        in_specs=[pl.BlockSpec(memory_space=pltpu.SMEM)]
        + [pl.BlockSpec(memory_space=pltpu.VMEM)] * len(blocks)
        + [pl.BlockSpec(memory_space=pltpu.HBM)] * 2
        + [pl.BlockSpec(memory_space=pltpu.VMEM)],
        out_specs=[pl.BlockSpec(memory_space=pltpu.VMEM)] * (2 * len(sizes)),
        out_shape=[
            jax.ShapeDtypeStruct((size, chunk), jnp.bfloat16)
            for chunk in (split, width - split)
            for size in sizes
        ],
        scratch_shapes=[
            pltpu.VMEM((rows, units), jnp.bfloat16),
            pltpu.VMEM((rows, 128), jnp.float32),
            pltpu.VMEM((width, units), jnp.bfloat16),
            pltpu.VMEM((width, units), jnp.bfloat16),
            pltpu.VMEM((rows, units), jnp.float32),
            pltpu.VMEM((rows, units), jnp.float32),
            pltpu.SemaphoreType.DMA((width // tile,)),
            pltpu.SemaphoreType.DMA((width // tile,)),
        ],
        cost_estimate=pl.CostEstimate(
            flops=6 * rows * width * units,
            bytes_accessed=6 * units * width,
            transcendentals=rows * units,
        ),
        compiler_params=pltpu.CompilerParams(vmem_limit_bytes=24 * MEBI),
        name="expert",
    )(node, *blocks, in_hbm(w_gate), in_hbm(w_up), w_down)


def body(
    moe_rows,
    route_ids,
    route_gates,
    w_gate,
    w_up,
    w_down,
    query_latent,
    query_rope,
    cache_latent,
    cache_rope,
    cache_lengths,
):
    grid = Grid()
    high, middle, cores, _ = grid.sizes
    experts = high * middle * cores
    tokens, width = moe_rows.shape
    node = lax.axis_index(("high", "middle", "core")).astype(jnp.int32).reshape(1)
    tied = lax.optimization_barrier
    attn_latent = attention(query_latent, query_rope, cache_latent, cache_rope, cache_lengths)

    outgoing = pack(experts, moe_rows, route_ids, route_gates)
    masks = grid.masks()
    came = grid.swap(outgoing, grid.high, masks[0])
    near = grid.near(join(grid.lines(outgoing, masks[1:])))
    far = grid.far(near[:-1])
    lines = grid.lines(came, masks[1:])
    lines[-1], near[-1], far[0] = tied((lines[-1], near[-1], far[0]))
    later_near = grid.near(join(lines))
    later_far = grid.far(later_near[:-1])
    far += grid.far(near[-1:])
    far[-1], later_near[-1], later_far[0], attn_latent = tied(
        (far[-1], later_near[-1], later_far[0], attn_latent)
    )
    rows = later_near[-1].shape[0] // 2
    last = grid.far([later_near[-1][:rows], later_near[-1][rows:]])
    mine = [[block] for block in near + far]
    for place, block in zip(mine, later_near + later_far):
        place.append(block)
    mine[-1] += last
    other = [grid.other(place) for place in mine]
    size, count = high * tokens, len(mine)
    sizes = [size] * count + [size, size * (count - 1)]
    split = width // 2
    places = mine + other[-1:] + other[:-1]
    products = expert(
        [block for place in places for block in place],
        w_gate[0],
        w_up[0],
        w_down[0],
        experts,
        node,
        sizes,
        split,
    )

    def returned(parts):
        last = grid.last_sum(parts[:count], parts[count:])
        sums = grid.rest_sums(parts[:count], parts[count:]) + [last]
        return grid.high_sum(grid.line_sum(sums, grid.back(sums, count - 1)))

    head, tail = returned(products[: len(sizes)]), returned(products[len(sizes) :])
    return (jnp.concatenate([head, tail], axis=1), attn_latent)


def solution(mesh):
    groups, nodes, local = mesh.devices.shape
    split = Mesh(mesh.devices.reshape(groups, nodes // 4, 2, 2, local), ("group",) + everyone)
    node = ("high", "middle", "core")
    whole = ("group",) + everyone
    rows = P(whole, None)
    blocks = P(whole, None, None)
    return jax.shard_map(
        body,
        mesh=split,
        in_specs=(
            rows,
            rows,
            rows,
            P(node, None, "local"),
            P(node, None, "local"),
            P(node, "local", None),
            blocks,
            blocks,
            blocks,
            blocks,
            P(whole),
        ),
        out_specs=(rows, blocks),
        check_vma=False,
    )
```

```python
import functools

import jax
import jax.numpy as jnp
import numpy as np
from jax import lax
from jax.experimental import pallas as pl
from jax.experimental.pallas import tpu as pltpu
from jax.sharding import Mesh
from jax.sharding import PartitionSpec as P

score_scale = 192.0 ** (-0.5)
everyone = ("high", "middle", "core", "local")
MEBI = 1024 * 1024


def attention_kernel(lengths_ref, *refs):
    sources, (out_ref, *targets), sems = refs[:4], refs[4:-1], refs[-1]
    query_ref, query_rope_ref, cache_ref, cache_rope_ref = targets
    copies = []
    for row in range(out_ref.shape[0]):
        copies.append(
            [
                pltpu.make_async_copy(source.at[row], target.at[row], sems.at[row, i])
                for i, (source, target) in enumerate(zip(sources, targets))
            ]
        )
        for copy in copies[-1]:
            copy.start()
    for row in range(out_ref.shape[0]):
        for copy in copies[row]:
            copy.wait()
        cache = cache_ref[row]
        scores = lax.dot_general(
            query_ref[row], cache, (((1,), (1,)), ((), ())), preferred_element_type=jnp.float32
        )
        scores += jnp.dot(
            query_rope_ref[row], cache_rope_ref[row], preferred_element_type=jnp.float32
        )
        slot = lax.broadcasted_iota(jnp.int32, scores.shape, 1)
        in_range = slot < lengths_ref[row]
        scores = jnp.where(in_range, scores * score_scale, -jnp.inf)
        row_peak = jnp.max(scores, axis=1, keepdims=True)
        lifted = jnp.where(in_range, jnp.exp(scores - row_peak), 0.0)
        weights = (lifted / jnp.sum(lifted, axis=1, keepdims=True)).astype(jnp.bfloat16)
        value = jnp.dot(weights, cache, preferred_element_type=jnp.float32)
        out_ref[row] = value.astype(jnp.bfloat16)


def attention(query_latent, query_rope, cache_latent, cache_rope, cache_lengths):
    rows, heads, latent = query_latent.shape
    slots = cache_latent.shape[1]
    sources = (query_latent, query_rope, cache_latent, cache_rope)
    return pl.pallas_call(
        attention_kernel,
        in_specs=[pl.BlockSpec(memory_space=pltpu.SMEM)]
        + [pl.BlockSpec(memory_space=pltpu.HBM)] * 4,
        out_specs=pl.BlockSpec(memory_space=pltpu.VMEM),
        out_shape=jax.ShapeDtypeStruct(query_latent.shape, jnp.bfloat16),
        scratch_shapes=[pltpu.VMEM(source.shape, source.dtype) for source in sources]
        + [pltpu.SemaphoreType.DMA((rows, 4))],
        cost_estimate=pl.CostEstimate(
            flops=4 * rows * heads * slots * latent,
            bytes_accessed=2 * rows * slots * latent,
            transcendentals=rows * heads * slots,
        ),
        compiler_params=pltpu.CompilerParams(vmem_limit_bytes=8 * MEBI),
        name="attention",
    )(cache_lengths, *[in_hbm(source) for source in sources])


def in_hbm(array):
    return pltpu.with_memory_space_constraint(array, pltpu.HBM)


class Grid:
    def __init__(self):
        self.sizes = tuple(lax.axis_size(name) for name in everyone)
        self.mixed = self.sizes[1] == self.sizes[3]

    def swap(self, value, pick, mask):
        pairs = []
        for place in np.ndindex(*self.sizes):
            other = list(place)
            other[pick(place[2])] ^= mask
            pairs.append(
                (
                    int(np.ravel_multi_index(place, self.sizes)),
                    int(np.ravel_multi_index(other, self.sizes)),
                )
            )
        return lax.ppermute(value, everyone, pairs)

    def high(self, core):
        return 0

    def core(self, core):
        return 2

    def first(self, core):
        return 1 if self.mixed and core == 1 else 3

    def second(self, core):
        return 3 if self.mixed and core == 1 else 1

    def extent(self, pick):
        return self.sizes[pick(0)]

    def masks(self):
        masks, m = [], self.extent(self.high) // 2
        while m:
            masks.append(m)
            m //= 2
        return masks

    def lines(self, rows, masks):
        if not masks:
            return [rows]
        came = self.swap(rows, self.high, masks[0])
        return self.lines(rows, masks[1:]) + self.lines(came, masks[1:])

    def near(self, line):
        return [line] + [self.swap(line, self.first, m) for m in range(1, self.extent(self.first))]

    def far(self, near):
        return [self.swap(block, self.second, 1) for block in near]

    def other(self, mine):
        return [self.swap(block, self.core, 1) for block in mine]

    def last_sum(self, mine, other):
        return add([mine[-1], self.swap(other[0], self.core, 1)])

    def rest_sums(self, mine, other):
        size = mine[0].shape[0]
        rest = self.swap(other[1], self.core, 1)
        return [
            add([part, rest[i * size : (i + 1) * size]]) for i, part in enumerate(mine[:-1])
        ]

    def back(self, sums, place):
        return self.swap(sums[place], self.second, place // self.extent(self.first))

    def line_sum(self, sums, last):
        wide = self.extent(self.first)
        near = [[part] for part in sums[:wide]]
        for place in range(wide, len(sums)):
            moved = last if place == len(sums) - 1 else self.back(sums, place)
            near[place % wide].append(moved)
        near = [add(parts) for parts in near]
        return add([near[0]] + [self.swap(near[m], self.first, m) for m in range(1, wide)])

    def high_sum(self, line):
        rows = line.shape[0] // self.extent(self.high)
        parts = [line[:rows]]
        for m in range(1, self.extent(self.high)):
            parts.append(self.swap(line[m * rows : (m + 1) * rows], self.high, m))
        return add(parts)


def add(parts):
    total = parts[0].astype(jnp.float32)
    for part in parts[1:]:
        total = total + part.astype(jnp.float32)
    return total.astype(parts[0].dtype)


def join_kernel(count, ranges, *refs):
    for out, parts in zip(refs[count:], ranges):
        start = 0
        for first, size in parts:
            columns = pl.ds(first, size)
            out[:, start : start + size] = jnp.concatenate(
                [ref[:, columns] for ref in refs[:count]], axis=0
            )
            start += size


def join(parts, *ranges):
    rows = sum(part.shape[0] for part in parts)
    ranges = ranges or ([(0, parts[0].shape[1])],)
    outs = pl.pallas_call(
        functools.partial(join_kernel, len(parts), ranges),
        in_specs=[pl.BlockSpec(memory_space=pltpu.VMEM)] * len(parts),
        out_specs=[pl.BlockSpec(memory_space=pltpu.VMEM)] * len(ranges),
        out_shape=[
            jax.ShapeDtypeStruct((rows, sum(size for _, size in columns)), parts[0].dtype)
            for columns in ranges
        ],
        compiler_params=pltpu.CompilerParams(vmem_limit_bytes=4 * MEBI),
        name="join",
    )(*parts)
    return outs if len(ranges) > 1 else outs[0]


def table_width(experts):
    return pl.cdiv(2 * experts, 128) * 128


def pack_kernel(experts, *refs):
    sources, (out_ref, *targets), sems = refs[:3], refs[3:-1], refs[-1]
    copies = [
        pltpu.make_async_copy(source, target, sems.at[i])
        for i, (source, target) in enumerate(zip(sources, targets))
    ]
    for copy in copies:
        copy.start()
    rows_ref, ids_ref, gates_ref = targets
    for copy in copies[1:]:
        copy.wait()
    extra = table_width(experts)
    width = rows_ref.shape[1]
    gates = gates_ref[...]
    shares = 2.5 * gates / jnp.sum(gates, axis=1, keepdims=True)
    ids = ids_ref[...]
    lane = lax.broadcasted_iota(jnp.int32, (ids.shape[0], extra), 1)
    expert = jnp.where(lane < experts, lane, lane - experts)
    table = jnp.zeros(lane.shape, jnp.float32)
    for k in range(ids.shape[1]):
        table += jnp.where(expert == ids[:, k : k + 1], shares[:, k : k + 1], 0.0)
    high = table.astype(jnp.bfloat16).astype(jnp.float32)
    table = jnp.where(lane < experts, high, jnp.where(lane < 2 * experts, table - high, 0.0))
    out_ref[:, width:] = table.astype(jnp.bfloat16)
    copies[0].wait()
    out_ref[:, :width] = rows_ref[...]


def pack(experts, moe_rows, route_ids, route_gates):
    rows, width = moe_rows.shape
    sources = (moe_rows, route_ids, route_gates)
    return pl.pallas_call(
        functools.partial(pack_kernel, experts),
        in_specs=[pl.BlockSpec(memory_space=pltpu.HBM)] * 3,
        out_specs=pl.BlockSpec(memory_space=pltpu.VMEM),
        scratch_shapes=[pltpu.VMEM(source.shape, source.dtype) for source in sources]
        + [pltpu.SemaphoreType.DMA((3,))],
        out_shape=jax.ShapeDtypeStruct((rows, width + table_width(experts)), jnp.bfloat16),
        compiler_params=pltpu.CompilerParams(vmem_limit_bytes=4 * MEBI),
        name="pack",
    )(*[in_hbm(source) for source in sources])


def spread(product, outs):
    start = 0
    for out, columns in outs:
        size = out.shape[0]
        out[:, columns] = product[start : start + size]
        start += size


def fetch_columns(source, target, sems, tile):
    copies = []
    for k in range(sems.shape[0]):
        part = pl.ds(k * tile, min(tile, target.shape[1] - k * tile))
        copies.append(pltpu.make_async_copy(source.at[:, part], target.at[:, part], sems.at[k]))
        copies[-1].start()
    return copies


def fetch_both(gate_hbm, up_hbm, gate, up, gate_sem, up_sem, tile):
    copies = []
    for k in range(0, gate.shape[0], tile):
        part = pl.ds(k, tile)
        pair = (
            pltpu.make_async_copy(gate_hbm.at[part], gate.at[part], gate_sem.at[k // tile]),
            pltpu.make_async_copy(up_hbm.at[part], up.at[part], up_sem.at[k // tile]),
        )
        for copy in pair:
            copy.start()
        copies.append(pair)
    return copies


def project(blocks, copies, gate, up, gate_sum, up_sum, tile):
    for k, pair in enumerate(copies):
        part = pl.ds(k * tile, tile)
        rows = jnp.concatenate([block[:, part] for block in blocks], axis=0)
        for copy, weight, total in zip(pair, (gate, up), (gate_sum, up_sum)):
            copy.wait()
            product = jnp.dot(rows, weight[part], preferred_element_type=jnp.float32)
            if k == 0:
                total[...] = product
            else:
                total[...] += product


def expert_kernel(count, experts, tile, down_tile, split, node_ref, *refs):
    blocks = refs[:count]
    gate_hbm, up_hbm, down_hbm = refs[count : count + 3]
    outs = refs[count + 3 : -10]
    hidden_ref, share_ref, gate, up, down, gate_sum, up_sum, gate_sem, up_sem, down_sem = refs[-10:]
    copies = fetch_both(gate_hbm, up_hbm, gate, up, gate_sem, up_sem, tile)
    wide = 4 * down_tile
    down_copies = fetch_columns(down_hbm, down, down_sem, wide)

    table = jnp.concatenate([block[:, gate.shape[0] :] for block in blocks], axis=0)
    table = table.astype(jnp.float32)
    lane = lax.broadcasted_iota(jnp.int32, table.shape, 1)
    mine = (lane == node_ref[0]) | (lane == node_ref[0] + experts)
    share = jnp.sum(jnp.where(mine, table, 0.0), axis=1, keepdims=True)
    share_ref[...] = jnp.broadcast_to(share, share_ref.shape)
    project(blocks, copies, gate, up, gate_sum, up_sum, tile)
    hidden_ref[...] = (jax.nn.silu(gate_sum[...]) * up_sum[...]).astype(jnp.bfloat16)
    for k in range(0, down.shape[1], down_tile):
        if k % wide == 0:
            down_copies[k // wide].wait()
        product = jnp.dot(
            hidden_ref[...], down[:, pl.ds(k, down_tile)], preferred_element_type=jnp.float32
        )
        product = (product * share_ref[:, :1]).astype(jnp.bfloat16)
        if k < split:
            spread(product, [(out, pl.ds(k, down_tile)) for out in outs[: len(outs) // 2]])
        else:
            spread(product, [(out, pl.ds(k - split, down_tile)) for out in outs[len(outs) // 2 :]])


def expert(blocks, w_gate, w_up, w_down, experts, node, sizes, split):
    width, units = w_gate.shape
    rows = sum(sizes)
    tile, down_tile = 1024, 512
    return pl.pallas_call(
        functools.partial(expert_kernel, len(blocks), experts, tile, down_tile, split),
        in_specs=[pl.BlockSpec(memory_space=pltpu.SMEM)]
        + [pl.BlockSpec(memory_space=pltpu.VMEM)] * len(blocks)
        + [pl.BlockSpec(memory_space=pltpu.HBM)] * 3,
        out_specs=[pl.BlockSpec(memory_space=pltpu.VMEM)] * (2 * len(sizes)),
        out_shape=[
            jax.ShapeDtypeStruct((size, chunk), jnp.bfloat16)
            for chunk in (split, width - split)
            for size in sizes
        ],
        scratch_shapes=[
            pltpu.VMEM((rows, units), jnp.bfloat16),
            pltpu.VMEM((rows, 128), jnp.float32),
            pltpu.VMEM((width, units), jnp.bfloat16),
            pltpu.VMEM((width, units), jnp.bfloat16),
            pltpu.VMEM((units, width), jnp.bfloat16),
            pltpu.VMEM((rows, units), jnp.float32),
            pltpu.VMEM((rows, units), jnp.float32),
            pltpu.SemaphoreType.DMA((width // tile,)),
            pltpu.SemaphoreType.DMA((width // tile,)),
            pltpu.SemaphoreType.DMA((pl.cdiv(width, 4 * down_tile),)),
        ],
        cost_estimate=pl.CostEstimate(
            flops=6 * rows * width * units,
            bytes_accessed=6 * units * width,
            transcendentals=rows * units,
        ),
        compiler_params=pltpu.CompilerParams(vmem_limit_bytes=32 * MEBI),
        name="expert",
    )(node, *blocks, in_hbm(w_gate), in_hbm(w_up), in_hbm(w_down))


def body(
    moe_rows,
    route_ids,
    route_gates,
    w_gate,
    w_up,
    w_down,
    query_latent,
    query_rope,
    cache_latent,
    cache_rope,
    cache_lengths,
):
    grid = Grid()
    high, middle, cores, _ = grid.sizes
    experts = high * middle * cores
    tokens, width = moe_rows.shape
    node = lax.axis_index(("high", "middle", "core")).astype(jnp.int32).reshape(1)
    tied = lax.optimization_barrier
    attn_latent = attention(query_latent, query_rope, cache_latent, cache_rope, cache_lengths)

    outgoing = pack(experts, moe_rows, route_ids, route_gates)
    masks = grid.masks()
    came = grid.swap(outgoing, grid.high, masks[0])
    near = grid.near(join(grid.lines(outgoing, masks[1:])))
    far = grid.far(near[:-1])
    lines = grid.lines(came, masks[1:])
    lines[-1], near[-1], far[0] = tied((lines[-1], near[-1], far[0]))
    later_near = grid.near(join(lines))
    later_far = grid.far(later_near[:-1])
    far += grid.far(near[-1:])
    far[-1], later_near[-1], later_far[0], attn_latent = tied(
        (far[-1], later_near[-1], later_far[0], attn_latent)
    )
    rows = later_near[-1].shape[0] // 2
    last = grid.far([later_near[-1][:rows]])
    last.append(grid.swap(later_far[0][rows:], grid.first, grid.extent(grid.first) - 1))
    mine = [[block] for block in near + far]
    for place, block in zip(mine, later_near + later_far):
        place.append(block)
    mine[-1] += last
    other = [grid.other(place) for place in mine]
    size, count = high * tokens, len(mine)
    sizes = [size] * count + [size, size * (count - 1)]
    split = width * 4 // 7
    places = mine + other[-1:] + other[:-1]
    products = expert(
        [block for place in places for block in place],
        w_gate[0],
        w_up[0],
        w_down[0],
        experts,
        node,
        sizes,
        split,
    )

    def returned(parts):
        last = grid.last_sum(parts[:count], parts[count:])
        sums = grid.rest_sums(parts[:count], parts[count:]) + [last]
        return grid.high_sum(grid.line_sum(sums, grid.back(sums, count - 1)))

    head, tail = returned(products[: len(sizes)]), returned(products[len(sizes) :])
    return (jnp.concatenate([head, tail], axis=1), attn_latent)


def solution(mesh):
    groups, nodes, local = mesh.devices.shape
    split = Mesh(mesh.devices.reshape(groups, nodes // 4, 2, 2, local), ("group",) + everyone)
    node = ("high", "middle", "core")
    whole = ("group",) + everyone
    rows = P(whole, None)
    blocks = P(whole, None, None)
    return jax.shard_map(
        body,
        mesh=split,
        in_specs=(
            rows,
            rows,
            rows,
            P(node, None, "local"),
            P(node, None, "local"),
            P(node, "local", None),
            blocks,
            blocks,
            blocks,
            blocks,
            P(whole),
        ),
        out_specs=(rows, blocks),
        check_vma=False,
    )
```

```python
import functools

import jax
import jax.numpy as jnp
import numpy as np
from jax import lax
from jax.experimental import pallas as pl
from jax.experimental.pallas import tpu as pltpu
from jax.sharding import Mesh
from jax.sharding import PartitionSpec as P

score_scale = 192.0 ** (-0.5)
everyone = ("high", "middle", "core", "local")
MEBI = 1024 * 1024


def attention_kernel(lengths_ref, *refs):
    sources, (out_ref, *targets), sems = refs[:4], refs[4:-1], refs[-1]
    query_ref, query_rope_ref, cache_ref, cache_rope_ref = targets
    copies = []
    for row in range(out_ref.shape[0]):
        copies.append(
            [
                pltpu.make_async_copy(source.at[row], target.at[row], sems.at[row, i])
                for i, (source, target) in enumerate(zip(sources, targets))
            ]
        )
        for copy in copies[-1]:
            copy.start()
    for row in range(out_ref.shape[0]):
        for copy in copies[row]:
            copy.wait()
        cache = cache_ref[row]
        scores = lax.dot_general(
            query_ref[row], cache, (((1,), (1,)), ((), ())), preferred_element_type=jnp.float32
        )
        scores += jnp.dot(
            query_rope_ref[row], cache_rope_ref[row], preferred_element_type=jnp.float32
        )
        slot = lax.broadcasted_iota(jnp.int32, scores.shape, 1)
        in_range = slot < lengths_ref[row]
        scores = jnp.where(in_range, scores * score_scale, -jnp.inf)
        row_peak = jnp.max(scores, axis=1, keepdims=True)
        lifted = jnp.where(in_range, jnp.exp(scores - row_peak), 0.0)
        weights = (lifted / jnp.sum(lifted, axis=1, keepdims=True)).astype(jnp.bfloat16)
        value = jnp.dot(weights, cache, preferred_element_type=jnp.float32)
        out_ref[row] = value.astype(jnp.bfloat16)


def attention(query_latent, query_rope, cache_latent, cache_rope, cache_lengths):
    rows, heads, latent = query_latent.shape
    slots = cache_latent.shape[1]
    sources = (query_latent, query_rope, cache_latent, cache_rope)
    return pl.pallas_call(
        attention_kernel,
        in_specs=[pl.BlockSpec(memory_space=pltpu.SMEM)]
        + [pl.BlockSpec(memory_space=pltpu.HBM)] * 4,
        out_specs=pl.BlockSpec(memory_space=pltpu.VMEM),
        out_shape=jax.ShapeDtypeStruct(query_latent.shape, jnp.bfloat16),
        scratch_shapes=[pltpu.VMEM(source.shape, source.dtype) for source in sources]
        + [pltpu.SemaphoreType.DMA((rows, 4))],
        cost_estimate=pl.CostEstimate(
            flops=4 * rows * heads * slots * latent,
            bytes_accessed=2 * rows * slots * latent,
            transcendentals=rows * heads * slots,
        ),
        compiler_params=pltpu.CompilerParams(vmem_limit_bytes=8 * MEBI),
        name="attention",
    )(cache_lengths, *[in_hbm(source) for source in sources])


def in_hbm(array):
    return pltpu.with_memory_space_constraint(array, pltpu.HBM)


class Grid:
    def __init__(self):
        self.sizes = tuple(lax.axis_size(name) for name in everyone)
        self.mixed = self.sizes[1] == self.sizes[3]

    def swap(self, value, pick, mask):
        pairs = []
        for place in np.ndindex(*self.sizes):
            other = list(place)
            other[pick(place[2])] ^= mask
            pairs.append(
                (
                    int(np.ravel_multi_index(place, self.sizes)),
                    int(np.ravel_multi_index(other, self.sizes)),
                )
            )
        return lax.ppermute(value, everyone, pairs)

    def high(self, core):
        return 0

    def core(self, core):
        return 2

    def first(self, core):
        return 1 if self.mixed and core == 1 else 3

    def second(self, core):
        return 3 if self.mixed and core == 1 else 1

    def extent(self, pick):
        return self.sizes[pick(0)]

    def masks(self):
        masks, m = [], self.extent(self.high) // 2
        while m:
            masks.append(m)
            m //= 2
        return masks

    def lines(self, rows, masks):
        if not masks:
            return [rows]
        came = self.swap(rows, self.high, masks[0])
        return self.lines(rows, masks[1:]) + self.lines(came, masks[1:])

    def near(self, line):
        return [line] + [self.swap(line, self.first, m) for m in range(1, self.extent(self.first))]

    def far(self, near):
        return [self.swap(block, self.second, 1) for block in near]

    def other(self, mine):
        return [self.swap(block, self.core, 1) for block in mine]

    def last_sum(self, mine, other):
        return add([mine[-1], self.swap(other[0], self.core, 1)])

    def rest_sums(self, mine, other):
        size = mine[0].shape[0]
        rest = self.swap(other[1], self.core, 1)
        return [
            add([part, rest[i * size : (i + 1) * size]]) for i, part in enumerate(mine[:-1])
        ]

    def back(self, sums, place):
        return self.swap(sums[place], self.second, place // self.extent(self.first))

    def line_sum(self, sums, last):
        wide = self.extent(self.first)
        near = [[part] for part in sums[:wide]]
        for place in range(wide, len(sums)):
            moved = last if place == len(sums) - 1 else self.back(sums, place)
            near[place % wide].append(moved)
        near = [add(parts) for parts in near]
        return add([near[0]] + [self.swap(near[m], self.first, m) for m in range(1, wide)])

    def high_sum(self, line):
        rows = line.shape[0] // self.extent(self.high)
        parts = [line[:rows]]
        for m in range(1, self.extent(self.high)):
            parts.append(self.swap(line[m * rows : (m + 1) * rows], self.high, m))
        return add(parts)


def add(parts):
    total = parts[0].astype(jnp.float32)
    for part in parts[1:]:
        total = total + part.astype(jnp.float32)
    return total.astype(parts[0].dtype)


def join_kernel(count, ranges, *refs):
    for out, parts in zip(refs[count:], ranges):
        start = 0
        for first, size in parts:
            columns = pl.ds(first, size)
            out[:, start : start + size] = jnp.concatenate(
                [ref[:, columns] for ref in refs[:count]], axis=0
            )
            start += size


def join(parts, *ranges):
    rows = sum(part.shape[0] for part in parts)
    ranges = ranges or ([(0, parts[0].shape[1])],)
    outs = pl.pallas_call(
        functools.partial(join_kernel, len(parts), ranges),
        in_specs=[pl.BlockSpec(memory_space=pltpu.VMEM)] * len(parts),
        out_specs=[pl.BlockSpec(memory_space=pltpu.VMEM)] * len(ranges),
        out_shape=[
            jax.ShapeDtypeStruct((rows, sum(size for _, size in columns)), parts[0].dtype)
            for columns in ranges
        ],
        compiler_params=pltpu.CompilerParams(vmem_limit_bytes=4 * MEBI),
        name="join",
    )(*parts)
    return outs if len(ranges) > 1 else outs[0]


def table_width(experts):
    return pl.cdiv(2 * experts, 128) * 128


def pack_kernel(experts, *refs):
    sources, (out_ref, *targets), sems = refs[:3], refs[3:-1], refs[-1]
    copies = [
        pltpu.make_async_copy(source, target, sems.at[i])
        for i, (source, target) in enumerate(zip(sources, targets))
    ]
    for copy in copies:
        copy.start()
    rows_ref, ids_ref, gates_ref = targets
    for copy in copies[1:]:
        copy.wait()
    extra = table_width(experts)
    width = rows_ref.shape[1]
    gates = gates_ref[...]
    shares = 2.5 * gates / jnp.sum(gates, axis=1, keepdims=True)
    ids = ids_ref[...]
    lane = lax.broadcasted_iota(jnp.int32, (ids.shape[0], extra), 1)
    expert = jnp.where(lane < experts, lane, lane - experts)
    table = jnp.zeros(lane.shape, jnp.float32)
    for k in range(ids.shape[1]):
        table += jnp.where(expert == ids[:, k : k + 1], shares[:, k : k + 1], 0.0)
    high = table.astype(jnp.bfloat16).astype(jnp.float32)
    table = jnp.where(lane < experts, high, jnp.where(lane < 2 * experts, table - high, 0.0))
    out_ref[:, width:] = table.astype(jnp.bfloat16)
    copies[0].wait()
    out_ref[:, :width] = rows_ref[...]


def pack(experts, moe_rows, route_ids, route_gates):
    rows, width = moe_rows.shape
    sources = (moe_rows, route_ids, route_gates)
    return pl.pallas_call(
        functools.partial(pack_kernel, experts),
        in_specs=[pl.BlockSpec(memory_space=pltpu.HBM)] * 3,
        out_specs=pl.BlockSpec(memory_space=pltpu.VMEM),
        scratch_shapes=[pltpu.VMEM(source.shape, source.dtype) for source in sources]
        + [pltpu.SemaphoreType.DMA((3,))],
        out_shape=jax.ShapeDtypeStruct((rows, width + table_width(experts)), jnp.bfloat16),
        compiler_params=pltpu.CompilerParams(vmem_limit_bytes=4 * MEBI),
        name="pack",
    )(*[in_hbm(source) for source in sources])


def spread(product, outs):
    start = 0
    for out, columns in outs:
        size = out.shape[0]
        out[:, columns] = product[start : start + size]
        start += size


def fetch_columns(source, target, sems, tile):
    copies = []
    for k in range(sems.shape[0]):
        part = pl.ds(k * tile, min(tile, target.shape[1] - k * tile))
        copies.append(pltpu.make_async_copy(source.at[:, part], target.at[:, part], sems.at[k]))
        copies[-1].start()
    return copies


def fetch_both(gate_hbm, up_hbm, gate, up, gate_sem, up_sem, tile):
    copies = []
    for k in range(0, gate.shape[0], tile):
        part = pl.ds(k, tile)
        pair = (
            pltpu.make_async_copy(gate_hbm.at[part], gate.at[part], gate_sem.at[k // tile]),
            pltpu.make_async_copy(up_hbm.at[part], up.at[part], up_sem.at[k // tile]),
        )
        for copy in pair:
            copy.start()
        copies.append(pair)
    return copies


def project(blocks, copies, gate, up, gate_sum, up_sum, tile):
    for k, pair in enumerate(copies):
        part = pl.ds(k * tile, tile)
        rows = jnp.concatenate([block[:, part] for block in blocks], axis=0)
        for copy, weight, total in zip(pair, (gate, up), (gate_sum, up_sum)):
            copy.wait()
            product = jnp.dot(rows, weight[part], preferred_element_type=jnp.float32)
            if k == 0:
                total[...] = product
            else:
                total[...] += product


def expert_kernel(count, experts, tile, down_tile, split, node_ref, *refs):
    blocks = refs[:count]
    gate_hbm, up_hbm, down_hbm = refs[count : count + 3]
    outs = refs[count + 3 : -10]
    hidden_ref, share_ref, gate, up, down, gate_sum, up_sum, gate_sem, up_sem, down_sem = refs[-10:]
    copies = fetch_both(gate_hbm, up_hbm, gate, up, gate_sem, up_sem, tile)
    wide = 4 * down_tile
    down_copies = fetch_columns(down_hbm, down, down_sem, wide)

    table = jnp.concatenate([block[:, gate.shape[0] :] for block in blocks], axis=0)
    table = table.astype(jnp.float32)
    lane = lax.broadcasted_iota(jnp.int32, table.shape, 1)
    mine = (lane == node_ref[0]) | (lane == node_ref[0] + experts)
    share = jnp.sum(jnp.where(mine, table, 0.0), axis=1, keepdims=True)
    share_ref[...] = jnp.broadcast_to(share, share_ref.shape)
    project(blocks, copies, gate, up, gate_sum, up_sum, tile)
    hidden_ref[...] = (jax.nn.silu(gate_sum[...]) * up_sum[...]).astype(jnp.bfloat16)
    for k in range(0, down.shape[1], down_tile):
        if k % wide == 0:
            down_copies[k // wide].wait()
        product = jnp.dot(
            hidden_ref[...], down[:, pl.ds(k, down_tile)], preferred_element_type=jnp.float32
        )
        product = (product * share_ref[:, :1]).astype(jnp.bfloat16)
        if k < split:
            spread(product, [(out, pl.ds(k, down_tile)) for out in outs[: len(outs) // 2]])
        else:
            spread(product, [(out, pl.ds(k - split, down_tile)) for out in outs[len(outs) // 2 :]])


def expert(blocks, w_gate, w_up, w_down, experts, node, sizes, split):
    width, units = w_gate.shape
    rows = sum(sizes)
    tile, down_tile = 1024, 512
    return pl.pallas_call(
        functools.partial(expert_kernel, len(blocks), experts, tile, down_tile, split),
        in_specs=[pl.BlockSpec(memory_space=pltpu.SMEM)]
        + [pl.BlockSpec(memory_space=pltpu.VMEM)] * len(blocks)
        + [pl.BlockSpec(memory_space=pltpu.HBM)] * 3,
        out_specs=[pl.BlockSpec(memory_space=pltpu.VMEM)] * (2 * len(sizes)),
        out_shape=[
            jax.ShapeDtypeStruct((size, chunk), jnp.bfloat16)
            for chunk in (split, width - split)
            for size in sizes
        ],
        scratch_shapes=[
            pltpu.VMEM((rows, units), jnp.bfloat16),
            pltpu.VMEM((rows, 128), jnp.float32),
            pltpu.VMEM((width, units), jnp.bfloat16),
            pltpu.VMEM((width, units), jnp.bfloat16),
            pltpu.VMEM((units, width), jnp.bfloat16),
            pltpu.VMEM((rows, units), jnp.float32),
            pltpu.VMEM((rows, units), jnp.float32),
            pltpu.SemaphoreType.DMA((width // tile,)),
            pltpu.SemaphoreType.DMA((width // tile,)),
            pltpu.SemaphoreType.DMA((pl.cdiv(width, 4 * down_tile),)),
        ],
        cost_estimate=pl.CostEstimate(
            flops=6 * rows * width * units,
            bytes_accessed=6 * units * width,
            transcendentals=rows * units,
        ),
        compiler_params=pltpu.CompilerParams(vmem_limit_bytes=32 * MEBI),
        name="expert",
    )(node, *blocks, in_hbm(w_gate), in_hbm(w_up), in_hbm(w_down))


def body(
    moe_rows,
    route_ids,
    route_gates,
    w_gate,
    w_up,
    w_down,
    query_latent,
    query_rope,
    cache_latent,
    cache_rope,
    cache_lengths,
):
    grid = Grid()
    high, middle, cores, _ = grid.sizes
    experts = high * middle * cores
    tokens, width = moe_rows.shape
    node = lax.axis_index(("high", "middle", "core")).astype(jnp.int32).reshape(1)
    tied = lax.optimization_barrier
    attn_latent = attention(query_latent, query_rope, cache_latent, cache_rope, cache_lengths)

    outgoing = pack(experts, moe_rows, route_ids, route_gates)
    masks = grid.masks()
    came = grid.swap(outgoing, grid.high, masks[0])
    near = grid.near(join(grid.lines(outgoing, masks[1:])))
    far = grid.far(near[:-1])
    lines = grid.lines(came, masks[1:])
    lines[-1], near[-1], far[0], attn_latent = tied((lines[-1], near[-1], far[0], attn_latent))
    later_near = grid.near(join(lines))
    later_far = grid.far(later_near[:-1])
    far += grid.far(near[-1:])
    far[-1], later_near[-1], later_far[0] = tied((far[-1], later_near[-1], later_far[0]))
    rows = later_near[-1].shape[0] // 2
    last = grid.far([later_near[-1][:rows]])
    last.append(grid.swap(later_far[0][rows:], grid.first, grid.extent(grid.first) - 1))
    mine = [[block] for block in near + far]
    for place, block in zip(mine, later_near + later_far):
        place.append(block)
    mine[-1] += last
    other = [grid.other(place) for place in mine]
    size, count = high * tokens, len(mine)
    sizes = [size] * count + [size, size * (count - 1)]
    split = width // 2
    places = mine + other[-1:] + other[:-1]
    products = expert(
        [block for place in places for block in place],
        w_gate[0],
        w_up[0],
        w_down[0],
        experts,
        node,
        sizes,
        split,
    )

    def returned(parts):
        last = grid.last_sum(parts[:count], parts[count:])
        sums = grid.rest_sums(parts[:count], parts[count:]) + [last]
        return grid.high_sum(grid.line_sum(sums, grid.back(sums, count - 1)))

    head, tail = returned(products[: len(sizes)]), returned(products[len(sizes) :])
    return (jnp.concatenate([head, tail], axis=1), attn_latent)


def solution(mesh):
    groups, nodes, local = mesh.devices.shape
    split = Mesh(mesh.devices.reshape(groups, nodes // 4, 2, 2, local), ("group",) + everyone)
    node = ("high", "middle", "core")
    whole = ("group",) + everyone
    rows = P(whole, None)
    blocks = P(whole, None, None)
    return jax.shard_map(
        body,
        mesh=split,
        in_specs=(
            rows,
            rows,
            rows,
            P(node, None, "local"),
            P(node, None, "local"),
            P(node, "local", None),
            blocks,
            blocks,
            blocks,
            blocks,
            P(whole),
        ),
        out_specs=(rows, blocks),
        check_vma=False,
    )
```

```python
import functools

import jax
import jax.numpy as jnp
import numpy as np
from jax import lax
from jax.experimental import pallas as pl
from jax.experimental.pallas import tpu as pltpu
from jax.sharding import Mesh
from jax.sharding import PartitionSpec as P

score_scale = 192.0 ** (-0.5)
everyone = ("high", "middle", "core", "local")
MEBI = 1024 * 1024


def attention_kernel(lengths_ref, *refs):
    sources, (out_ref, *targets), sems = refs[:4], refs[4:-1], refs[-1]
    query_ref, query_rope_ref, cache_ref, cache_rope_ref = targets
    copies = []
    for row in range(out_ref.shape[0]):
        copies.append(
            [
                pltpu.make_async_copy(source.at[row], target.at[row], sems.at[row, i])
                for i, (source, target) in enumerate(zip(sources, targets))
            ]
        )
        for copy in copies[-1]:
            copy.start()
    for row in range(out_ref.shape[0]):
        for copy in copies[row]:
            copy.wait()
        cache = cache_ref[row]
        scores = lax.dot_general(
            query_ref[row], cache, (((1,), (1,)), ((), ())), preferred_element_type=jnp.float32
        )
        scores += jnp.dot(
            query_rope_ref[row], cache_rope_ref[row], preferred_element_type=jnp.float32
        )
        slot = lax.broadcasted_iota(jnp.int32, scores.shape, 1)
        in_range = slot < lengths_ref[row]
        scores = jnp.where(in_range, scores * score_scale, -jnp.inf)
        row_peak = jnp.max(scores, axis=1, keepdims=True)
        lifted = jnp.where(in_range, jnp.exp(scores - row_peak), 0.0)
        weights = (lifted / jnp.sum(lifted, axis=1, keepdims=True)).astype(jnp.bfloat16)
        value = jnp.dot(weights, cache, preferred_element_type=jnp.float32)
        out_ref[row] = value.astype(jnp.bfloat16)


def attention(query_latent, query_rope, cache_latent, cache_rope, cache_lengths):
    rows, heads, latent = query_latent.shape
    slots = cache_latent.shape[1]
    sources = (query_latent, query_rope, cache_latent, cache_rope)
    return pl.pallas_call(
        attention_kernel,
        in_specs=[pl.BlockSpec(memory_space=pltpu.SMEM)]
        + [pl.BlockSpec(memory_space=pltpu.HBM)] * 4,
        out_specs=pl.BlockSpec(memory_space=pltpu.VMEM),
        out_shape=jax.ShapeDtypeStruct(query_latent.shape, jnp.bfloat16),
        scratch_shapes=[pltpu.VMEM(source.shape, source.dtype) for source in sources]
        + [pltpu.SemaphoreType.DMA((rows, 4))],
        cost_estimate=pl.CostEstimate(
            flops=4 * rows * heads * slots * latent,
            bytes_accessed=2 * rows * slots * latent,
            transcendentals=rows * heads * slots,
        ),
        compiler_params=pltpu.CompilerParams(vmem_limit_bytes=8 * MEBI),
        name="attention",
    )(cache_lengths, *[in_hbm(source) for source in sources])


def in_hbm(array):
    return pltpu.with_memory_space_constraint(array, pltpu.HBM)


class Grid:
    def __init__(self):
        self.sizes = tuple(lax.axis_size(name) for name in everyone)
        self.mixed = self.sizes[1] == self.sizes[3]

    def swap(self, value, pick, mask):
        pairs = []
        for place in np.ndindex(*self.sizes):
            other = list(place)
            other[pick(place[2])] ^= mask
            pairs.append(
                (
                    int(np.ravel_multi_index(place, self.sizes)),
                    int(np.ravel_multi_index(other, self.sizes)),
                )
            )
        return lax.ppermute(value, everyone, pairs)

    def high(self, core):
        return 0

    def core(self, core):
        return 2

    def first(self, core):
        return 1 if self.mixed and core == 1 else 3

    def second(self, core):
        return 3 if self.mixed and core == 1 else 1

    def extent(self, pick):
        return self.sizes[pick(0)]

    def masks(self):
        masks, m = [], self.extent(self.high) // 2
        while m:
            masks.append(m)
            m //= 2
        return masks

    def lines(self, rows, masks):
        if not masks:
            return [rows]
        came = self.swap(rows, self.high, masks[0])
        return self.lines(rows, masks[1:]) + self.lines(came, masks[1:])

    def near(self, line):
        return [line] + [self.swap(line, self.first, m) for m in range(1, self.extent(self.first))]

    def far(self, near):
        return [self.swap(block, self.second, 1) for block in near]

    def other(self, mine):
        return [self.swap(block, self.core, 1) for block in mine]

    def last_sum(self, mine, other):
        return add([mine[-1], self.swap(other[0], self.core, 1)])

    def rest_sums(self, mine, other):
        size = mine[0].shape[0]
        rest = self.swap(other[1], self.core, 1)
        return [
            add([part, rest[i * size : (i + 1) * size]]) for i, part in enumerate(mine[:-1])
        ]

    def back(self, sums, place):
        return self.swap(sums[place], self.second, place // self.extent(self.first))

    def line_sum(self, sums, last):
        wide = self.extent(self.first)
        near = [[part] for part in sums[:wide]]
        for place in range(wide, len(sums)):
            moved = last if place == len(sums) - 1 else self.back(sums, place)
            near[place % wide].append(moved)
        near = [add(parts) for parts in near]
        return add([near[0]] + [self.swap(near[m], self.first, m) for m in range(1, wide)])

    def high_sum(self, line):
        rows = line.shape[0] // self.extent(self.high)
        parts = [line[:rows]]
        for m in range(1, self.extent(self.high)):
            parts.append(self.swap(line[m * rows : (m + 1) * rows], self.high, m))
        return add(parts)


def add(parts):
    total = parts[0].astype(jnp.float32)
    for part in parts[1:]:
        total = total + part.astype(jnp.float32)
    return total.astype(parts[0].dtype)


def join_kernel(count, ranges, *refs):
    for out, parts in zip(refs[count:], ranges):
        start = 0
        for first, size in parts:
            columns = pl.ds(first, size)
            out[:, start : start + size] = jnp.concatenate(
                [ref[:, columns] for ref in refs[:count]], axis=0
            )
            start += size


def join(parts, *ranges):
    rows = sum(part.shape[0] for part in parts)
    ranges = ranges or ([(0, parts[0].shape[1])],)
    outs = pl.pallas_call(
        functools.partial(join_kernel, len(parts), ranges),
        in_specs=[pl.BlockSpec(memory_space=pltpu.VMEM)] * len(parts),
        out_specs=[pl.BlockSpec(memory_space=pltpu.VMEM)] * len(ranges),
        out_shape=[
            jax.ShapeDtypeStruct((rows, sum(size for _, size in columns)), parts[0].dtype)
            for columns in ranges
        ],
        compiler_params=pltpu.CompilerParams(vmem_limit_bytes=4 * MEBI),
        name="join",
    )(*parts)
    return outs if len(ranges) > 1 else outs[0]


def table_width(experts):
    return pl.cdiv(2 * experts, 128) * 128


def pack_kernel(experts, *refs):
    sources, (out_ref, *targets), sems = refs[:3], refs[3:-1], refs[-1]
    copies = [
        pltpu.make_async_copy(source, target, sems.at[i])
        for i, (source, target) in enumerate(zip(sources, targets))
    ]
    for copy in copies:
        copy.start()
    rows_ref, ids_ref, gates_ref = targets
    for copy in copies[1:]:
        copy.wait()
    extra = table_width(experts)
    width = rows_ref.shape[1]
    gates = gates_ref[...]
    shares = 2.5 * gates / jnp.sum(gates, axis=1, keepdims=True)
    ids = ids_ref[...]
    lane = lax.broadcasted_iota(jnp.int32, (ids.shape[0], extra), 1)
    expert = jnp.where(lane < experts, lane, lane - experts)
    table = jnp.zeros(lane.shape, jnp.float32)
    for k in range(ids.shape[1]):
        table += jnp.where(expert == ids[:, k : k + 1], shares[:, k : k + 1], 0.0)
    high = table.astype(jnp.bfloat16).astype(jnp.float32)
    table = jnp.where(lane < experts, high, jnp.where(lane < 2 * experts, table - high, 0.0))
    out_ref[:, width:] = table.astype(jnp.bfloat16)
    copies[0].wait()
    out_ref[:, :width] = rows_ref[...]


def pack(experts, moe_rows, route_ids, route_gates):
    rows, width = moe_rows.shape
    sources = (moe_rows, route_ids, route_gates)
    return pl.pallas_call(
        functools.partial(pack_kernel, experts),
        in_specs=[pl.BlockSpec(memory_space=pltpu.HBM)] * 3,
        out_specs=pl.BlockSpec(memory_space=pltpu.VMEM),
        scratch_shapes=[pltpu.VMEM(source.shape, source.dtype) for source in sources]
        + [pltpu.SemaphoreType.DMA((3,))],
        out_shape=jax.ShapeDtypeStruct((rows, width + table_width(experts)), jnp.bfloat16),
        compiler_params=pltpu.CompilerParams(vmem_limit_bytes=4 * MEBI),
        name="pack",
    )(*[in_hbm(source) for source in sources])


def spread(product, outs):
    start = 0
    for out, columns in outs:
        size = out.shape[0]
        out[:, columns] = product[start : start + size]
        start += size


def fetch_columns(source, target, sems, tile):
    copies = []
    for k in range(sems.shape[0]):
        part = pl.ds(k * tile, min(tile, target.shape[1] - k * tile))
        copies.append(pltpu.make_async_copy(source.at[:, part], target.at[:, part], sems.at[k]))
        copies[-1].start()
    return copies


def fetch_both(gate_hbm, up_hbm, gate, up, gate_sem, up_sem, tile):
    copies = []
    for k in range(0, gate.shape[0], tile):
        part = pl.ds(k, tile)
        pair = (
            pltpu.make_async_copy(gate_hbm.at[part], gate.at[part], gate_sem.at[k // tile]),
            pltpu.make_async_copy(up_hbm.at[part], up.at[part], up_sem.at[k // tile]),
        )
        for copy in pair:
            copy.start()
        copies.append(pair)
    return copies


def project(blocks, copies, gate, up, gate_sum, up_sum, tile):
    for k, pair in enumerate(copies):
        part = pl.ds(k * tile, tile)
        rows = jnp.concatenate([block[:, part] for block in blocks], axis=0)
        for copy, weight, total in zip(pair, (gate, up), (gate_sum, up_sum)):
            copy.wait()
            product = jnp.dot(rows, weight[part], preferred_element_type=jnp.float32)
            if k == 0:
                total[...] = product
            else:
                total[...] += product


def expert_kernel(count, experts, tile, down_tile, split, node_ref, *refs):
    blocks = refs[:count]
    gate_hbm, up_hbm, down_hbm = refs[count : count + 3]
    outs = refs[count + 3 : -10]
    hidden_ref, share_ref, gate, up, down, gate_sum, up_sum, gate_sem, up_sem, down_sem = refs[-10:]
    copies = fetch_both(gate_hbm, up_hbm, gate, up, gate_sem, up_sem, tile)
    wide = 4 * down_tile
    down_copies = fetch_columns(down_hbm, down, down_sem, wide)

    table = jnp.concatenate([block[:, gate.shape[0] :] for block in blocks], axis=0)
    table = table.astype(jnp.float32)
    lane = lax.broadcasted_iota(jnp.int32, table.shape, 1)
    mine = (lane == node_ref[0]) | (lane == node_ref[0] + experts)
    share = jnp.sum(jnp.where(mine, table, 0.0), axis=1, keepdims=True)
    share_ref[...] = jnp.broadcast_to(share, share_ref.shape)
    project(blocks, copies, gate, up, gate_sum, up_sum, tile)
    hidden_ref[...] = (jax.nn.silu(gate_sum[...]) * up_sum[...]).astype(jnp.bfloat16)
    for k in range(0, down.shape[1], down_tile):
        if k % wide == 0:
            down_copies[k // wide].wait()
        product = jnp.dot(
            hidden_ref[...], down[:, pl.ds(k, down_tile)], preferred_element_type=jnp.float32
        )
        product = (product * share_ref[:, :1]).astype(jnp.bfloat16)
        if k < split:
            spread(product, [(out, pl.ds(k, down_tile)) for out in outs[: len(outs) // 2]])
        else:
            spread(product, [(out, pl.ds(k - split, down_tile)) for out in outs[len(outs) // 2 :]])


def expert(blocks, w_gate, w_up, w_down, experts, node, sizes, split):
    width, units = w_gate.shape
    rows = sum(sizes)
    tile, down_tile = 1024, 512
    return pl.pallas_call(
        functools.partial(expert_kernel, len(blocks), experts, tile, down_tile, split),
        in_specs=[pl.BlockSpec(memory_space=pltpu.SMEM)]
        + [pl.BlockSpec(memory_space=pltpu.VMEM)] * len(blocks)
        + [pl.BlockSpec(memory_space=pltpu.HBM)] * 3,
        out_specs=[pl.BlockSpec(memory_space=pltpu.VMEM)] * (2 * len(sizes)),
        out_shape=[
            jax.ShapeDtypeStruct((size, chunk), jnp.bfloat16)
            for chunk in (split, width - split)
            for size in sizes
        ],
        scratch_shapes=[
            pltpu.VMEM((rows, units), jnp.bfloat16),
            pltpu.VMEM((rows, 128), jnp.float32),
            pltpu.VMEM((width, units), jnp.bfloat16),
            pltpu.VMEM((width, units), jnp.bfloat16),
            pltpu.VMEM((units, width), jnp.bfloat16),
            pltpu.VMEM((rows, units), jnp.float32),
            pltpu.VMEM((rows, units), jnp.float32),
            pltpu.SemaphoreType.DMA((width // tile,)),
            pltpu.SemaphoreType.DMA((width // tile,)),
            pltpu.SemaphoreType.DMA((pl.cdiv(width, 4 * down_tile),)),
        ],
        cost_estimate=pl.CostEstimate(
            flops=6 * rows * width * units,
            bytes_accessed=6 * units * width,
            transcendentals=rows * units,
        ),
        compiler_params=pltpu.CompilerParams(vmem_limit_bytes=32 * MEBI),
        name="expert",
    )(node, *blocks, in_hbm(w_gate), in_hbm(w_up), in_hbm(w_down))


def body(
    moe_rows,
    route_ids,
    route_gates,
    w_gate,
    w_up,
    w_down,
    query_latent,
    query_rope,
    cache_latent,
    cache_rope,
    cache_lengths,
):
    grid = Grid()
    high, middle, cores, _ = grid.sizes
    experts = high * middle * cores
    tokens, width = moe_rows.shape
    node = lax.axis_index(("high", "middle", "core")).astype(jnp.int32).reshape(1)
    tied = lax.optimization_barrier
    attn_latent = attention(query_latent, query_rope, cache_latent, cache_rope, cache_lengths)

    outgoing = pack(experts, moe_rows, route_ids, route_gates)
    masks = grid.masks()
    came = grid.swap(outgoing, grid.high, masks[0])
    near = grid.near(join(grid.lines(outgoing, masks[1:])))
    far = grid.far(near[:-1])
    lines = grid.lines(came, masks[1:])
    lines[-1], near[-1], far[0], attn_latent = tied((lines[-1], near[-1], far[0], attn_latent))
    later_near = grid.near(join(lines))
    later_far = grid.far(later_near[:-1])

    def last_place(near, far):
        rows = near[-1].shape[0] // 2
        halves = grid.far([near[-1][:rows]])
        return halves + [grid.swap(far[0][rows:], grid.first, grid.extent(grid.first) - 1)]

    last = last_place(near, far)
    last, later_near[-1], later_far[0] = tied((last, later_near[-1], later_far[0]))
    mine = [list(blocks) for blocks in zip(near + far, later_near + later_far)]
    mine.append(last + last_place(later_near, later_far))
    other = [grid.other(place) for place in mine]
    size, count = high * tokens, len(mine)
    sizes = [size] * count + [size, size * (count - 1)]
    split = width // 2
    places = mine + other[-1:] + other[:-1]
    products = expert(
        [block for place in places for block in place],
        w_gate[0],
        w_up[0],
        w_down[0],
        experts,
        node,
        sizes,
        split,
    )

    def returned(parts):
        last = grid.last_sum(parts[:count], parts[count:])
        sums = grid.rest_sums(parts[:count], parts[count:]) + [last]
        return grid.high_sum(grid.line_sum(sums, grid.back(sums, count - 1)))

    head, tail = returned(products[: len(sizes)]), returned(products[len(sizes) :])
    return (jnp.concatenate([head, tail], axis=1), attn_latent)


def solution(mesh):
    groups, nodes, local = mesh.devices.shape
    split = Mesh(mesh.devices.reshape(groups, nodes // 4, 2, 2, local), ("group",) + everyone)
    node = ("high", "middle", "core")
    whole = ("group",) + everyone
    rows = P(whole, None)
    blocks = P(whole, None, None)
    return jax.shard_map(
        body,
        mesh=split,
        in_specs=(
            rows,
            rows,
            rows,
            P(node, None, "local"),
            P(node, None, "local"),
            P(node, "local", None),
            blocks,
            blocks,
            blocks,
            blocks,
            P(whole),
        ),
        out_specs=(rows, blocks),
        check_vma=False,
    )
```
